256 devices in a mesh: ctx: 16 (over z, y_hi), head: 16 (over y_lo, x, core).
Axes of the slice: x: 4, y: 4 (y_hi: 2, y_lo: 2; y = y_hi * 2 + y_lo), z: 8, core: 2. Of those that a mesh axis runs over, the one named last changes fastest.
Arguments:
- main_query: bfloat16 [4096, 128, 576], P('ctx', 'head'), may hold values from -12 to 12
- key_latent: bfloat16 [12288, 576], P('ctx'), may hold values from -6 to 6
- index_query: bfloat16 [4096, 64, 128], P('ctx', 'head'), may hold values from -0.53033009 to 0.53033009
- index_key: bfloat16 [12288, 128], P('ctx'), may hold values from -6 to 6
- index_weight: float32 [4096, 64], P('ctx', 'head'), may hold values from -1.6 to 1.6
- selection: int32 [16, 16], replicated, may hold values from 0 to 95, as said below
- loss_grad: float32 [4096], P('ctx'), may hold values from 8 to 64
Outputs:
- query_grad: float32 [4096, 64, 128], P('ctx', 'head')
- weight_grad: float32 [4096, 64], P('ctx', 'head')
- key_grad: float32 [12288, 128], P(('ctx', 'head'))
- query_loss: float32 [4096], P('ctx')
The draws below stay inside these ranges and needn't reach their ends.
Inputs may be any that keep to these rules, and one draw needn't show every extreme that they name: `selection`: row b lists 16 different key tiles, all at or below key tile 16 * 4 + 2 * b + 1, and includes the 2 tiles from 16 * 4 + 2 * b upward. Within any aligned group of 6 tiles (the keys of one device) a row names at most 3 tiles; in every draw one group that lies below all queries is named exactly 3 times by every row.
All inputs are finite; a program needn't handle non-finite values.
Results may differ from the reference program's by a relative error of at most 0.012.
Values may be sent and summed in bfloat16 or wider, within the bound.
No kernel may reach another device: no remote copies, remote signals or barrier semaphores. Data moves between devices by JAX's collectives and lax.ppermute only.
A program may use at most 128 MiB of HBM per device.

```python
import math
import jax
import jax.numpy as jnp
from jax import lax

TILE = 128
QT = 2
KT_DEV = 6
SEL = 16
OWNER_MOST = 3
MLA_HEADS = 128
IDX_HEADS = 64
IDX_DIM = 128
LATENT = 576
QUERIES = 4096
CONTEXT = 12288
N_CTX = 16


score_scale = 192.0 ** (-0.5)


def chosen_rows(query_index):
    inside = (query_index >= 0) & (query_index < QUERIES)
    return inside & (query_index % TILE == TILE - 1) & (query_index // TILE % 4 == 1)


def strength_levels(query_index, lowest, middle, highest):
    level = query_index // TILE // 4 % 3
    return jnp.where(level == 0, lowest, jnp.where(level == 1, middle, highest))


def raw_keys(key, salt, width, flatness):
    sub_key = jax.random.fold_in(key, salt)
    gauss = jnp.clip(jax.random.normal(sub_key, (CONTEXT, width), jnp.float32), -6.0, 6.0)
    even = jax.random.uniform(sub_key, (CONTEXT, width), jnp.float32, -3.0 ** 0.5, 3.0 ** 0.5)
    return flatness * even + (1.0 - flatness) * gauss


def tied_keys(raw_rows, lowest, middle, highest, unit, tie):
    query_index = jnp.arange(CONTEXT) + 1 - (CONTEXT - QUERIES)
    strength = strength_levels(query_index, lowest, middle, highest)
    factor = 1.0 - 2.0 / (unit * strength)
    following = jnp.concatenate([raw_rows[1:], raw_rows[:1]], axis=0)
    paired = chosen_rows(query_index) & (tie > 0.5)
    return jnp.where(paired[:, None], factor[:, None] * following, raw_rows)


def draw_key_latent(key, part):
    flatness, tie = (0.0, 0.0)
    raw_rows = raw_keys(key, 101, LATENT, flatness)
    return tied_keys(raw_rows, 3.0, 4.5, 6.5, score_scale * LATENT, tie).astype(jnp.bfloat16)


def draw_index_key(key, part):
    flatness, tie = (0.0, 0.0)
    raw_rows = raw_keys(key, 202, IDX_DIM, flatness)
    return tied_keys(raw_rows, 2.5, 4.0, 6.5, 0.75 * IDX_HEADS, tie).astype(jnp.bfloat16)


def draw_main_query(key, part):
    flatness, tie = (0.0, 0.0)
    latent_rows = raw_keys(key, 101, LATENT, flatness)
    own_key = jax.random.fold_in(key, 5)
    full_shape = (QUERIES, MLA_HEADS, LATENT)
    values = jnp.clip(jax.random.normal(own_key, full_shape, jnp.float32), -6.0, 6.0)
    query_index = jnp.arange(QUERIES)
    own_rows = latent_rows[CONTEXT - QUERIES:]
    strength = strength_levels(query_index, 3.0, 4.5, 6.5)
    aligned = strength[:, None, None] * own_rows[:, None, :]
    paired = chosen_rows(query_index) & (tie > 0.5)
    return jnp.where(paired[:, None, None], aligned, values).astype(jnp.bfloat16)


def draw_index_query(key, part):
    flatness, tie = (0.0, 0.0)
    index_rows = raw_keys(key, 202, IDX_DIM, flatness)
    own_key = jax.random.fold_in(key, 7)
    full_shape = (QUERIES, IDX_HEADS, IDX_DIM)
    values = jnp.clip(jax.random.normal(own_key, full_shape, jnp.float32), -6.0, 6.0)
    values = values * IDX_DIM ** (-0.5)
    query_index = jnp.arange(QUERIES)
    own_rows = index_rows[CONTEXT - QUERIES:]
    strength = strength_levels(query_index, 2.5, 4.0, 6.5) / IDX_DIM
    aligned = strength[:, None, None] * own_rows[:, None, :]
    paired = chosen_rows(query_index) & (tie > 0.5)
    return jnp.where(paired[:, None, None], aligned, values).astype(jnp.bfloat16)


def draw_index_weight(key, part):
    key = jax.random.fold_in(key, 9)
    full_shape = (QUERIES, IDX_HEADS)
    return jnp.clip(0.4 * jax.random.normal(key, full_shape, jnp.float32), -1.6, 1.6)


def draw_selection(key, part):
    key = jax.random.fold_in(key, 13)
    tile_total = N_CTX * KT_DEV
    block_ids = jnp.arange(N_CTX)
    base_tile = N_CTX * (KT_DEV - QT)
    own_first = base_tile + QT * block_ids
    own_last = own_first + QT - 1
    full_groups = base_tile // KT_DEV
    hot_group = jax.random.randint(jax.random.fold_in(key, 1), (), 0, full_groups)
    tile_ids = jnp.arange(tile_total)
    group_of = tile_ids // KT_DEV
    noise = jax.random.randint(jax.random.fold_in(key, 2), (N_CTX, tile_total), 0, 2 ** 16)
    order = noise * tile_total + tile_ids[None, :]
    own_tiles = (tile_ids[None, :] >= own_first[:, None]) & (tile_ids[None, :] <= own_last[:, None])
    below = tile_ids[None, :] < own_first[:, None]
    order_groups = order.reshape(N_CTX, N_CTX, KT_DEV)
    below_groups = below.reshape(N_CTX, N_CTX, KT_DEV)
    beaten = below_groups[:, :, None, :] & (order_groups[:, :, None, :] < order_groups[:, :, :, None])
    slot_rank = jnp.sum(beaten, axis=3).reshape(N_CTX, tile_total)
    own_group = own_first // KT_DEV
    limit = jnp.where(group_of[None, :] == hot_group, OWNER_MOST, jnp.where(group_of[None, :] == own_group[:, None], OWNER_MOST - QT, OWNER_MOST))
    eligible = below & (slot_rank < limit)
    hot_pick = eligible & (group_of[None, :] == hot_group)
    level = jnp.where(own_tiles | hot_pick, 0, jnp.where(eligible, 1, 2))
    ranked = level * 2 ** 27 + order
    best_values, best_tiles = lax.top_k(-ranked, SEL)
    return jnp.sort(best_tiles, axis=1).astype(jnp.int32)


def steps_of(rng, dims, pieces, low, top_value):
    gain, own = 1.0, jax.random.fold_in(rng, 6)
    for dim, parts in pieces:
        heights = jnp.exp(jax.random.uniform(jax.random.fold_in(own, dim), (parts,), jnp.float32, low / len(pieces), top_value / len(pieces)))
        gain = gain * jnp.repeat(heights, dims[dim] // parts).reshape([-1 if axis == dim else 1 for axis in range(len(dims))])
    return gain


def setup_inputs(seed: int = 0) -> dict:
    arg_keys = jax.random.split(jax.random.key(seed), 8)
    main_query = draw_main_query(jax.random.fold_in(arg_keys[7], 71), 0)
    key_latent = draw_key_latent(jax.random.fold_in(arg_keys[7], 71), 0)
    index_query = draw_index_query(jax.random.fold_in(arg_keys[7], 71), 0)
    index_key = draw_index_key(jax.random.fold_in(arg_keys[7], 71), 0)
    index_weight = draw_index_weight(jax.random.fold_in(arg_keys[7], 71), 0)
    selection = draw_selection(jax.random.fold_in(arg_keys[7], 71), 0)
    loss_grad = jnp.clip(jnp.exp(math.log(64.0) - 2.0794415 * jax.random.uniform(arg_keys[6], (QUERIES,), jnp.float32) ** steps_of(arg_keys[6], (QUERIES,), ((0, 16),), -0.2, 0.2)), 8.0, 64.0)
    return dict(main_query=main_query, key_latent=key_latent, index_query=index_query, index_key=index_key, index_weight=index_weight, selection=selection, loss_grad=loss_grad)


score_scale = 192.0 ** -0.5
far_below = -1.0e30


def masked_softmax(raw_scores, allowed):
    masked = jnp.where(allowed, raw_scores, far_below)
    row_max = jnp.max(masked, axis=-1, keepdims=True)
    weights = jnp.where(allowed, jnp.exp(raw_scores - row_max), 0.0)
    return weights / jnp.sum(weights, axis=-1, keepdims=True)


def finish_scores(total_target, total_score, allowed, grad_rows):
    target = total_target / MLA_HEADS
    masked = jnp.where(allowed, total_score, far_below)
    row_max = jnp.max(masked, axis=-1, keepdims=True)
    weights = jnp.where(allowed, jnp.exp(total_score - row_max), 0.0)
    row_sum = jnp.sum(weights, axis=-1, keepdims=True)
    index_prob = weights / row_sum
    log_prob = total_score - row_max - jnp.log(row_sum)
    positive = target > 0
    self_term = jnp.where(positive, target * jnp.log(jnp.where(positive, target, 1.0)), 0.0)
    loss_rows = jnp.sum(jnp.where(allowed, self_term - target * log_prob, 0.0), axis=-1)
    score_grad = grad_rows[:, None] * jnp.where(allowed, index_prob - target, 0.0)
    return score_grad, loss_rows


def reference(main_query, key_latent, index_query, index_key, index_weight, selection, loss_grad):
    block_rows = QT * TILE
    key_span = SEL * TILE
    latent_tiles = key_latent.reshape(CONTEXT // TILE, TILE, LATENT)
    index_tiles = index_key.reshape(CONTEXT // TILE, TILE, IDX_DIM)
    head_block = math.gcd(MLA_HEADS, 16)

    def one_block(block_id):
        picked = selection[block_id]
        keys_latent = jnp.take(latent_tiles, picked, axis=0).reshape(key_span, LATENT)
        keys_index = jnp.take(index_tiles, picked, axis=0).reshape(key_span, IDX_DIM)
        first_row = block_id * block_rows
        query_pos = CONTEXT - QUERIES + first_row + jnp.arange(block_rows, dtype=jnp.int32)
        key_pos = (picked[:, None] * TILE + jnp.arange(TILE, dtype=jnp.int32)[None, :]).reshape(key_span)
        allowed = key_pos[None, :] <= query_pos[:, None]
        main_rows = lax.dynamic_slice_in_dim(main_query, first_row, block_rows, 0)

        def add_heads(block_step, summed):
            head_rows = lax.dynamic_slice_in_dim(main_rows, block_step * head_block, head_block, 1)
            head_rows = head_rows.reshape(block_rows * head_block, LATENT)
            raw_scores = jnp.dot(head_rows, keys_latent.T, preferred_element_type=jnp.float32) * score_scale
            attend = masked_softmax(raw_scores.reshape(block_rows, head_block, key_span), allowed[:, None, :])
            return summed + jnp.sum(attend, axis=1)

        target_sum = lax.fori_loop(0, MLA_HEADS // head_block, add_heads,
                                   jnp.zeros((block_rows, key_span), jnp.float32))
        query_rows = lax.dynamic_slice_in_dim(index_query, first_row, block_rows, 0)
        weight_rows = lax.dynamic_slice_in_dim(index_weight, first_row, block_rows, 0)
        grad_rows = lax.dynamic_slice_in_dim(loss_grad, first_row, block_rows, 0)
        query_flat = query_rows.reshape(block_rows * IDX_HEADS, IDX_DIM)
        logits = jnp.dot(query_flat, keys_index.T, preferred_element_type=jnp.float32)
        logits = logits.reshape(block_rows, IDX_HEADS, key_span)
        lifted = jnp.maximum(logits, 0.0)
        index_score = jnp.sum(weight_rows[:, :, None] * lifted, axis=1)
        score_grad, loss_rows = finish_scores(target_sum, index_score, allowed, grad_rows)
        coefficient = (score_grad[:, None, :] * weight_rows[:, :, None] * (logits > 0)).astype(jnp.bfloat16)
        coef_flat = coefficient.reshape(block_rows * IDX_HEADS, key_span)
        query_part = jnp.dot(coef_flat, keys_index, preferred_element_type=jnp.float32)
        weight_part = jnp.sum(score_grad[:, None, :] * lifted, axis=2)
        key_part = jnp.dot(coef_flat.T, query_flat, preferred_element_type=jnp.float32)
        return query_part.reshape(block_rows, IDX_HEADS, IDX_DIM), weight_part, loss_rows, key_part

    query_parts, weight_parts, loss_parts, key_parts = lax.map(one_block, jnp.arange(N_CTX, dtype=jnp.int32))
    key_grad = jnp.zeros((CONTEXT // TILE, TILE, IDX_DIM), jnp.float32)
    key_grad = key_grad.at[selection.reshape(N_CTX * SEL)].add(key_parts.reshape(N_CTX * SEL, TILE, IDX_DIM))
    query_grad = query_parts.reshape(QUERIES, IDX_HEADS, IDX_DIM)
    weight_grad = weight_parts.reshape(QUERIES, IDX_HEADS)
    query_loss = loss_parts.reshape(QUERIES)
    return query_grad, weight_grad, key_grad.reshape(CONTEXT, IDX_DIM), query_loss
```

```python
import jax
import jax.numpy as jnp
from jax import lax
from jax.experimental import pallas as pl
from jax.experimental.pallas import tpu as pltpu
from jax.sharding import Mesh, PartitionSpec as P

TILE = 128
MLA_HEADS = 128
OWNER_MOST = 3
QROWS = 16
STRIPE = 8
VMEM = 50 * 1024 * 1024

CTX = ("z", "yh")
HEAD = ("yl", "x", "core")
ROWS = ("core", "yl", "x")
score_scale = 192.0 ** (-0.5)
far_below = -1e30


def allowed_keys(query_first, key_pos):
    rows = lax.broadcasted_iota(jnp.int32, (QROWS, key_pos.shape[1]), 0)
    return key_pos <= rows + query_first


def attend_kernel(place, query_first, *refs):
    pieces, (q_own, q_other, key_pos, target, index_keys, keys) = refs[:8], refs[8:]

    @pl.when(pl.program_id(0) == 0)
    def _():
        for i, piece in enumerate(pieces):
            for j in range(2):
                spot = pl.ds(pl.multiple_of(place[2 * i + j] * TILE, TILE), TILE)
                keys[spot, :] = piece[j]
                index_keys[spot, :] = piece[j, :, :TILE]

    latent = keys[:, TILE:]
    allowed = allowed_keys(query_first[0] + pl.program_id(0) * QROWS, key_pos[...])
    bias = jnp.where(allowed, 0.0, far_below)
    total = jnp.zeros(target.shape, jnp.float32)
    for q in (q_own, q_other):
        heads, rows, width = q.shape
        raw = lax.dot_general(
            q[...].reshape(heads * rows, width),
            latent,
            (((1,), (1,)), ((), ())),
            preferred_element_type=jnp.float32,
        ).reshape(heads, rows, latent.shape[0])
        raw = raw * score_scale + bias[None]
        top = jnp.max(raw, axis=-1, keepdims=True)
        weights = jnp.exp(raw - top)
        share = 1.0 / (jnp.sum(weights, axis=-1, keepdims=True) * MLA_HEADS)
        total = total + jnp.sum(weights * share, axis=0)
    target[...] = total


def index_logits(iq, keys, heads_step, step):
    rows = heads_step * QROWS
    block = iq[pl.ds(step * rows, rows), :]
    return lax.dot_general(
        block, keys[...], (((1,), (1,)), ((), ())), preferred_element_type=jnp.float32
    )


def score_kernel(iq, weight, keys, score):
    heads_step = 8
    rows = heads_step * QROWS
    span = keys.shape[0]
    total = jnp.zeros((QROWS, span), jnp.float32)
    for step in range(iq.shape[0] // rows):
        lifted = jnp.maximum(index_logits(iq, keys, heads_step, step), 0.0)
        lifted = lifted * weight[pl.ds(step * rows, rows), :]
        total = total + jnp.sum(lifted.reshape(heads_step, QROWS, span), axis=0)
    score[...] = total


def grad_kernel(
    query_first, parts, score, iq, iq_t, weight, keys, key_pos, loss_grad,
    query_grad, weight_grad, key_grad, loss, coef
):
    allowed = allowed_keys(query_first[0], key_pos[...])
    target = jnp.sum(parts[...], axis=0)
    masked = jnp.where(allowed, score[...], far_below)
    shifted = masked - jnp.max(masked, axis=-1, keepdims=True)
    weights = jnp.where(allowed, jnp.exp(shifted), 0.0)
    row_sum = jnp.sum(weights, axis=-1, keepdims=True)
    log_prob = shifted - jnp.log(row_sum)
    positive = target > 0
    self_term = jnp.where(positive, target * jnp.log(jnp.where(positive, target, 1.0)), 0.0)
    loss[...] = jnp.sum(
        jnp.where(allowed, self_term - target * log_prob, 0.0), axis=-1, keepdims=True
    )
    score_grad = loss_grad[...] * jnp.where(allowed, weights / row_sum - target, 0.0)
    heads_step = 8
    rows = heads_step * QROWS
    span = keys.shape[0]
    for step in range(iq.shape[0] // rows):
        spot = pl.ds(step * rows, rows)
        logits = index_logits(iq, keys, heads_step, step).reshape(heads_step, QROWS, span)
        scaled = score_grad[None] * weight[spot, :].reshape(heads_step, QROWS, 1)
        coef[spot, :] = (
            jnp.where(logits > 0, scaled, 0.0).astype(jnp.bfloat16).reshape(rows, span)
        )
        weight_grad[spot, :] = jnp.sum(
            score_grad[None] * jnp.maximum(logits, 0.0), axis=-1, keepdims=True
        ).reshape(rows, 1)
    query_grad[...] = jnp.dot(coef[...], keys[...], preferred_element_type=jnp.float32)
    flat = jnp.dot(iq_t[...], coef[...], preferred_element_type=jnp.float32)
    lanes = key_grad.shape[0] * key_grad.shape[1]
    for lane in range(lanes):
        key_grad[lane % 2, lane // 2] = flat[:, lane * TILE : (lane + 1) * TILE]


def whole(shape):
    return pl.BlockSpec(shape, lambda *_: (0,) * len(shape))


def one_hot_rows(table, block):
    a, b = table.shape
    eye = jnp.eye(block, dtype=table.dtype)
    return (table[:, None, :, None] * eye[None, :, None, :]).reshape(a * block, b * block)


def body(main_query, key_latent, index_query, index_key, index_weight, selection, loss_grad):
    bf16, f32 = jnp.bfloat16, jnp.float32
    ctx_index = lax.axis_index(CTX)
    ctx_count = lax.axis_size(CTX)
    lane = lax.axis_index(HEAD)
    lanes = lax.axis_size(HEAD)
    yl, x, core = lax.axis_index("yl"), lax.axis_index("x"), lax.axis_index("core")
    x_count = lax.axis_size("x")
    query_rows, main_local, lat_width = main_query.shape
    index_local, idx_width = index_query.shape[1:]
    key_tiles = key_latent.shape[0] // TILE
    sel_count = selection.shape[1]
    key_span = sel_count * TILE
    context = key_tiles * TILE * ctx_count
    width = idx_width + lat_width
    swap = [(0, 1), (1, 0)]

    owner = selection // key_tiles
    inner = selection % key_tiles
    earlier = jnp.tril(jnp.ones((sel_count, sel_count), jnp.int32), -1)
    rank = jnp.sum((owner[:, :, None] == owner[:, None, :]) * earlier[None], axis=2)
    ranks = jnp.arange(OWNER_MOST)
    picked = lax.dynamic_index_in_dim(selection, ctx_index, 0, keepdims=False)
    my_owner = lax.dynamic_index_in_dim(owner, ctx_index, 0, keepdims=False)
    my_rank = lax.dynamic_index_in_dim(rank, ctx_index, 0, keepdims=False)
    sent = jnp.any(
        (owner[:, None, :, None] == ctx_index)
        & (rank[:, None, :, None] == ranks[None, :, None, None])
        & (inner[:, None, :, None] == jnp.arange(key_tiles)[None, None, None, :]),
        axis=2,
    ).reshape(ctx_count * OWNER_MOST, key_tiles)
    got = (
        (my_owner[:, None, None] == jnp.arange(ctx_count)[None, :, None])
        & (my_rank[:, None, None] == ranks[None, None, :])
    ).reshape(sel_count, ctx_count * OWNER_MOST)

    own = jnp.concatenate([index_key, key_latent], axis=1)
    own = own.reshape(key_tiles, lanes, STRIPE, width)
    own = lax.dynamic_index_in_dim(own, lane, 1, keepdims=False).reshape(key_tiles * STRIPE, width)
    send = jnp.dot(one_hot_rows(sent.astype(bf16), STRIPE), own, preferred_element_type=bf16)
    arrived = lax.all_to_all(send, CTX, 0, 0, tiled=True)
    stripe = jnp.dot(one_hot_rows(got.astype(bf16), STRIPE), arrived, preferred_element_type=bf16)

    by_head = jnp.transpose(main_query, (1, 0, 2))
    half = query_rows // 2
    q_own = lax.dynamic_slice_in_dim(by_head, core * half, half, 1)
    q_other = lax.ppermute(
        lax.dynamic_slice_in_dim(by_head, (1 - core) * half, half, 1), "core", swap
    )

    near = jnp.stack([stripe, lax.ppermute(stripe, "yl", swap)])
    pieces = [near]
    for shift in range(1, x_count):
        ring = [(i, (i + shift) % x_count) for i in range(x_count)]
        pieces.append(lax.ppermute(near, "x", ring))
    pieces += [lax.ppermute(piece, "core", swap) for piece in pieces]
    place = jnp.stack(
        [
            ((yl ^ j) * x_count + (x - shift) % x_count) * 2 + (core ^ k)
            for k in range(2)
            for shift in range(x_count)
            for j in range(2)
        ]
    ).astype(jnp.int32)

    iq, _ = lax.optimization_barrier((index_query, stripe))
    iq = iq.reshape(lanes, QROWS, index_local, idx_width).transpose(0, 2, 1, 3)
    iq = lax.all_to_all(iq, ROWS, 0, 0, tiled=True).reshape(-1, idx_width)
    heads_all = lanes * index_local
    weight = lax.all_gather(index_weight, ROWS, axis=0, tiled=False)
    chunk = core * (lanes // 2) + yl * x_count + x
    weight = lax.dynamic_slice_in_dim(weight, chunk * QROWS, QROWS, 1)
    weight = weight.transpose(0, 2, 1).reshape(heads_all * QROWS, 1)
    grad_rows = lax.dynamic_slice_in_dim(loss_grad, chunk * QROWS, QROWS, 0).reshape(QROWS, 1)

    key_pos = (
        jnp.arange(lanes)[:, None, None] * STRIPE
        + picked[None, :, None] * TILE
        + jnp.arange(STRIPE)[None, None, :]
    ).reshape(1, key_span)
    block_first = context - query_rows * ctx_count + ctx_index * query_rows
    half_first = (block_first + core * half).reshape(1).astype(jnp.int32)
    chunk_first = (block_first + chunk * QROWS).reshape(1).astype(jnp.int32)

    params = pltpu.CompilerParams(vmem_limit_bytes=VMEM)
    q_spec = pl.BlockSpec((main_local, QROWS, lat_width), lambda i, *_: (0, i, 0))
    steps = half // QROWS
    target_part, index_keys = pl.pallas_call(
        attend_kernel,
        grid_spec=pltpu.PrefetchScalarGridSpec(
            num_scalar_prefetch=2,
            grid=(steps,),
            in_specs=[whole((2, TILE, width))] * 8 + [q_spec, q_spec, whole((1, key_span))],
            out_specs=[
                pl.BlockSpec((QROWS, key_span), lambda i, *_: (i, 0)),
                whole((key_span, idx_width)),
            ],
            scratch_shapes=[pltpu.VMEM((key_span, width), bf16)],
        ),
        out_shape=[
            jax.ShapeDtypeStruct((half, key_span), f32),
            jax.ShapeDtypeStruct((key_span, idx_width), bf16),
        ],
        compiler_params=params,
        cost_estimate=pl.CostEstimate(
            flops=4 * main_local * half * key_span * lat_width,
            bytes_accessed=8 * 2**20,
            transcendentals=2 * main_local * half * key_span,
        ),
        name="attend",
    )(place, half_first, *pieces, q_own, q_other, key_pos)

    target_parts = lax.all_to_all(target_part, ("yl", "x"), 0, 0, tiled=True)
    target_parts = target_parts.reshape(steps, QROWS, key_span)

    score = pl.pallas_call(
        score_kernel,
        out_shape=jax.ShapeDtypeStruct((QROWS, key_span), f32),
        compiler_params=params,
        cost_estimate=pl.CostEstimate(
            flops=2 * heads_all * QROWS * key_span * idx_width,
            bytes_accessed=2**20,
            transcendentals=0,
        ),
        name="score",
    )(iq, weight, index_keys)

    rows_all = heads_all * QROWS
    vmem = pl.BlockSpec(memory_space=pltpu.VMEM)
    query_grad, weight_grad, key_part, loss = pl.pallas_call(
        grad_kernel,
        in_specs=[pl.BlockSpec(memory_space=pltpu.SMEM)] + [vmem] * 8,
        out_shape=[
            jax.ShapeDtypeStruct((rows_all, idx_width), f32),
            jax.ShapeDtypeStruct((rows_all, 1), f32),
            jax.ShapeDtypeStruct((2, lanes // 2, idx_width, TILE), f32),
            jax.ShapeDtypeStruct((QROWS, 1), f32),
        ],
        scratch_shapes=[pltpu.VMEM((rows_all, key_span), bf16)],
        compiler_params=params,
        cost_estimate=pl.CostEstimate(
            flops=6 * rows_all * key_span * idx_width,
            bytes_accessed=4 * 2**20,
            transcendentals=0,
        ),
        name="grad",
    )(chunk_first, target_parts, score, iq, iq.T, weight, index_keys, key_pos, grad_rows)

    exact = lax.Precision.HIGHEST
    key_keep = lax.dynamic_index_in_dim(key_part, core, 0, keepdims=False)
    key_give = lax.dynamic_index_in_dim(key_part, 1 - core, 0, keepdims=False)
    key_sum = key_keep + lax.ppermute(key_give, "core", swap)
    key_sum = jnp.sum(
        lax.all_to_all(key_sum, ("yl", "x"), 0, 0, tiled=True), axis=0
    )
    back = lax.dot_general(
        one_hot_rows(got.astype(f32), STRIPE), key_sum, (((0,), (1,)), ((), ())), precision=exact
    )
    back = lax.all_to_all(back, CTX, 0, 0, tiled=True)
    own_blocks = lax.dot_general(
        one_hot_rows(sent.astype(f32), STRIPE), back, (((0,), (0,)), ((), ())), precision=exact
    ).reshape(key_tiles, STRIPE, idx_width)
    order = jnp.arange(lanes)
    natural = order % (lanes // 2) * 2 + order // (lanes // 2)
    goes = (jnp.arange(key_tiles)[None, :] * lanes + lane) // key_tiles == natural[:, None]
    key_send = jnp.sum(jnp.where(goes[:, :, None, None], own_blocks[None], 0.0), axis=1)

    small = jnp.concatenate(
        [
            weight_grad.reshape(lanes, index_local * QROWS),
            jnp.broadcast_to(loss.reshape(1, QROWS), (lanes, QROWS)),
            jnp.zeros((lanes, idx_width - (index_local + 1) * QROWS), f32),
        ],
        axis=1,
    ).reshape(lanes, 1, idx_width)
    packed = jnp.concatenate(
        [query_grad.reshape(lanes, index_local * QROWS, idx_width), key_send, small], axis=1
    )
    packed = lax.all_to_all(packed, ROWS, 0, 0, tiled=True)
    heads_rows = index_local * QROWS
    query_out = packed[:, :heads_rows].reshape(lanes, index_local, QROWS, idx_width)
    query_out = query_out.transpose(0, 2, 1, 3).reshape(query_rows, index_local, idx_width)
    blocks = packed[:, heads_rows : heads_rows + STRIPE]
    source = (lane * key_tiles + jnp.arange(key_tiles)) % lanes
    source = source % 2 * (lanes // 2) + source // 2
    comes = source[:, None] == order[None, :]
    key_out = jnp.sum(jnp.where(comes[:, :, None, None], blocks[None], 0.0), axis=1)
    key_out = key_out.reshape(key_tiles * STRIPE, idx_width)
    small = packed[:, heads_rows + STRIPE]
    weight_out = small[:, :heads_rows].reshape(lanes, index_local, QROWS)
    weight_out = weight_out.transpose(0, 2, 1).reshape(query_rows, index_local)
    loss_out = small[:, heads_rows : heads_rows + QROWS].reshape(query_rows)
    return (query_out, weight_out, key_out, loss_out)


def solution(mesh):
    fine = Mesh(mesh.devices.reshape(8, 2, 2, 4, 2), CTX + HEAD)
    return jax.shard_map(
        body,
        mesh=fine,
        in_specs=(
            P(CTX, HEAD, None),
            P(CTX, None),
            P(CTX, HEAD, None),
            P(CTX, None),
            P(CTX, HEAD),
            P(),
            P(CTX),
        ),
        out_specs=(P(CTX, HEAD, None), P(CTX, HEAD), P(CTX + HEAD, None), P(CTX)),
        check_vma=False,
    )
```

```python
import math

import jax
import jax.numpy as jnp
from jax import lax
from jax.experimental import pallas as pl
from jax.experimental.pallas import tpu as pltpu
from jax.sharding import Mesh, PartitionSpec as P

TILE = 128
MLA_HEADS = 128
OWNER_MOST = 3
QROWS = 16
STRIPE = 8
VMEM = 60 * 1024 * 1024

PICKED, FIRSTS, CHUNKS = 16, 32, 34

CTX = ("z", "yh")
HEAD = ("yl", "x", "core")
ROWS = ("x", "core", "yl")
exp_scale = 192.0 ** (-0.5) * math.log2(math.e)
far_below = -1e30


def allowed_keys(query_first, key_pos):
    rows = lax.broadcasted_iota(jnp.int32, (QROWS, key_pos.shape[1]), 0)
    return key_pos <= rows + query_first


def stripes_kernel(where, selection, index_key, key_latent, send):
    ctx, lane = where[0], where[1]
    rows, (blocks, slots) = send.shape[0], selection.shape
    per_block = OWNER_MOST * STRIPE
    tiles = key_latent.shape[0] // TILE
    row = lax.broadcasted_iota(jnp.int32, (rows, slots), 0)
    slot = lax.broadcasted_iota(jnp.int32, (rows, slots), 1)
    first = slot * per_block
    repeat = ((row >= first) & (row < first + per_block)).astype(jnp.float32)
    picked = jnp.dot(
        repeat.astype(jnp.bfloat16),
        selection[...].astype(jnp.float32).astype(jnp.bfloat16),
        preferred_element_type=jnp.float32,
    ).astype(jnp.int32)
    inner = picked - ctx * tiles
    mine = (inner >= 0) & (inner < tiles)
    a = lax.broadcasted_iota(jnp.int32, (slots, slots), 0)
    b = lax.broadcasted_iota(jnp.int32, (slots, slots), 1)
    earlier = (a < b).astype(jnp.float32).astype(jnp.bfloat16)
    rank = jnp.dot(
        mine.astype(jnp.float32).astype(jnp.bfloat16), earlier, preferred_element_type=jnp.float32
    ).astype(jnp.int32)
    block = jnp.sum(jnp.where(repeat > 0, slot, 0), axis=1, keepdims=True)
    row = lax.broadcasted_iota(jnp.int32, (rows, 1), 0)
    wanted = lax.shift_right_logical(row - block * per_block, 3)
    source = inner * TILE + lane * STRIPE + (row & (STRIPE - 1)) + 1
    source = jnp.sum(jnp.where(mine & (rank == wanted), source, 0), axis=1, keepdims=True) - 1
    spot = lax.broadcasted_iota(jnp.int32, (rows, key_latent.shape[0]), 1)
    pick = (spot == source).astype(jnp.float32).astype(jnp.bfloat16)
    for part, cols in ((index_key, slice(0, TILE)), (key_latent, slice(TILE, None))):
        send[:, cols] = jnp.dot(pick, part[...], preferred_element_type=jnp.float32).astype(
            jnp.bfloat16
        )


def attend_rows(chunk, q_parts, keys, target, q_rows, raw, total):
    heads, width = q_parts[0].shape[-2:]
    spare = q_rows.shape[1] - width
    part_rows = QROWS * heads
    shape = (QROWS, heads, spare)
    column = lax.broadcasted_iota(jnp.int32, shape, 2)
    row = lax.broadcasted_iota(jnp.int32, shape, 0)
    hot = (column == row + chunk * QROWS).astype(jnp.float32)
    hot = hot.reshape(part_rows, spare).astype(jnp.bfloat16)
    for i, part in enumerate(q_parts):
        spot = slice(i * part_rows, (i + 1) * part_rows)
        rows = part[...].reshape(QROWS, heads, width).astype(jnp.float32)
        q_rows[spot, :width] = rows.reshape(part_rows, width).astype(jnp.bfloat16)
        q_rows[spot, width:] = hot
    group = raw[0].shape[0]

    def scores(step):
        raw[step % 2][...] = lax.dot_general(
            q_rows[step * group : (step + 1) * group, :],
            keys[:, TILE:],
            (((1,), (1,)), ((), ())),
            preferred_element_type=jnp.float32,
        )

    def softmax(step):
        for start in range(0, group, QROWS):
            part = raw[step % 2][start : start + QROWS, :]
            top = jnp.max(part, axis=-1, keepdims=True)
            weights = jnp.exp2((part - top) * exp_scale)
            share = 1.0 / (jnp.sum(weights, axis=-1, keepdims=True) * MLA_HEADS)
            spot = slice(start % part_rows, start % part_rows + QROWS)
            if step == 0 and start < part_rows:
                total[spot, :] = weights * share
            else:
                total[spot, :] += weights * share

    steps = q_rows.shape[0] // group
    for step in range(steps):
        scores(step)
        if step:
            softmax(step - 1)
    softmax(steps - 1)
    target[...] = jnp.sum(total[...].reshape(QROWS, heads, total.shape[1]), axis=1)


def attend_first_kernel(facts, *refs):
    pieces, q_parts, (target, keys, q_rows, total, *raw) = refs[:16], refs[16:24], refs[24:]
    width = pieces[0].shape[1]
    spare = keys.shape[1] - width
    picked = [facts[PICKED + slot] * TILE for slot in range(TILE // STRIPE)]
    row = lax.broadcasted_iota(jnp.int32, (STRIPE, spare), 0)
    key_pos = jnp.concatenate([row + first for first in picked], axis=0)
    column = lax.broadcasted_iota(jnp.int32, (TILE, spare), 1)
    last = jnp.where(column < QROWS, column + facts[FIRSTS], column - QROWS + facts[FIRSTS + 1])
    last = jnp.where(column < 2 * QROWS, last, 2**30)
    for i, piece in enumerate(pieces):
        spot = pl.ds(pl.multiple_of(facts[i] * TILE, TILE), TILE)
        keys[spot, :width] = piece[...]
        late = key_pos + facts[i] * STRIPE > last
        keys[spot, width:] = jnp.where(late, far_below, 0.0).astype(jnp.bfloat16)
    attend_rows(0, q_parts, keys, target, q_rows, raw, total)


def attend_second_kernel(facts, *refs):
    q_parts, (keys, target, q_rows, total, *raw) = refs[:8], refs[8:]
    attend_rows(1, q_parts, keys, target, q_rows, raw, total)


def row_groups(rows, heads):
    row = lax.broadcasted_iota(jnp.int32, (rows, rows * heads), 0) * heads
    both = lax.broadcasted_iota(jnp.int32, (rows, rows * heads), 1)
    return ((both >= row) & (both < row + heads)).astype(jnp.float32)


def index_logits(queries, keys, step, count):
    block = queries[step * count : (step + 1) * count, :, :TILE]
    return lax.dot_general(
        block.reshape(-1, TILE),
        keys[...],
        (((1,), (1,)), ((), ())),
        preferred_element_type=jnp.float32,
    ).reshape(count, -1, keys.shape[0])


def index_weights(queries, step, count):
    terms = queries[step * count : (step + 1) * count, :, TILE : 2 * TILE].astype(jnp.float32)
    return terms[:, :, 0:1] + terms[:, :, 1:2] + terms[:, :, 2:3]


def score_kernel(queries, keys, score):
    count = 2
    heads_rows = queries.shape[1]
    total = jnp.zeros((heads_rows, keys.shape[0]), jnp.float32)
    for step in range(queries.shape[0] // count):
        lifted = jnp.maximum(index_logits(queries, keys, step, count), 0.0)
        total = total + jnp.sum(lifted * index_weights(queries, step, count), axis=0)
    score[...] = jnp.dot(
        row_groups(QROWS, heads_rows // QROWS),
        total,
        precision=lax.Precision.HIGHEST,
        preferred_element_type=jnp.float32,
    )


def grad_kernel(
    facts, target_own, target_other, score, queries, keys, key_pos, loss_grad,
    query_grad, weight_grad, key_grad, loss, coef
):
    allowed = allowed_keys(facts[FIRSTS + 1], key_pos[...])
    target = target_own[...] + target_other[...]
    masked = jnp.where(allowed, score[...], far_below)
    shifted = masked - jnp.max(masked, axis=-1, keepdims=True)
    weights = jnp.where(allowed, jnp.exp(shifted), 0.0)
    row_sum = jnp.sum(weights, axis=-1, keepdims=True)
    log_prob = shifted - jnp.log(row_sum)
    positive = target > 0
    self_term = jnp.where(positive, target * jnp.log(jnp.where(positive, target, 1.0)), 0.0)
    loss[...] = jnp.sum(
        jnp.where(allowed, self_term - target * log_prob, 0.0), axis=-1, keepdims=True
    )
    score_grad = loss_grad[...] * jnp.where(allowed, weights / row_sum - target, 0.0)
    count = 2
    sources, heads_rows = queries.shape[:2]
    score_grad = lax.dot_general(
        row_groups(QROWS, heads_rows // QROWS),
        score_grad,
        (((0,), (0,)), ((), ())),
        precision=lax.Precision.HIGHEST,
        preferred_element_type=jnp.float32,
    )[None]
    rows = count * heads_rows
    for step in range(sources // count):
        spot = slice(step * rows, (step + 1) * rows)
        logits = index_logits(queries, keys, step, count)
        scaled = score_grad * index_weights(queries, step, count)
        scaled = jnp.where(logits > 0, scaled, 0.0).reshape(rows, -1)
        coef[spot, :] = scaled.astype(jnp.bfloat16)
        lifted = score_grad * jnp.maximum(logits, 0.0)
        weight_grad[spot, :] = jnp.sum(lifted, axis=-1, keepdims=True).reshape(rows, 1)
    query_grad[...] = jnp.dot(coef[...], keys[...], preferred_element_type=jnp.float32)
    flat = queries[:, :, :TILE].reshape(sources * heads_rows, TILE)
    flat = lax.dot_general(
        flat, coef[...], (((0,), (0,)), ((), ())), preferred_element_type=jnp.float32
    )
    for lane in range(key_grad.shape[0] * key_grad.shape[1]):
        key_grad[lane % 2, lane // 2] = flat[:, lane * TILE : (lane + 1) * TILE]


def whole(shape):
    return pl.BlockSpec(shape, lambda *_: (0,) * len(shape))


def one_hot_rows(table, block):
    a, b = table.shape
    eye = jnp.eye(block, dtype=table.dtype)
    return (table[:, None, :, None] * eye[None, :, None, :]).reshape(a * block, b * block)


def body(main_query, key_latent, index_query, index_key, index_weight, selection, loss_grad):
    bf16, f32 = jnp.bfloat16, jnp.float32
    ctx_index = lax.axis_index(CTX)
    ctx_count = lax.axis_size(CTX)
    lane = lax.axis_index(HEAD)
    lanes = lax.axis_size(HEAD)
    yl, x, core = lax.axis_index("yl"), lax.axis_index("x"), lax.axis_index("core")
    x_count = lax.axis_size("x")
    query_rows, main_local, lat_width = main_query.shape
    index_local, idx_width = index_query.shape[1:]
    key_tiles = key_latent.shape[0] // TILE
    sel_count = selection.shape[1]
    key_span = sel_count * TILE
    context = key_tiles * TILE * ctx_count
    width = idx_width + lat_width
    wide = width + 64
    heads_all = lanes * index_local
    rows_all = heads_all * QROWS
    heads_rows = index_local * QROWS
    swap = [(0, 1), (1, 0)]
    params = pltpu.CompilerParams(vmem_limit_bytes=VMEM)
    vmem = pl.BlockSpec(memory_space=pltpu.VMEM)
    smem = pl.BlockSpec(memory_space=pltpu.SMEM)

    def shifted(value, shift):
        ring = [(i, (i + shift) % x_count) for i in range(x_count)]
        return lax.ppermute(value, "x", ring)

    send = pl.pallas_call(
        stripes_kernel,
        in_specs=[smem, vmem, vmem, vmem],
        out_shape=jax.ShapeDtypeStruct((ctx_count * OWNER_MOST * STRIPE, width), bf16),
        compiler_params=params,
        name="stripes",
    )(jnp.stack([ctx_index, lane]).astype(jnp.int32), selection, index_key, key_latent)
    arrived = lax.all_to_all(send, CTX, 0, 0, tiled=True)

    part_rows = query_rows // x_count
    half = part_rows // 2
    q_near = [
        shifted(
            lax.dynamic_slice_in_dim(main_query, (x + shift) % x_count * part_rows, part_rows, 0),
            shift,
        )
        for shift in range(1, x_count)
    ]
    q_far = jnp.stack(
        [lax.dynamic_slice_in_dim(main_query, x * part_rows + (1 - core) * half, half, 0)]
        + [lax.dynamic_slice_in_dim(part, (1 - core) * half, half, 0) for part in q_near]
    )
    q_far = lax.ppermute(q_far, "core", swap)

    first_term = lax.reduce_precision(index_weight, 8, 7)
    rest = index_weight - first_term
    second_term = lax.reduce_precision(rest, 8, 7)
    terms = jnp.stack([first_term, second_term, rest - second_term], axis=-1).astype(bf16)
    iq = jnp.concatenate(
        [index_query, jnp.pad(terms, ((0, 0), (0, 0), (0, idx_width - 3)))], axis=-1
    ).reshape(lanes, heads_rows, 2 * idx_width)

    owner = selection // key_tiles
    inner = selection % key_tiles
    earlier = jnp.tril(jnp.ones((sel_count, sel_count), jnp.int32), -1)
    rank = jnp.sum((owner[:, :, None] == owner[:, None, :]) * earlier[None], axis=2)
    ranks = jnp.arange(OWNER_MOST)
    picked = lax.dynamic_index_in_dim(selection, ctx_index, 0, keepdims=False)
    my_owner = lax.dynamic_index_in_dim(owner, ctx_index, 0, keepdims=False)
    my_rank = lax.dynamic_index_in_dim(rank, ctx_index, 0, keepdims=False)
    sent = jnp.any(
        (owner[:, None, :, None] == ctx_index)
        & (rank[:, None, :, None] == ranks[None, :, None, None])
        & (inner[:, None, :, None] == jnp.arange(key_tiles)[None, None, None, :]),
        axis=2,
    ).reshape(ctx_count * OWNER_MOST, key_tiles)
    got = (
        (my_owner[:, None, None] == jnp.arange(ctx_count)[None, :, None])
        & (my_rank[:, None, None] == ranks[None, None, :])
    ).reshape(sel_count, ctx_count * OWNER_MOST)
    got_rows = one_hot_rows(got.astype(bf16), STRIPE)
    sent_rows = one_hot_rows(sent.astype(bf16), STRIPE)
    chunk = x * 4 + core * 2 + yl
    grad_rows = lax.dynamic_slice_in_dim(loss_grad, chunk * QROWS, QROWS, 0).reshape(QROWS, 1)
    key_pos = (
        jnp.arange(lanes)[:, None, None] * STRIPE
        + picked[None, :, None] * TILE
        + jnp.arange(STRIPE)[None, None, :]
    ).reshape(1, key_span)
    place = [
        ((yl ^ j) * x_count + (x - shift) % x_count) * 2 + (core ^ k)
        for k in range(2)
        for j in range(2)
        for shift in (0, 1, 3, 2)
    ]
    block_first = context - query_rows * ctx_count + ctx_index * query_rows
    mine = x * 4 + core * 2
    firsts = [block_first + (mine + 1 - yl) * QROWS, block_first + (mine + yl) * QROWS]
    chunks = [mine + 1 - yl, core * 2 + 1 - yl, 1 - yl, mine + yl, core * 2 + yl, yl]
    facts = jnp.concatenate([jnp.stack(place), picked, jnp.stack(firsts + chunks)])
    facts = facts.astype(jnp.int32)
    arrived, got_rows, sent_rows, key_pos, grad_rows, facts, iq = lax.optimization_barrier(
        (arrived, got_rows, sent_rows, key_pos, grad_rows, facts, iq)
    )
    stripe = jnp.dot(got_rows, arrived, preferred_element_type=bf16)

    iq = lax.all_to_all(iq, ROWS, 0, 0, tiled=True)
    other = lax.ppermute(stripe, "yl", swap)
    pieces = [stripe] + [shifted(stripe, shift) for shift in (1, 3, 2)]
    pieces += [other] + [shifted(other, shift) for shift in (1, 3, 2)]
    *pieces, iq = lax.optimization_barrier((*pieces, iq))
    pieces += [lax.ppermute(piece, "core", swap) for piece in pieces]

    steps = 4
    q_count = 2 * x_count * main_local * QROWS
    attend_scratch = [pltpu.VMEM((q_count, wide - idx_width), bf16)]
    attend_scratch += [pltpu.VMEM((QROWS * main_local, key_span), f32)]
    attend_scratch += [pltpu.VMEM((q_count // steps, key_span), f32)] * 2
    q_block = (QROWS, main_local, lat_width)

    def q_specs(at):
        specs = [pl.BlockSpec(q_block, lambda i, facts: (facts[CHUNKS + at], 0, 0))]
        specs += [pl.BlockSpec(q_block, lambda i, facts: (facts[CHUNKS + at + 1], 0, 0))] * 3
        specs += [
            pl.BlockSpec((1, *q_block), lambda i, facts, s=s: (s, facts[CHUNKS + at + 2], 0, 0))
            for s in range(x_count)
        ]
        return specs

    q_parts = [main_query, *q_near] + [q_far] * x_count
    cost = pl.CostEstimate(
        flops=2 * q_count * key_span * (wide - idx_width),
        bytes_accessed=8 * 2**20,
        transcendentals=q_count * key_span,
    )
    target_given, keys = pl.pallas_call(
        attend_first_kernel,
        grid_spec=pltpu.PrefetchScalarGridSpec(
            num_scalar_prefetch=1,
            grid=(1,),
            in_specs=[whole((TILE, width))] * 16 + q_specs(0),
            out_specs=[whole((QROWS, key_span)), whole((key_span, wide))],
            scratch_shapes=attend_scratch,
        ),
        out_shape=[
            jax.ShapeDtypeStruct((QROWS, key_span), f32),
            jax.ShapeDtypeStruct((key_span, wide), bf16),
        ],
        compiler_params=params,
        cost_estimate=cost,
        name="attend_first",
    )(facts, *pieces, *q_parts)
    target_other = lax.ppermute(target_given, "yl", swap)
    target_own = pl.pallas_call(
        attend_second_kernel,
        grid_spec=pltpu.PrefetchScalarGridSpec(
            num_scalar_prefetch=1,
            grid=(1,),
            in_specs=q_specs(3) + [whole((key_span, wide))],
            out_specs=whole((QROWS, key_span)),
            scratch_shapes=attend_scratch,
        ),
        out_shape=jax.ShapeDtypeStruct((QROWS, key_span), f32),
        compiler_params=params,
        cost_estimate=cost,
        name="attend_second",
    )(facts, *q_parts, keys)

    index_keys = pl.BlockSpec((key_span, idx_width), lambda i: (0, 0))
    score = pl.pallas_call(
        score_kernel,
        grid=(1,),
        in_specs=[whole(iq.shape), index_keys],
        out_specs=whole((QROWS, key_span)),
        out_shape=jax.ShapeDtypeStruct((QROWS, key_span), f32),
        compiler_params=params,
        cost_estimate=pl.CostEstimate(
            flops=2 * rows_all * key_span * idx_width, bytes_accessed=2**20, transcendentals=0
        ),
        name="score",
    )(iq, keys)

    query_grad, weight_grad, key_part, loss = pl.pallas_call(
        grad_kernel,
        grid=(1,),
        in_specs=[smem]
        + [whole((QROWS, key_span))] * 3
        + [whole(iq.shape), index_keys, whole((1, key_span)), whole((QROWS, 1))],
        out_specs=[
            whole((rows_all, idx_width)),
            whole((rows_all, 1)),
            whole((2, lanes // 2, idx_width, TILE)),
            whole((QROWS, 1)),
        ],
        out_shape=[
            jax.ShapeDtypeStruct((rows_all, idx_width), f32),
            jax.ShapeDtypeStruct((rows_all, 1), f32),
            jax.ShapeDtypeStruct((2, lanes // 2, idx_width, TILE), f32),
            jax.ShapeDtypeStruct((QROWS, 1), f32),
        ],
        scratch_shapes=[pltpu.VMEM((rows_all, key_span), bf16)],
        compiler_params=params,
        cost_estimate=pl.CostEstimate(
            flops=6 * rows_all * key_span * idx_width, bytes_accessed=4 * 2**20, transcendentals=0
        ),
        name="grad",
    )(facts, target_own, target_other, score, iq, keys, key_pos, grad_rows)

    exact = lax.Precision.HIGHEST
    key_keep = lax.dynamic_index_in_dim(key_part, core, 0, keepdims=False)
    key_give = lax.dynamic_index_in_dim(key_part, 1 - core, 0, keepdims=False)
    key_sum = key_keep + lax.ppermute(key_give, "core", swap)
    key_sum = jnp.sum(
        lax.all_to_all(key_sum, ("yl", "x"), 0, 0, tiled=True), axis=0
    )
    back = lax.dot_general(
        got_rows.astype(f32), key_sum, (((0,), (1,)), ((), ())), precision=exact
    )
    back = lax.all_to_all(back, CTX, 0, 0, tiled=True)
    own_blocks = lax.dot_general(
        sent_rows.astype(f32), back, (((0,), (0,)), ((), ())), precision=exact
    ).reshape(key_tiles, STRIPE, idx_width)
    order = jnp.arange(lanes)
    natural = order % 2 * (lanes // 2) + order // 2
    goes = (jnp.arange(key_tiles)[None, :] * lanes + lane) // key_tiles == natural[:, None]
    key_send = jnp.sum(jnp.where(goes[:, :, None, None], own_blocks[None], 0.0), axis=1)

    small = jnp.concatenate(
        [
            weight_grad.reshape(lanes, heads_rows),
            jnp.broadcast_to(loss.reshape(1, QROWS), (lanes, QROWS)),
            jnp.zeros((lanes, idx_width - heads_rows - QROWS), f32),
        ],
        axis=1,
    ).reshape(lanes, 1, idx_width)
    packed = jnp.concatenate(
        [query_grad.reshape(lanes, heads_rows, idx_width), key_send, small], axis=1
    )
    packed = lax.all_to_all(packed, ROWS, 0, 0, tiled=True)
    query_out = packed[:, :heads_rows].reshape(query_rows, index_local, idx_width)
    blocks = packed[:, heads_rows : heads_rows + STRIPE]
    source = (lane * key_tiles + jnp.arange(key_tiles)) % lanes
    source = source % (lanes // 2) * 2 + source // (lanes // 2)
    comes = source[:, None] == order[None, :]
    key_out = jnp.sum(jnp.where(comes[:, :, None, None], blocks[None], 0.0), axis=1)
    key_out = key_out.reshape(key_tiles * STRIPE, idx_width)
    small = packed[:, heads_rows + STRIPE]
    weight_out = small[:, :heads_rows].reshape(query_rows, index_local)
    loss_out = small[:, heads_rows : heads_rows + QROWS].reshape(query_rows)
    return (query_out, weight_out, key_out, loss_out)


def solution(mesh):
    fine = Mesh(mesh.devices.reshape(8, 2, 2, 4, 2), CTX + HEAD)
    return jax.shard_map(
        body,
        mesh=fine,
        in_specs=(
            P(CTX, HEAD, None),
            P(CTX, None),
            P(CTX, HEAD, None),
            P(CTX, None),
            P(CTX, HEAD),
            P(),
            P(CTX),
        ),
        out_specs=(P(CTX, HEAD, None), P(CTX, HEAD), P(CTX + HEAD, None), P(CTX)),
        check_vma=False,
    )
```

```python
import functools
import math

import jax
import jax.numpy as jnp
from jax import lax
from jax.experimental import pallas as pl
from jax.experimental.pallas import tpu as pltpu
from jax.sharding import Mesh, PartitionSpec as P

TILE = 128
MLA_HEADS = 128
OWNER_MOST = 3
QROWS = 16
STRIPE = 8
VMEM = 60 * 1024 * 1024

SLOTS, CORE, FIRST = 16, 18, 19

CTX = ("z", "yh")
HEAD = ("yl", "x", "core")
ROWS = ("core", "yl", "x")
exp_scale = 192.0 ** (-0.5) * math.log2(math.e)
far_below = -1e30


def allowed_keys(query_first, key_pos):
    rows = lax.broadcasted_iota(jnp.int32, (QROWS, key_pos.shape[1]), 0)
    return key_pos <= rows + query_first


def stripes_kernel(where, selection, index_key, key_latent, send):
    ctx, lane = where[0], where[1]
    rows, (blocks, slots) = send.shape[0], selection.shape
    per_block = OWNER_MOST * STRIPE
    tiles = index_key.shape[0] // TILE
    row = lax.broadcasted_iota(jnp.int32, (rows, slots), 0)
    slot = lax.broadcasted_iota(jnp.int32, (rows, slots), 1)
    first = slot * per_block
    repeat = ((row >= first) & (row < first + per_block)).astype(jnp.float32)
    picked = jnp.dot(
        repeat.astype(jnp.bfloat16),
        selection[...].astype(jnp.float32).astype(jnp.bfloat16),
        preferred_element_type=jnp.float32,
    ).astype(jnp.int32)
    inner = picked - ctx * tiles
    mine = (inner >= 0) & (inner < tiles)
    a = lax.broadcasted_iota(jnp.int32, (slots, slots), 0)
    b = lax.broadcasted_iota(jnp.int32, (slots, slots), 1)
    earlier = (a < b).astype(jnp.float32).astype(jnp.bfloat16)
    rank = jnp.dot(
        mine.astype(jnp.float32).astype(jnp.bfloat16), earlier, preferred_element_type=jnp.float32
    ).astype(jnp.int32)
    block = jnp.sum(jnp.where(repeat > 0, slot, 0), axis=1, keepdims=True)
    row = lax.broadcasted_iota(jnp.int32, (rows, 1), 0)
    wanted = lax.shift_right_logical(row - block * per_block, 3)
    source = inner * TILE + lane * STRIPE + (row & (STRIPE - 1)) + 1
    source = jnp.sum(jnp.where(mine & (rank == wanted), source, 0), axis=1, keepdims=True) - 1
    spot = lax.broadcasted_iota(jnp.int32, (rows, index_key.shape[0]), 1)
    pick = (spot == source).astype(jnp.float32).astype(jnp.bfloat16)
    send[:, :TILE] = jnp.dot(pick, index_key[...], preferred_element_type=jnp.float32).astype(
        jnp.bfloat16
    )
    send[:, TILE:] = lax.dot_general(
        pick, key_latent[...], (((1,), (1,)), ((), ())), preferred_element_type=jnp.float32
    ).astype(jnp.bfloat16)


def attend_kernel(facts, *refs):
    pieces, (q_own, q_other, target, index_keys, keys, total, *raw) = refs[:16], refs[16:]
    for i, piece in enumerate(pieces):
        spot = pl.ds(pl.multiple_of(facts[i] * TILE, TILE), TILE)
        index_keys[spot, :] = piece[:, :TILE]
        keys[spot, :] = piece[:, TILE:]
    span = keys.shape[0]
    shape = (STRIPE, 2 * TILE)
    behind = lax.broadcasted_iota(jnp.int32, shape, 0) - (
        lax.broadcasted_iota(jnp.int32, shape, 1) & (TILE - 1)
    )
    behind = behind - facts[CORE] * TILE
    pairs = [(part, head) for part in (q_own, q_other) for head in range(0, part.shape[0], 2)]

    def scores(step):
        part, head = pairs[step]
        both = jnp.concatenate([part[head], part[head + 1]], axis=1)
        out = raw[step % 2]
        out[...] = jnp.dot(keys[...], both, preferred_element_type=jnp.float32)
        for tile in range(2):
            for stripe in range(span // TILE):
                spot = pl.ds(pl.multiple_of(stripe * TILE + facts[SLOTS + tile] * STRIPE, STRIPE), STRIPE)
                late = behind + (tile * TILE + stripe * STRIPE) > 0
                out[spot, :] = jnp.where(late, far_below, out[spot, :])

    def softmax(step):
        part = raw[step % 2]
        spots = [slice(i, i + TILE) for i in range(0, span, TILE)]
        folded = (TILE // 8, 8, 2 * TILE)
        top = functools.reduce(
            jnp.maximum, [jnp.max(part[spot, :].reshape(folded), axis=0) for spot in spots]
        )
        top = jnp.max(top, axis=0, keepdims=True)
        row_sum = jnp.zeros((8, 2 * TILE), jnp.float32)
        for spot in spots:
            weights = jnp.exp2((part[spot, :] - top) * exp_scale)
            part[spot, :] = weights
            row_sum = row_sum + jnp.sum(weights.reshape(folded), axis=0)
        share = 1.0 / (jnp.sum(row_sum, axis=0, keepdims=True) * MLA_HEADS)
        for spot in spots:
            weights = part[spot, :] * share
            weights = weights[:, :TILE] + weights[:, TILE:]
            if step == 0:
                total[spot, :] = weights
            else:
                total[spot, :] += weights

    for step in range(len(pairs)):
        scores(step)
        if step:
            softmax(step - 1)
    softmax(len(pairs) - 1)
    for i in range(0, span, TILE):
        target[:, i : i + TILE] = total[i : i + TILE, :].T


def row_groups(rows, heads):
    row = lax.broadcasted_iota(jnp.int32, (rows, rows * heads), 0) * heads
    both = lax.broadcasted_iota(jnp.int32, (rows, rows * heads), 1)
    return ((both >= row) & (both < row + heads)).astype(jnp.float32)


def index_logits(queries, keys, step, count):
    block = queries[step * count : (step + 1) * count, :, :TILE]
    return lax.dot_general(
        block.reshape(-1, TILE),
        keys[...],
        (((1,), (1,)), ((), ())),
        preferred_element_type=jnp.float32,
    ).reshape(count, -1, keys.shape[0])


def index_weights(queries, step, count):
    terms = queries[step * count : (step + 1) * count, :, TILE : 2 * TILE].astype(jnp.float32)
    return terms[:, :, 0:1] + terms[:, :, 1:2] + terms[:, :, 2:3]


def score_kernel(queries, keys, score):
    count = 2
    heads_rows = queries.shape[1]
    total = jnp.zeros((heads_rows, keys.shape[0]), jnp.float32)
    for step in range(queries.shape[0] // count):
        lifted = jnp.maximum(index_logits(queries, keys, step, count), 0.0)
        total = total + jnp.sum(lifted * index_weights(queries, step, count), axis=0)
    score[...] = jnp.dot(
        row_groups(QROWS, heads_rows // QROWS),
        total,
        precision=lax.Precision.HIGHEST,
        preferred_element_type=jnp.float32,
    )


def grad_kernel(
    facts, target_parts, score, queries, keys, key_pos, loss_grad,
    query_grad, weight_grad, key_grad, loss, coef
):
    allowed = allowed_keys(facts[FIRST], key_pos[...])
    target = jnp.sum(target_parts[...], axis=0)
    masked = jnp.where(allowed, score[...], far_below)
    shifted = masked - jnp.max(masked, axis=-1, keepdims=True)
    weights = jnp.where(allowed, jnp.exp(shifted), 0.0)
    row_sum = jnp.sum(weights, axis=-1, keepdims=True)
    log_prob = shifted - jnp.log(row_sum)
    positive = target > 0
    self_term = jnp.where(positive, target * jnp.log(jnp.where(positive, target, 1.0)), 0.0)
    loss[...] = jnp.sum(
        jnp.where(allowed, self_term - target * log_prob, 0.0), axis=-1, keepdims=True
    )
    score_grad = loss_grad[...] * jnp.where(allowed, weights / row_sum - target, 0.0)
    count = 2
    sources, heads_rows = queries.shape[:2]
    score_grad = lax.dot_general(
        row_groups(QROWS, heads_rows // QROWS),
        score_grad,
        (((0,), (0,)), ((), ())),
        precision=lax.Precision.HIGHEST,
        preferred_element_type=jnp.float32,
    )[None]
    rows = count * heads_rows
    for step in range(sources // count):
        spot = slice(step * rows, (step + 1) * rows)
        logits = index_logits(queries, keys, step, count)
        scaled = score_grad * index_weights(queries, step, count)
        scaled = jnp.where(logits > 0, scaled, 0.0).reshape(rows, -1)
        coef[spot, :] = scaled.astype(jnp.bfloat16)
        lifted = score_grad * jnp.maximum(logits, 0.0)
        weight_grad[spot, :] = jnp.sum(lifted, axis=-1, keepdims=True).reshape(rows, 1)
    query_grad[...] = jnp.dot(coef[...], keys[...], preferred_element_type=jnp.float32)
    flat = queries[:, :, :TILE].reshape(sources * heads_rows, TILE)
    flat = lax.dot_general(
        flat, coef[...], (((0,), (0,)), ((), ())), preferred_element_type=jnp.float32
    )
    for lane in range(key_grad.shape[0] * key_grad.shape[1]):
        key_grad[lane % 2, lane // 2] = flat[:, lane * TILE : (lane + 1) * TILE]


def whole(shape):
    return pl.BlockSpec(shape, lambda *_: (0,) * len(shape))


def one_hot_rows(table, block):
    a, b = table.shape
    eye = jnp.eye(block, dtype=table.dtype)
    return (table[:, None, :, None] * eye[None, :, None, :]).reshape(a * block, b * block)


def body(main_query, key_latent, index_query, index_key, index_weight, selection, loss_grad):
    bf16, f32 = jnp.bfloat16, jnp.float32
    ctx_index = lax.axis_index(CTX)
    ctx_count = lax.axis_size(CTX)
    lane = lax.axis_index(HEAD)
    lanes = lax.axis_size(HEAD)
    yl, x, core = lax.axis_index("yl"), lax.axis_index("x"), lax.axis_index("core")
    x_count = lax.axis_size("x")
    query_rows, main_local, lat_width = main_query.shape
    index_local, idx_width = index_query.shape[1:]
    key_tiles = key_latent.shape[0] // TILE
    sel_count = selection.shape[1]
    key_span = sel_count * TILE
    context = key_tiles * TILE * ctx_count
    width = idx_width + lat_width
    heads_all = lanes * index_local
    rows_all = heads_all * QROWS
    heads_rows = index_local * QROWS
    swap = [(0, 1), (1, 0)]
    params = pltpu.CompilerParams(vmem_limit_bytes=VMEM)
    vmem = pl.BlockSpec(memory_space=pltpu.VMEM)
    smem = pl.BlockSpec(memory_space=pltpu.SMEM)

    def shifted(value, shift):
        ring = [(i, (i + shift) % x_count) for i in range(x_count)]
        return lax.ppermute(value, "x", ring)

    send = pl.pallas_call(
        stripes_kernel,
        in_specs=[smem, vmem, vmem, vmem],
        out_shape=jax.ShapeDtypeStruct((ctx_count * OWNER_MOST * STRIPE, width), bf16),
        compiler_params=params,
        name="stripes",
    )(jnp.stack([ctx_index, lane]).astype(jnp.int32), selection, index_key, key_latent.T)
    arrived = lax.all_to_all(send, CTX, 0, 0, tiled=True)

    queries = jnp.transpose(main_query, (1, 2, 0))
    q_other = lax.dynamic_slice_in_dim(queries, (1 - core) * TILE, TILE, 2)
    q_other = lax.ppermute(q_other, "core", swap)

    first_term = lax.reduce_precision(index_weight, 8, 7)
    rest = index_weight - first_term
    second_term = lax.reduce_precision(rest, 8, 7)
    terms = jnp.stack([first_term, second_term, rest - second_term], axis=-1).astype(bf16)
    iq = jnp.concatenate(
        [index_query, jnp.pad(terms, ((0, 0), (0, 0), (0, idx_width - 3)))], axis=-1
    ).reshape(lanes, heads_rows, 2 * idx_width)

    owner = selection // key_tiles
    inner = selection % key_tiles
    earlier = jnp.tril(jnp.ones((sel_count, sel_count), jnp.int32), -1)
    rank = jnp.sum((owner[:, :, None] == owner[:, None, :]) * earlier[None], axis=2)
    ranks = jnp.arange(OWNER_MOST)
    picked = lax.dynamic_index_in_dim(selection, ctx_index, 0, keepdims=False)
    my_owner = lax.dynamic_index_in_dim(owner, ctx_index, 0, keepdims=False)
    my_rank = lax.dynamic_index_in_dim(rank, ctx_index, 0, keepdims=False)
    sent = jnp.any(
        (owner[:, None, :, None] == ctx_index)
        & (rank[:, None, :, None] == ranks[None, :, None, None])
        & (inner[:, None, :, None] == jnp.arange(key_tiles)[None, None, None, :]),
        axis=2,
    ).reshape(ctx_count * OWNER_MOST, key_tiles)
    got = (
        (my_owner[:, None, None] == jnp.arange(ctx_count)[None, :, None])
        & (my_rank[:, None, None] == ranks[None, None, :])
    ).reshape(sel_count, ctx_count * OWNER_MOST)
    got_rows = one_hot_rows(got.astype(bf16), STRIPE)
    sent_rows = one_hot_rows(sent.astype(bf16), STRIPE)
    chunk = core * (lanes // 2) + yl * x_count + x
    grad_rows = lax.dynamic_slice_in_dim(loss_grad, chunk * QROWS, QROWS, 0).reshape(QROWS, 1)
    key_pos = (
        jnp.arange(lanes)[:, None, None] * STRIPE
        + picked[None, :, None] * TILE
        + jnp.arange(STRIPE)[None, None, :]
    ).reshape(1, key_span)
    place = [
        ((yl ^ j) * x_count + (x - shift) % x_count) * 2 + (core ^ k)
        for k in range(2)
        for j in range(2)
        for shift in (0, 1, 3, 2)
    ]
    block_first = context - query_rows * ctx_count + ctx_index * query_rows
    own = block_first // TILE + jnp.arange(2)
    slots = jnp.argmax(picked[None, :] == own[:, None], axis=1)
    facts = jnp.concatenate(
        [jnp.stack(place), slots, jnp.stack([core, block_first + chunk * QROWS])]
    ).astype(jnp.int32)
    arrived, got_rows, sent_rows, key_pos, grad_rows, facts, iq = lax.optimization_barrier(
        (arrived, got_rows, sent_rows, key_pos, grad_rows, facts, iq)
    )
    stripe = jnp.dot(got_rows, arrived, preferred_element_type=bf16)

    other = lax.ppermute(stripe, "yl", swap)
    pieces = [stripe] + [shifted(stripe, shift) for shift in (1, 3, 2)]
    iq, *pieces = lax.optimization_barrier((iq, *pieces))
    iq = lax.all_to_all(iq, ROWS, 0, 0, tiled=True)
    pieces += [other] + [shifted(other, shift) for shift in (1, 3, 2)]
    pieces += [lax.ppermute(piece, "core", swap) for piece in pieces]

    count = 2 * main_local * TILE
    target_part, index_keys = pl.pallas_call(
        attend_kernel,
        grid_spec=pltpu.PrefetchScalarGridSpec(
            num_scalar_prefetch=1,
            grid=(1,),
            in_specs=[whole((TILE, width))] * 16
            + [
                pl.BlockSpec((main_local, lat_width, TILE), lambda i, facts: (0, 0, facts[CORE])),
                whole((main_local, lat_width, TILE)),
            ],
            out_specs=[whole((TILE, key_span)), whole((key_span, idx_width))],
            scratch_shapes=[
                pltpu.VMEM((key_span, lat_width), bf16),
                pltpu.VMEM((key_span, TILE), f32),
                pltpu.VMEM((key_span, 2 * TILE), f32),
                pltpu.VMEM((key_span, 2 * TILE), f32),
            ],
        ),
        out_shape=[
            jax.ShapeDtypeStruct((TILE, key_span), f32),
            jax.ShapeDtypeStruct((key_span, idx_width), bf16),
        ],
        compiler_params=params,
        cost_estimate=pl.CostEstimate(
            flops=2 * count * key_span * lat_width,
            bytes_accessed=8 * 2**20,
            transcendentals=count * key_span,
        ),
        name="attend",
    )(facts, *pieces, queries, q_other)
    target_parts = lax.all_to_all(target_part, ("yl", "x"), 0, 0, tiled=True)
    target_parts = target_parts.reshape(lanes // 2, QROWS, key_span)

    score = pl.pallas_call(
        score_kernel,
        grid=(1,),
        in_specs=[whole(iq.shape), whole((key_span, idx_width))],
        out_specs=whole((QROWS, key_span)),
        out_shape=jax.ShapeDtypeStruct((QROWS, key_span), f32),
        compiler_params=params,
        cost_estimate=pl.CostEstimate(
            flops=2 * rows_all * key_span * idx_width, bytes_accessed=2**20, transcendentals=0
        ),
        name="score",
    )(iq, index_keys)

    query_grad, weight_grad, key_part, loss = pl.pallas_call(
        grad_kernel,
        grid=(1,),
        in_specs=[smem]
        + [whole((lanes // 2, QROWS, key_span)), whole((QROWS, key_span))]
        + [whole(iq.shape), whole((key_span, idx_width)), whole((1, key_span)), whole((QROWS, 1))],
        out_specs=[
            whole((rows_all, idx_width)),
            whole((rows_all, 1)),
            whole((2, lanes // 2, idx_width, TILE)),
            whole((QROWS, 1)),
        ],
        out_shape=[
            jax.ShapeDtypeStruct((rows_all, idx_width), f32),
            jax.ShapeDtypeStruct((rows_all, 1), f32),
            jax.ShapeDtypeStruct((2, lanes // 2, idx_width, TILE), f32),
            jax.ShapeDtypeStruct((QROWS, 1), f32),
        ],
        scratch_shapes=[pltpu.VMEM((rows_all, key_span), bf16)],
        compiler_params=params,
        cost_estimate=pl.CostEstimate(
            flops=6 * rows_all * key_span * idx_width, bytes_accessed=4 * 2**20, transcendentals=0
        ),
        name="grad",
    )(facts, target_parts, score, iq, index_keys, key_pos, grad_rows)

    exact = lax.Precision.HIGHEST
    key_keep = lax.dynamic_index_in_dim(key_part, core, 0, keepdims=False)
    key_give = lax.dynamic_index_in_dim(key_part, 1 - core, 0, keepdims=False)
    key_sum = key_keep + lax.ppermute(key_give, "core", swap)
    key_sum = jnp.sum(
        lax.all_to_all(key_sum, ("yl", "x"), 0, 0, tiled=True), axis=0
    )
    back = lax.dot_general(
        got_rows.astype(f32), key_sum, (((0,), (1,)), ((), ())), precision=exact
    )
    back = lax.all_to_all(back, CTX, 0, 0, tiled=True)
    own_blocks = lax.dot_general(
        sent_rows.astype(f32), back, (((0,), (0,)), ((), ())), precision=exact
    ).reshape(key_tiles, STRIPE, idx_width)
    order = jnp.arange(lanes)
    natural = order % (lanes // 2) * 2 + order // (lanes // 2)
    goes = (jnp.arange(key_tiles)[None, :] * lanes + lane) // key_tiles == natural[:, None]
    key_send = jnp.sum(jnp.where(goes[:, :, None, None], own_blocks[None], 0.0), axis=1)

    small = jnp.concatenate(
        [
            weight_grad.reshape(lanes, heads_rows),
            jnp.broadcast_to(loss.reshape(1, QROWS), (lanes, QROWS)),
            jnp.zeros((lanes, idx_width - heads_rows - QROWS), f32),
        ],
        axis=1,
    ).reshape(lanes, 1, idx_width)
    packed = jnp.concatenate(
        [query_grad.reshape(lanes, heads_rows, idx_width), key_send, small], axis=1
    )
    packed = lax.all_to_all(packed, ROWS, 0, 0, tiled=True)
    query_out = packed[:, :heads_rows].reshape(query_rows, index_local, idx_width)
    blocks = packed[:, heads_rows : heads_rows + STRIPE]
    source = (lane * key_tiles + jnp.arange(key_tiles)) % lanes
    source = source % 2 * (lanes // 2) + source // 2
    comes = source[:, None] == order[None, :]
    key_out = jnp.sum(jnp.where(comes[:, :, None, None], blocks[None], 0.0), axis=1)
    key_out = key_out.reshape(key_tiles * STRIPE, idx_width)
    small = packed[:, heads_rows + STRIPE]
    weight_out = small[:, :heads_rows].reshape(query_rows, index_local)
    loss_out = small[:, heads_rows : heads_rows + QROWS].reshape(query_rows)
    return (query_out, weight_out, key_out, loss_out)


def solution(mesh):
    fine = Mesh(mesh.devices.reshape(8, 2, 2, 4, 2), CTX + HEAD)
    return jax.shard_map(
        body,
        mesh=fine,
        in_specs=(
            P(CTX, HEAD, None),
            P(CTX, None),
            P(CTX, HEAD, None),
            P(CTX, None),
            P(CTX, HEAD),
            P(),
            P(CTX),
        ),
        out_specs=(P(CTX, HEAD, None), P(CTX, HEAD), P(CTX + HEAD, None), P(CTX)),
        check_vma=False,
    )
```

```python
import functools
import math

import jax
import jax.numpy as jnp
from jax import lax
from jax.experimental import pallas as pl
from jax.experimental.pallas import tpu as pltpu
from jax.sharding import Mesh, PartitionSpec as P

TILE = 128
MLA_HEADS = 128
OWNER_MOST = 3
QROWS = 16
STRIPE = 8
VMEM = 60 * 1024 * 1024

SLOTS, CORE, FIRST, SOURCES = 16, 18, 19, 20

CTX = ("z", "yh")
HEAD = ("yl", "x", "core")
ROWS = ("core", "yl", "x")
exp_scale = 192.0 ** (-0.5) * math.log2(math.e)
far_below = -1e30


def allowed_keys(query_first, key_pos):
    rows = lax.broadcasted_iota(jnp.int32, (QROWS, key_pos.shape[1]), 0)
    return key_pos <= rows + query_first


def stripes_kernel(where, selection, index_key, key_latent, send):
    ctx, lane = where[0], where[1]
    rows, (blocks, slots) = send.shape[0], selection.shape
    per_block = OWNER_MOST * STRIPE
    tiles = index_key.shape[0] // TILE
    row = lax.broadcasted_iota(jnp.int32, (rows, slots), 0)
    slot = lax.broadcasted_iota(jnp.int32, (rows, slots), 1)
    first = slot * per_block
    repeat = ((row >= first) & (row < first + per_block)).astype(jnp.float32)
    picked = jnp.dot(
        repeat.astype(jnp.bfloat16),
        selection[...].astype(jnp.float32).astype(jnp.bfloat16),
        preferred_element_type=jnp.float32,
    ).astype(jnp.int32)
    inner = picked - ctx * tiles
    mine = (inner >= 0) & (inner < tiles)
    a = lax.broadcasted_iota(jnp.int32, (slots, slots), 0)
    b = lax.broadcasted_iota(jnp.int32, (slots, slots), 1)
    earlier = (a < b).astype(jnp.float32).astype(jnp.bfloat16)
    rank = jnp.dot(
        mine.astype(jnp.float32).astype(jnp.bfloat16), earlier, preferred_element_type=jnp.float32
    ).astype(jnp.int32)
    block = jnp.sum(jnp.where(repeat > 0, slot, 0), axis=1, keepdims=True)
    row = lax.broadcasted_iota(jnp.int32, (rows, 1), 0)
    wanted = lax.shift_right_logical(row - block * per_block, 3)
    source = inner * TILE + lane * STRIPE + (row & (STRIPE - 1)) + 1
    source = jnp.sum(jnp.where(mine & (rank == wanted), source, 0), axis=1, keepdims=True) - 1
    spot = lax.broadcasted_iota(jnp.int32, (rows, index_key.shape[0]), 1)
    pick = (spot == source).astype(jnp.float32).astype(jnp.bfloat16)
    send[:, :TILE] = jnp.dot(pick, index_key[...], preferred_element_type=jnp.float32).astype(
        jnp.bfloat16
    )
    send[:, TILE:] = lax.dot_general(
        pick, key_latent[...], (((1,), (1,)), ((), ())), preferred_element_type=jnp.float32
    ).astype(jnp.bfloat16)


def attend_kernel(facts, *refs):
    pieces, (q_own, q_other, target, index_keys, keys, total, *raw) = refs[:16], refs[16:]
    for i, piece in enumerate(pieces):
        spot = pl.ds(pl.multiple_of(facts[i] * TILE, TILE), TILE)
        index_keys[spot, :] = piece[:, :TILE]
        keys[spot, :] = piece[:, TILE:]
    span = keys.shape[0]
    shape = (STRIPE, 2 * TILE)
    behind = lax.broadcasted_iota(jnp.int32, shape, 0) - (
        lax.broadcasted_iota(jnp.int32, shape, 1) & (TILE - 1)
    )
    behind = behind - facts[CORE] * TILE
    pairs = [(part, head) for part in (q_own, q_other) for head in range(0, part.shape[0], 2)]

    def scores(step):
        part, head = pairs[step]
        both = jnp.concatenate([part[head], part[head + 1]], axis=1)
        out = raw[step % 2]
        out[...] = jnp.dot(keys[...], both, preferred_element_type=jnp.float32)
        for tile in range(2):
            for stripe in range(span // TILE):
                spot = pl.ds(pl.multiple_of(stripe * TILE + facts[SLOTS + tile] * STRIPE, STRIPE), STRIPE)
                late = behind + (tile * TILE + stripe * STRIPE) > 0
                out[spot, :] = jnp.where(late, far_below, out[spot, :])

    def softmax(step):
        part = raw[step % 2]
        spots = [slice(i, i + TILE) for i in range(0, span, TILE)]
        folded = (TILE // 8, 8, 2 * TILE)
        top = functools.reduce(
            jnp.maximum, [jnp.max(part[spot, :].reshape(folded), axis=0) for spot in spots]
        )
        top = jnp.max(top, axis=0, keepdims=True)
        row_sum = jnp.zeros((8, 2 * TILE), jnp.float32)
        for spot in spots:
            weights = jnp.exp2((part[spot, :] - top) * exp_scale)
            part[spot, :] = weights
            row_sum = row_sum + jnp.sum(weights.reshape(folded), axis=0)
        share = 1.0 / (jnp.sum(row_sum, axis=0, keepdims=True) * MLA_HEADS)
        for spot in spots:
            weights = part[spot, :] * share
            weights = weights[:, :TILE] + weights[:, TILE:]
            if step == 0:
                total[spot, :] = weights
            else:
                total[spot, :] += weights

    for step in range(len(pairs)):
        scores(step)
        if step:
            softmax(step - 1)
    softmax(len(pairs) - 1)
    for i in range(0, span, TILE):
        target[:, i : i + TILE] = total[i : i + TILE, :].T


def row_groups(rows, heads):
    row = lax.broadcasted_iota(jnp.int32, (rows, rows * heads), 0) * heads
    both = lax.broadcasted_iota(jnp.int32, (rows, rows * heads), 1)
    return ((both >= row) & (both < row + heads)).astype(jnp.float32)


def index_logits(block, keys):
    return lax.dot_general(
        block[:, :, :TILE].reshape(-1, TILE),
        keys[...],
        (((1,), (1,)), ((), ())),
        preferred_element_type=jnp.float32,
    ).reshape(*block.shape[:2], keys.shape[0])


def index_weights(block):
    terms = block[:, :, TILE : 2 * TILE].astype(jnp.float32)
    return terms[:, :, 0:1] + terms[:, :, 1:2] + terms[:, :, 2:3]


def source_blocks(parts, count):
    return [part.at[i : i + count] for part in parts for i in range(0, part.shape[0], count)]


def score_kernel(near, far, keys, score):
    heads_rows = near.shape[1]
    total = jnp.zeros((heads_rows, keys.shape[0]), jnp.float32)
    for block in source_blocks((near, far), 2):
        lifted = jnp.maximum(index_logits(block, keys), 0.0)
        total = total + jnp.sum(lifted * index_weights(block), axis=0)
    score[...] = jnp.dot(
        row_groups(QROWS, heads_rows // QROWS),
        total,
        precision=lax.Precision.HIGHEST,
        preferred_element_type=jnp.float32,
    )


def grad_kernel(
    facts, target_parts, score, near, far, keys, key_pos, loss_grad,
    query_grad, weight_grad, key_grad, loss, coef
):
    allowed = allowed_keys(facts[FIRST], key_pos[...])
    target = jnp.sum(target_parts[...], axis=0)
    masked = jnp.where(allowed, score[...], far_below)
    shifted = masked - jnp.max(masked, axis=-1, keepdims=True)
    weights = jnp.where(allowed, jnp.exp(shifted), 0.0)
    row_sum = jnp.sum(weights, axis=-1, keepdims=True)
    log_prob = shifted - jnp.log(row_sum)
    positive = target > 0
    self_term = jnp.where(positive, target * jnp.log(jnp.where(positive, target, 1.0)), 0.0)
    loss[...] = jnp.sum(
        jnp.where(allowed, self_term - target * log_prob, 0.0), axis=-1, keepdims=True
    )
    score_grad = loss_grad[...] * jnp.where(allowed, weights / row_sum - target, 0.0)
    count = 2
    heads_rows = near.shape[1]
    score_grad = lax.dot_general(
        row_groups(QROWS, heads_rows // QROWS),
        score_grad,
        (((0,), (0,)), ((), ())),
        precision=lax.Precision.HIGHEST,
        preferred_element_type=jnp.float32,
    )[None]
    rows = count * heads_rows
    for step, block in enumerate(source_blocks((near, far), count)):
        spot = slice(step * rows, (step + 1) * rows)
        logits = index_logits(block, keys)
        scaled = score_grad * index_weights(block)
        scaled = jnp.where(logits > 0, scaled, 0.0).reshape(rows, -1)
        coef[spot, :] = scaled.astype(jnp.bfloat16)
        lifted = jnp.sum(score_grad * jnp.maximum(logits, 0.0), axis=-1, keepdims=True)
        query = jnp.dot(coef[spot, :], keys[...], preferred_element_type=jnp.float32)
        query = query.reshape(count, heads_rows, TILE)
        for i in range(count):
            query_grad[facts[SOURCES + step * count + i]] = query[i]
            weight_grad[facts[SOURCES + step * count + i]] = lifted[i]
    flat = jnp.concatenate(
        [part[:, :, :TILE].reshape(-1, TILE) for part in (near, far)], axis=0
    )
    flat = lax.dot_general(
        flat, coef[...], (((0,), (0,)), ((), ())), preferred_element_type=jnp.float32
    ).astype(jnp.bfloat16)
    for lane in range(key_grad.shape[0]):
        key_grad[lane] = flat[:, lane * TILE : (lane + 1) * TILE]


def whole(shape):
    return pl.BlockSpec(shape, lambda *_: (0,) * len(shape))


def one_hot_rows(table, block):
    a, b = table.shape
    eye = jnp.eye(block, dtype=table.dtype)
    return (table[:, None, :, None] * eye[None, :, None, :]).reshape(a * block, b * block)


def body(main_query, key_latent, index_query, index_key, index_weight, selection, loss_grad):
    bf16, f32 = jnp.bfloat16, jnp.float32
    ctx_index = lax.axis_index(CTX)
    ctx_count = lax.axis_size(CTX)
    lane = lax.axis_index(HEAD)
    lanes = lax.axis_size(HEAD)
    yl, x, core = lax.axis_index("yl"), lax.axis_index("x"), lax.axis_index("core")
    x_count = lax.axis_size("x")
    query_rows, main_local, lat_width = main_query.shape
    index_local, idx_width = index_query.shape[1:]
    key_tiles = key_latent.shape[0] // TILE
    sel_count = selection.shape[1]
    key_span = sel_count * TILE
    context = key_tiles * TILE * ctx_count
    width = idx_width + lat_width
    heads_all = lanes * index_local
    rows_all = heads_all * QROWS
    heads_rows = index_local * QROWS
    swap = [(0, 1), (1, 0)]
    params = pltpu.CompilerParams(vmem_limit_bytes=VMEM)
    vmem = pl.BlockSpec(memory_space=pltpu.VMEM)
    smem = pl.BlockSpec(memory_space=pltpu.SMEM)

    def shifted(value, shift):
        ring = [(i, (i + shift) % x_count) for i in range(x_count)]
        return lax.ppermute(value, "x", ring)

    send = pl.pallas_call(
        stripes_kernel,
        in_specs=[smem, vmem, vmem, vmem],
        out_shape=jax.ShapeDtypeStruct((ctx_count * OWNER_MOST * STRIPE, width), bf16),
        compiler_params=params,
        name="stripes",
    )(jnp.stack([ctx_index, lane]).astype(jnp.int32), selection, index_key, key_latent.T)
    arrived = lax.all_to_all(send, CTX, 0, 0, tiled=True)

    queries = jnp.transpose(main_query, (1, 2, 0))
    q_other = lax.dynamic_slice_in_dim(queries, (1 - core) * TILE, TILE, 2)
    q_other = lax.ppermute(q_other, "core", swap)

    first_term = lax.reduce_precision(index_weight, 8, 7)
    rest = index_weight - first_term
    second_term = lax.reduce_precision(rest, 8, 7)
    terms = jnp.stack([first_term, second_term, rest - second_term], axis=-1).astype(bf16)
    iq = jnp.concatenate(
        [index_query, jnp.pad(terms, ((0, 0), (0, 0), (0, idx_width - 3)))], axis=-1
    ).reshape(2, 2, x_count, heads_rows, 2 * idx_width)
    iq = [
        lax.dynamic_index_in_dim(iq, (x + shift) % x_count, 2, keepdims=False)
        for shift in range(x_count)
    ]
    iq = jnp.stack([part if shift == 0 else shifted(part, shift) for shift, part in enumerate(iq)])
    iq_far = lax.ppermute(
        lax.dynamic_index_in_dim(iq, 1 - core, 1, keepdims=False), "core", swap
    )
    iq = jnp.stack([lax.dynamic_index_in_dim(iq, core, 1, keepdims=False), iq_far])
    iq_far = lax.ppermute(lax.dynamic_index_in_dim(iq, 1 - yl, 2, keepdims=False), "yl", swap)
    iq_near = lax.dynamic_index_in_dim(iq, yl, 2, keepdims=False)
    iq_shape = (lanes // 2, heads_rows, 2 * idx_width)
    iq_near, iq_far = iq_near.reshape(iq_shape), iq_far.reshape(iq_shape)

    owner = selection // key_tiles
    inner = selection % key_tiles
    earlier = jnp.tril(jnp.ones((sel_count, sel_count), jnp.int32), -1)
    rank = jnp.sum((owner[:, :, None] == owner[:, None, :]) * earlier[None], axis=2)
    ranks = jnp.arange(OWNER_MOST)
    picked = lax.dynamic_index_in_dim(selection, ctx_index, 0, keepdims=False)
    my_owner = lax.dynamic_index_in_dim(owner, ctx_index, 0, keepdims=False)
    my_rank = lax.dynamic_index_in_dim(rank, ctx_index, 0, keepdims=False)
    sent = jnp.any(
        (owner[:, None, :, None] == ctx_index)
        & (rank[:, None, :, None] == ranks[None, :, None, None])
        & (inner[:, None, :, None] == jnp.arange(key_tiles)[None, None, None, :]),
        axis=2,
    ).reshape(ctx_count * OWNER_MOST, key_tiles)
    got = (
        (my_owner[:, None, None] == jnp.arange(ctx_count)[None, :, None])
        & (my_rank[:, None, None] == ranks[None, None, :])
    ).reshape(sel_count, ctx_count * OWNER_MOST)
    got_rows = one_hot_rows(got.astype(bf16), STRIPE)
    sent_rows = one_hot_rows(sent.astype(bf16), STRIPE)
    chunk = core * (lanes // 2) + yl * x_count + x
    grad_rows = lax.dynamic_slice_in_dim(loss_grad, chunk * QROWS, QROWS, 0).reshape(QROWS, 1)
    key_pos = (
        jnp.arange(lanes)[:, None, None] * STRIPE
        + picked[None, :, None] * TILE
        + jnp.arange(STRIPE)[None, None, :]
    ).reshape(1, key_span)
    place = [
        ((yl ^ j) * x_count + (x - shift) % x_count) * 2 + (core ^ k)
        for k in range(2)
        for j in range(2)
        for shift in (0, 1, 3, 2)
    ]
    block_first = context - query_rows * ctx_count + ctx_index * query_rows
    own = block_first // TILE + jnp.arange(2)
    slots = jnp.argmax(picked[None, :] == own[:, None], axis=1)
    sources = [
        (core ^ j) * (lanes // 2) + (yl ^ k) * x_count + (x - shift) % x_count
        for k in range(2)
        for j in range(2)
        for shift in range(x_count)
    ]
    facts = jnp.concatenate(
        [jnp.stack(place), slots, jnp.stack([core, block_first + chunk * QROWS, *sources])]
    ).astype(jnp.int32)
    arrived, got_rows, sent_rows, key_pos, grad_rows, facts = lax.optimization_barrier(
        (arrived, got_rows, sent_rows, key_pos, grad_rows, facts)
    )
    stripe = jnp.dot(got_rows, arrived, preferred_element_type=bf16)

    other = lax.ppermute(stripe, "yl", swap)
    pieces = [stripe] + [shifted(stripe, shift) for shift in (1, 3, 2)]
    pieces += [other] + [shifted(other, shift) for shift in (1, 3, 2)]
    pieces += [lax.ppermute(piece, "core", swap) for piece in pieces]

    count = 2 * main_local * TILE
    target_part, index_keys = pl.pallas_call(
        attend_kernel,
        grid_spec=pltpu.PrefetchScalarGridSpec(
            num_scalar_prefetch=1,
            grid=(1,),
            in_specs=[whole((TILE, width))] * 16
            + [
                pl.BlockSpec((main_local, lat_width, TILE), lambda i, facts: (0, 0, facts[CORE])),
                whole((main_local, lat_width, TILE)),
            ],
            out_specs=[whole((TILE, key_span)), whole((key_span, idx_width))],
            scratch_shapes=[
                pltpu.VMEM((key_span, lat_width), bf16),
                pltpu.VMEM((key_span, TILE), f32),
                pltpu.VMEM((key_span, 2 * TILE), f32),
                pltpu.VMEM((key_span, 2 * TILE), f32),
            ],
        ),
        out_shape=[
            jax.ShapeDtypeStruct((TILE, key_span), f32),
            jax.ShapeDtypeStruct((key_span, idx_width), bf16),
        ],
        compiler_params=params,
        cost_estimate=pl.CostEstimate(
            flops=2 * count * key_span * lat_width,
            bytes_accessed=8 * 2**20,
            transcendentals=count * key_span,
        ),
        name="attend",
    )(facts, *pieces, queries, q_other)
    target_parts = lax.all_to_all(target_part, ("yl", "x"), 0, 0, tiled=True)
    target_parts = target_parts.reshape(lanes // 2, QROWS, key_span)

    score = pl.pallas_call(
        score_kernel,
        grid=(1,),
        in_specs=[whole(iq_shape), whole(iq_shape), whole((key_span, idx_width))],
        out_specs=whole((QROWS, key_span)),
        out_shape=jax.ShapeDtypeStruct((QROWS, key_span), f32),
        compiler_params=params,
        cost_estimate=pl.CostEstimate(
            flops=2 * rows_all * key_span * idx_width, bytes_accessed=2**20, transcendentals=0
        ),
        name="score",
    )(iq_near, iq_far, index_keys)

    query_grad, weight_grad, key_part, loss = pl.pallas_call(
        grad_kernel,
        grid=(1,),
        in_specs=[smem]
        + [whole((lanes // 2, QROWS, key_span)), whole((QROWS, key_span))]
        + [whole(iq_shape), whole(iq_shape), whole((key_span, idx_width))]
        + [whole((1, key_span)), whole((QROWS, 1))],
        out_specs=[
            whole((lanes, heads_rows, idx_width)),
            whole((lanes, heads_rows, 1)),
            whole((lanes, idx_width, TILE)),
            whole((QROWS, 1)),
        ],
        out_shape=[
            jax.ShapeDtypeStruct((lanes, heads_rows, idx_width), f32),
            jax.ShapeDtypeStruct((lanes, heads_rows, 1), f32),
            jax.ShapeDtypeStruct((lanes, idx_width, TILE), bf16),
            jax.ShapeDtypeStruct((QROWS, 1), f32),
        ],
        scratch_shapes=[pltpu.VMEM((rows_all, key_span), bf16)],
        compiler_params=params,
        cost_estimate=pl.CostEstimate(
            flops=6 * rows_all * key_span * idx_width, bytes_accessed=4 * 2**20, transcendentals=0
        ),
        name="grad",
    )(facts, target_parts, score, iq_near, iq_far, index_keys, key_pos, grad_rows)

    exact = lax.Precision.HIGHEST
    key_sum = lax.all_to_all(key_part, HEAD, 0, 0, tiled=True)
    key_sum = jnp.sum(key_sum.astype(f32), axis=0)
    back = lax.dot_general(
        got_rows.astype(f32), key_sum, (((0,), (1,)), ((), ())), precision=exact
    )
    back = lax.all_to_all(back, CTX, 0, 0, tiled=True)
    own_blocks = lax.dot_general(
        sent_rows.astype(f32), back, (((0,), (0,)), ((), ())), precision=exact
    ).reshape(key_tiles, STRIPE, idx_width)
    order = jnp.arange(lanes)
    natural = order % (lanes // 2) * 2 + order // (lanes // 2)
    goes = (jnp.arange(key_tiles)[None, :] * lanes + lane) // key_tiles == natural[:, None]
    key_send = jnp.sum(jnp.where(goes[:, :, None, None], own_blocks[None], 0.0), axis=1)

    small = jnp.concatenate(
        [
            weight_grad.reshape(lanes, heads_rows),
            jnp.broadcast_to(loss.reshape(1, QROWS), (lanes, QROWS)),
            jnp.zeros((lanes, idx_width - heads_rows - QROWS), f32),
        ],
        axis=1,
    ).reshape(lanes, 1, idx_width)
    packed = jnp.concatenate(
        [query_grad, key_send, small], axis=1
    )
    packed = lax.all_to_all(packed, ROWS, 0, 0, tiled=True)
    query_out = packed[:, :heads_rows].reshape(query_rows, index_local, idx_width)
    blocks = packed[:, heads_rows : heads_rows + STRIPE]
    source = (lane * key_tiles + jnp.arange(key_tiles)) % lanes
    source = source % 2 * (lanes // 2) + source // 2
    comes = source[:, None] == order[None, :]
    key_out = jnp.sum(jnp.where(comes[:, :, None, None], blocks[None], 0.0), axis=1)
    key_out = key_out.reshape(key_tiles * STRIPE, idx_width)
    small = packed[:, heads_rows + STRIPE]
    weight_out = small[:, :heads_rows].reshape(query_rows, index_local)
    loss_out = small[:, heads_rows : heads_rows + QROWS].reshape(query_rows)
    return (query_out, weight_out, key_out, loss_out)


def solution(mesh):
    fine = Mesh(mesh.devices.reshape(8, 2, 2, 4, 2), CTX + HEAD)
    return jax.shard_map(
        body,
        mesh=fine,
        in_specs=(
            P(CTX, HEAD, None),
            P(CTX, None),
            P(CTX, HEAD, None),
            P(CTX, None),
            P(CTX, HEAD),
            P(),
            P(CTX),
        ),
        out_specs=(P(CTX, HEAD, None), P(CTX, HEAD), P(CTX + HEAD, None), P(CTX)),
        check_vma=False,
    )
```

```python
import functools
import math

import jax
import jax.numpy as jnp
from jax import lax
from jax.experimental import pallas as pl
from jax.experimental.pallas import tpu as pltpu
from jax.sharding import Mesh, PartitionSpec as P

TILE = 128
MLA_HEADS = 128
OWNER_MOST = 3
QROWS = 16
STRIPE = 8
VMEM = 60 * 1024 * 1024

SLOTS, CORE, FIRST = 16, 18, 19

CTX = ("z", "yh")
HEAD = ("yl", "x", "core")
ROWS = ("core", "yl", "x")
exp_scale = 192.0 ** (-0.5) * math.log2(math.e)
far_below = -1e30


def allowed_keys(query_first, key_pos):
    rows = lax.broadcasted_iota(jnp.int32, (QROWS, key_pos.shape[1]), 0)
    return key_pos <= rows + query_first


def stripes_kernel(where, selection, index_key, key_latent, send):
    ctx, lane = where[0], where[1]
    rows, (blocks, slots) = send.shape[0], selection.shape
    per_block = OWNER_MOST * STRIPE
    tiles = index_key.shape[0] // TILE
    row = lax.broadcasted_iota(jnp.int32, (rows, slots), 0)
    slot = lax.broadcasted_iota(jnp.int32, (rows, slots), 1)
    first = slot * per_block
    repeat = ((row >= first) & (row < first + per_block)).astype(jnp.float32)
    picked = jnp.dot(
        repeat.astype(jnp.bfloat16),
        selection[...].astype(jnp.float32).astype(jnp.bfloat16),
        preferred_element_type=jnp.float32,
    ).astype(jnp.int32)
    inner = picked - ctx * tiles
    mine = (inner >= 0) & (inner < tiles)
    a = lax.broadcasted_iota(jnp.int32, (slots, slots), 0)
    b = lax.broadcasted_iota(jnp.int32, (slots, slots), 1)
    earlier = (a < b).astype(jnp.float32).astype(jnp.bfloat16)
    rank = jnp.dot(
        mine.astype(jnp.float32).astype(jnp.bfloat16), earlier, preferred_element_type=jnp.float32
    ).astype(jnp.int32)
    block = jnp.sum(jnp.where(repeat > 0, slot, 0), axis=1, keepdims=True)
    row = lax.broadcasted_iota(jnp.int32, (rows, 1), 0)
    wanted = lax.shift_right_logical(row - block * per_block, 3)
    source = inner * TILE + lane * STRIPE + (row & (STRIPE - 1)) + 1
    source = jnp.sum(jnp.where(mine & (rank == wanted), source, 0), axis=1, keepdims=True) - 1
    spot = lax.broadcasted_iota(jnp.int32, (rows, index_key.shape[0]), 1)
    pick = (spot == source).astype(jnp.float32).astype(jnp.bfloat16)
    send[:, :TILE] = jnp.dot(pick, index_key[...], preferred_element_type=jnp.float32).astype(
        jnp.bfloat16
    )
    send[:, TILE:] = lax.dot_general(
        pick, key_latent[...], (((1,), (1,)), ((), ())), preferred_element_type=jnp.float32
    ).astype(jnp.bfloat16)


def attend_kernel(facts, *refs):
    pieces, (q_own, q_other, target, index_keys, keys, total, *raw) = refs[:16], refs[16:]
    for i, piece in enumerate(pieces):
        spot = pl.ds(pl.multiple_of(facts[i] * TILE, TILE), TILE)
        index_keys[spot, :] = piece[:, :TILE]
        keys[spot, :] = piece[:, TILE:]
    span = keys.shape[0]
    shape = (STRIPE, 2 * TILE)
    behind = lax.broadcasted_iota(jnp.int32, shape, 0) - (
        lax.broadcasted_iota(jnp.int32, shape, 1) & (TILE - 1)
    )
    behind = behind - facts[CORE] * TILE
    pairs = [(part, head) for part in (q_own, q_other) for head in range(0, part.shape[0], 2)]

    def scores(step):
        part, head = pairs[step]
        both = jnp.concatenate([part[head], part[head + 1]], axis=1)
        out = raw[step % 2]
        out[...] = jnp.dot(keys[...], both, preferred_element_type=jnp.float32)
        for tile in range(2):
            for stripe in range(span // TILE):
                spot = pl.ds(pl.multiple_of(stripe * TILE + facts[SLOTS + tile] * STRIPE, STRIPE), STRIPE)
                late = behind + (tile * TILE + stripe * STRIPE) > 0
                out[spot, :] = jnp.where(late, far_below, out[spot, :])

    def softmax(step):
        part = raw[step % 2]
        spots = [slice(i, i + TILE) for i in range(0, span, TILE)]
        folded = (TILE // 8, 8, 2 * TILE)
        top = functools.reduce(
            jnp.maximum, [jnp.max(part[spot, :].reshape(folded), axis=0) for spot in spots]
        )
        top = jnp.max(top, axis=0, keepdims=True)
        row_sum = jnp.zeros((8, 2 * TILE), jnp.float32)
        for spot in spots:
            weights = jnp.exp2((part[spot, :] - top) * exp_scale)
            part[spot, :] = weights
            row_sum = row_sum + jnp.sum(weights.reshape(folded), axis=0)
        share = 1.0 / (jnp.sum(row_sum, axis=0, keepdims=True) * MLA_HEADS)
        for spot in spots:
            weights = part[spot, :] * share
            weights = weights[:, :TILE] + weights[:, TILE:]
            if step == 0:
                total[spot, :] = weights
            else:
                total[spot, :] += weights

    for step in range(len(pairs)):
        scores(step)
        if step:
            softmax(step - 1)
    softmax(len(pairs) - 1)
    for i in range(0, span, TILE):
        target[:, i : i + TILE] = total[i : i + TILE, :].T


def row_groups(rows, heads):
    row = lax.broadcasted_iota(jnp.int32, (rows, rows * heads), 0) * heads
    both = lax.broadcasted_iota(jnp.int32, (rows, rows * heads), 1)
    return ((both >= row) & (both < row + heads)).astype(jnp.float32)


def index_logits(block, keys):
    return lax.dot_general(
        block[:, :, :TILE].reshape(-1, TILE),
        keys[...],
        (((1,), (1,)), ((), ())),
        preferred_element_type=jnp.float32,
    ).reshape(*block.shape[:2], keys.shape[0])


def index_weights(block):
    terms = block[:, :, TILE : 2 * TILE].astype(jnp.float32)
    return terms[:, :, 0:1] + terms[:, :, 1:2] + terms[:, :, 2:3]


def source_blocks(queries, count):
    return [queries.at[i : i + count] for i in range(0, queries.shape[0], count)]


def score_kernel(queries, keys, score):
    heads_rows = queries.shape[1]
    total = jnp.zeros((heads_rows, keys.shape[0]), jnp.float32)
    for block in source_blocks(queries, 2):
        lifted = jnp.maximum(index_logits(block, keys), 0.0)
        total = total + jnp.sum(lifted * index_weights(block), axis=0)
    score[...] = jnp.dot(
        row_groups(QROWS, heads_rows // QROWS),
        total,
        precision=lax.Precision.HIGHEST,
        preferred_element_type=jnp.float32,
    )


def index_coefs(block, keys, score_grad):
    logits = index_logits(block, keys)
    scaled = jnp.where(logits > 0, score_grad[None] * index_weights(block), 0.0)
    return logits, scaled.astype(jnp.bfloat16).reshape(-1, logits.shape[-1])


def key_grad_kernel(
    facts, target_parts, score, queries, keys, key_pos, loss_grad,
    score_grad, loss, key_grad, coef
):
    allowed = allowed_keys(facts[FIRST], key_pos[...])
    target = jnp.sum(target_parts[...], axis=0)
    masked = jnp.where(allowed, score[...], far_below)
    shifted = masked - jnp.max(masked, axis=-1, keepdims=True)
    weights = jnp.where(allowed, jnp.exp(shifted), 0.0)
    row_sum = jnp.sum(weights, axis=-1, keepdims=True)
    log_prob = shifted - jnp.log(row_sum)
    positive = target > 0
    self_term = jnp.where(positive, target * jnp.log(jnp.where(positive, target, 1.0)), 0.0)
    loss[...] = jnp.sum(
        jnp.where(allowed, self_term - target * log_prob, 0.0), axis=-1, keepdims=True
    )
    rows_grad = loss_grad[...] * jnp.where(allowed, weights / row_sum - target, 0.0)
    heads_rows = queries.shape[1]
    score_grad[...] = lax.dot_general(
        row_groups(QROWS, heads_rows // QROWS),
        rows_grad,
        (((0,), (0,)), ((), ())),
        precision=lax.Precision.HIGHEST,
        preferred_element_type=jnp.float32,
    )
    count = 2
    rows = count * heads_rows
    for step, block in enumerate(source_blocks(queries, count)):
        coef[step * rows : (step + 1) * rows, :] = index_coefs(block, keys, score_grad[...])[1]
    flat = queries[:, :, :TILE].reshape(-1, TILE)
    flat = lax.dot_general(
        flat, coef[...], (((0,), (0,)), ((), ())), preferred_element_type=jnp.float32
    ).astype(jnp.bfloat16)
    for lane in range(key_grad.shape[0]):
        key_grad[lane] = flat[:, lane * TILE : (lane + 1) * TILE]


def as_row(column):
    n = column.shape[0]
    here = lax.broadcasted_iota(jnp.int32, (n, n), 0) == lax.broadcasted_iota(
        jnp.int32, (n, n), 1
    )
    return jnp.sum(jnp.where(here, column, 0.0), axis=0, keepdims=True)


def query_grad_kernel(score_grad, loss, queries, keys, packed):
    count = 2
    heads_rows = queries.shape[1]
    losses = as_row(loss[...])
    blank = jnp.zeros((1, packed.shape[2] - heads_rows - QROWS), jnp.float32)
    rest = jnp.zeros((packed.shape[1] - heads_rows - STRIPE - 1, packed.shape[2]), jnp.float32)
    for step, block in enumerate(source_blocks(queries, count)):
        logits, coef = index_coefs(block, keys, score_grad[...])
        query = jnp.dot(coef, keys[...], preferred_element_type=jnp.float32)
        query = query.reshape(count, heads_rows, TILE)
        lifted = jnp.sum(score_grad[...][None] * jnp.maximum(logits, 0.0), axis=-1, keepdims=True)
        for i in range(count):
            place = step * count + i
            packed[place, :heads_rows] = query[i]
            last = jnp.concatenate([as_row(lifted[i]), losses, blank], axis=1)
            packed[place, heads_rows + STRIPE :] = jnp.concatenate([last, rest], axis=0)


def whole(shape):
    return pl.BlockSpec(shape, lambda *_: (0,) * len(shape))


def one_hot_rows(table, block):
    a, b = table.shape
    eye = jnp.eye(block, dtype=table.dtype)
    return (table[:, None, :, None] * eye[None, :, None, :]).reshape(a * block, b * block)


def body(main_query, key_latent, index_query, index_key, index_weight, selection, loss_grad):
    bf16, f32 = jnp.bfloat16, jnp.float32
    ctx_index = lax.axis_index(CTX)
    ctx_count = lax.axis_size(CTX)
    lane = lax.axis_index(HEAD)
    lanes = lax.axis_size(HEAD)
    yl, x, core = lax.axis_index("yl"), lax.axis_index("x"), lax.axis_index("core")
    x_count = lax.axis_size("x")
    query_rows, main_local, lat_width = main_query.shape
    index_local, idx_width = index_query.shape[1:]
    key_tiles = key_latent.shape[0] // TILE
    sel_count = selection.shape[1]
    key_span = sel_count * TILE
    context = key_tiles * TILE * ctx_count
    width = idx_width + lat_width
    heads_all = lanes * index_local
    rows_all = heads_all * QROWS
    heads_rows = index_local * QROWS
    swap = [(0, 1), (1, 0)]
    params = pltpu.CompilerParams(vmem_limit_bytes=VMEM)
    vmem = pl.BlockSpec(memory_space=pltpu.VMEM)
    smem = pl.BlockSpec(memory_space=pltpu.SMEM)

    def shifted(value, shift):
        ring = [(i, (i + shift) % x_count) for i in range(x_count)]
        return lax.ppermute(value, "x", ring)

    send = pl.pallas_call(
        stripes_kernel,
        in_specs=[smem, vmem, vmem, vmem],
        out_shape=jax.ShapeDtypeStruct((ctx_count * OWNER_MOST * STRIPE, width), bf16),
        compiler_params=params,
        name="stripes",
    )(jnp.stack([ctx_index, lane]).astype(jnp.int32), selection, index_key, key_latent.T)
    send, index_query, index_weight, main_query = lax.optimization_barrier(
        (send, index_query, index_weight, main_query)
    )
    arrived = lax.all_to_all(send, CTX, 0, 0, tiled=True)

    queries = jnp.transpose(main_query, (1, 2, 0))
    q_other = lax.dynamic_slice_in_dim(queries, (1 - core) * TILE, TILE, 2)
    q_other = lax.ppermute(q_other, "core", swap)

    first_term = lax.reduce_precision(index_weight, 8, 7)
    rest = index_weight - first_term
    second_term = lax.reduce_precision(rest, 8, 7)
    terms = jnp.stack([first_term, second_term, rest - second_term], axis=-1).astype(bf16)
    iq = jnp.concatenate(
        [index_query, jnp.pad(terms, ((0, 0), (0, 0), (0, idx_width - 3)))], axis=-1
    ).reshape(lanes, heads_rows, 2 * idx_width)

    owner = selection // key_tiles
    inner = selection % key_tiles
    earlier = jnp.tril(jnp.ones((sel_count, sel_count), jnp.int32), -1)
    rank = jnp.sum((owner[:, :, None] == owner[:, None, :]) * earlier[None], axis=2)
    ranks = jnp.arange(OWNER_MOST)
    picked = lax.dynamic_index_in_dim(selection, ctx_index, 0, keepdims=False)
    my_owner = lax.dynamic_index_in_dim(owner, ctx_index, 0, keepdims=False)
    my_rank = lax.dynamic_index_in_dim(rank, ctx_index, 0, keepdims=False)
    sent = jnp.any(
        (owner[:, None, :, None] == ctx_index)
        & (rank[:, None, :, None] == ranks[None, :, None, None])
        & (inner[:, None, :, None] == jnp.arange(key_tiles)[None, None, None, :]),
        axis=2,
    ).reshape(ctx_count * OWNER_MOST, key_tiles)
    got = (
        (my_owner[:, None, None] == jnp.arange(ctx_count)[None, :, None])
        & (my_rank[:, None, None] == ranks[None, None, :])
    ).reshape(sel_count, ctx_count * OWNER_MOST)
    got_rows = one_hot_rows(got.astype(bf16), STRIPE)
    sent_rows = one_hot_rows(sent.astype(bf16), STRIPE)
    chunk = core * (lanes // 2) + yl * x_count + x
    grad_rows = lax.dynamic_slice_in_dim(loss_grad, chunk * QROWS, QROWS, 0).reshape(QROWS, 1)
    key_pos = (
        jnp.arange(lanes)[:, None, None] * STRIPE
        + picked[None, :, None] * TILE
        + jnp.arange(STRIPE)[None, None, :]
    ).reshape(1, key_span)
    place = [
        ((yl ^ j) * x_count + (x - shift) % x_count) * 2 + (core ^ k)
        for k in range(2)
        for j in range(2)
        for shift in (0, 1, 3, 2)
    ]
    block_first = context - query_rows * ctx_count + ctx_index * query_rows
    own = block_first // TILE + jnp.arange(2)
    slots = jnp.argmax(picked[None, :] == own[:, None], axis=1)
    facts = jnp.concatenate(
        [jnp.stack(place), slots, jnp.stack([core, block_first + chunk * QROWS])]
    ).astype(jnp.int32)
    arrived, got_rows, sent_rows, key_pos, grad_rows, facts, iq = lax.optimization_barrier(
        (arrived, got_rows, sent_rows, key_pos, grad_rows, facts, iq)
    )
    stripe = jnp.dot(got_rows, arrived, preferred_element_type=bf16)

    other = lax.ppermute(stripe, "yl", swap)
    pieces = [stripe] + [shifted(stripe, shift) for shift in (1, 3, 2)]
    iq, *pieces = lax.optimization_barrier((iq, *pieces))
    iq = lax.all_to_all(iq, ROWS, 0, 0, tiled=True)
    pieces += [other] + [shifted(other, shift) for shift in (1, 3, 2)]
    pieces += [lax.ppermute(piece, "core", swap) for piece in pieces]

    count = 2 * main_local * TILE
    target_part, index_keys = pl.pallas_call(
        attend_kernel,
        grid_spec=pltpu.PrefetchScalarGridSpec(
            num_scalar_prefetch=1,
            grid=(1,),
            in_specs=[whole((TILE, width))] * 16
            + [
                pl.BlockSpec((main_local, lat_width, TILE), lambda i, facts: (0, 0, facts[CORE])),
                whole((main_local, lat_width, TILE)),
            ],
            out_specs=[whole((TILE, key_span)), whole((key_span, idx_width))],
            scratch_shapes=[
                pltpu.VMEM((key_span, lat_width), bf16),
                pltpu.VMEM((key_span, TILE), f32),
                pltpu.VMEM((key_span, 2 * TILE), f32),
                pltpu.VMEM((key_span, 2 * TILE), f32),
            ],
        ),
        out_shape=[
            jax.ShapeDtypeStruct((TILE, key_span), f32),
            jax.ShapeDtypeStruct((key_span, idx_width), bf16),
        ],
        compiler_params=params,
        cost_estimate=pl.CostEstimate(
            flops=2 * count * key_span * lat_width,
            bytes_accessed=8 * 2**20,
            transcendentals=count * key_span,
        ),
        name="attend",
    )(facts, *pieces, queries, q_other)
    target_parts = lax.all_to_all(target_part, ("yl", "x"), 0, 0, tiled=True)
    target_parts = target_parts.reshape(lanes // 2, QROWS, key_span)

    score = pl.pallas_call(
        score_kernel,
        grid=(1,),
        in_specs=[whole(iq.shape), whole((key_span, idx_width))],
        out_specs=whole((QROWS, key_span)),
        out_shape=jax.ShapeDtypeStruct((QROWS, key_span), f32),
        compiler_params=params,
        cost_estimate=pl.CostEstimate(
            flops=2 * rows_all * key_span * idx_width, bytes_accessed=2**20, transcendentals=0
        ),
        name="score",
    )(iq, index_keys)

    score_grad, loss, key_part = pl.pallas_call(
        key_grad_kernel,
        grid=(1,),
        in_specs=[smem]
        + [whole((lanes // 2, QROWS, key_span)), whole((QROWS, key_span))]
        + [whole(iq.shape), whole((key_span, idx_width))]
        + [whole((1, key_span)), whole((QROWS, 1))],
        out_specs=[
            whole((heads_rows, key_span)),
            whole((QROWS, 1)),
            whole((lanes, idx_width, TILE)),
        ],
        out_shape=[
            jax.ShapeDtypeStruct((heads_rows, key_span), f32),
            jax.ShapeDtypeStruct((QROWS, 1), f32),
            jax.ShapeDtypeStruct((lanes, idx_width, TILE), bf16),
        ],
        scratch_shapes=[pltpu.VMEM((rows_all, key_span), bf16)],
        compiler_params=params,
        cost_estimate=pl.CostEstimate(
            flops=4 * rows_all * key_span * idx_width, bytes_accessed=4 * 2**20, transcendentals=0
        ),
        name="key_grad",
    )(facts, target_parts, score, iq, index_keys, key_pos, grad_rows)

    packed_shape = (lanes, heads_rows + 2 * STRIPE, idx_width)
    packed = pl.pallas_call(
        query_grad_kernel,
        grid=(1,),
        in_specs=[whole((heads_rows, key_span)), whole((QROWS, 1))]
        + [whole(iq.shape), whole((key_span, idx_width))],
        out_specs=whole(packed_shape),
        out_shape=jax.ShapeDtypeStruct(packed_shape, f32),
        compiler_params=params,
        cost_estimate=pl.CostEstimate(
            flops=4 * rows_all * key_span * idx_width, bytes_accessed=4 * 2**20, transcendentals=0
        ),
        name="query_grad",
    )(score_grad, loss, iq, index_keys)

    exact = lax.Precision.HIGHEST
    key_sum = lax.all_to_all(key_part, HEAD, 0, 0, tiled=True)
    key_sum = jnp.sum(key_sum.astype(f32), axis=0)
    back = lax.dot_general(
        got_rows.astype(f32), key_sum, (((0,), (1,)), ((), ())), precision=exact
    )
    back = lax.all_to_all(back, CTX, 0, 0, tiled=True)
    own_blocks = lax.dot_general(
        sent_rows.astype(f32), back, (((0,), (0,)), ((), ())), precision=exact
    ).reshape(key_tiles, STRIPE, idx_width)
    order = jnp.arange(lanes)
    natural = order % (lanes // 2) * 2 + order // (lanes // 2)
    goes = (jnp.arange(key_tiles)[None, :] * lanes + lane) // key_tiles == natural[:, None]
    key_send = jnp.sum(jnp.where(goes[:, :, None, None], own_blocks[None], 0.0), axis=1)

    packed = lax.dynamic_update_slice(packed, key_send, (0, heads_rows, 0))
    packed = lax.all_to_all(packed, ROWS, 0, 0, tiled=True)
    query_out = packed[:, :heads_rows].reshape(query_rows, index_local, idx_width)
    blocks = packed[:, heads_rows : heads_rows + STRIPE]
    source = (lane * key_tiles + jnp.arange(key_tiles)) % lanes
    source = source % 2 * (lanes // 2) + source // 2
    comes = source[:, None] == order[None, :]
    key_out = jnp.sum(jnp.where(comes[:, :, None, None], blocks[None], 0.0), axis=1)
    key_out = key_out.reshape(key_tiles * STRIPE, idx_width)
    small = packed[:, heads_rows + STRIPE]
    weight_out = small[:, :heads_rows].reshape(query_rows, index_local)
    loss_out = small[:, heads_rows : heads_rows + QROWS].reshape(query_rows)
    return (query_out, weight_out, key_out, loss_out)


def solution(mesh):
    fine = Mesh(mesh.devices.reshape(8, 2, 2, 4, 2), CTX + HEAD)
    return jax.shard_map(
        body,
        mesh=fine,
        in_specs=(
            P(CTX, HEAD, None),
            P(CTX, None),
            P(CTX, HEAD, None),
            P(CTX, None),
            P(CTX, HEAD),
            P(),
            P(CTX),
        ),
        out_specs=(P(CTX, HEAD, None), P(CTX, HEAD), P(CTX + HEAD, None), P(CTX)),
        check_vma=False,
    )
```

```python
import functools
import math

import jax
import jax.numpy as jnp
from jax import lax
from jax.experimental import pallas as pl
from jax.experimental.pallas import tpu as pltpu
from jax.sharding import Mesh, PartitionSpec as P

TILE = 128
MLA_HEADS = 128
OWNER_MOST = 3
QROWS = 16
STRIPE = 8
VMEM = 32 * 1024 * 1024

SLOTS, CORE, FIRST = 16, 18, 19

CTX = ("z", "yh")
HEAD = ("yl", "x", "core")
ROWS = ("core", "yl", "x")
exp_scale = 192.0 ** (-0.5) * math.log2(math.e)
far_below = -1e30


def allowed_keys(query_first, key_pos):
    rows = lax.broadcasted_iota(jnp.int32, (QROWS, key_pos.shape[1]), 0)
    return key_pos <= rows + query_first


def stripes_kernel(where, selection, index_key, key_latent, send):
    ctx, lane = where[0], where[1]
    rows, (blocks, slots) = send.shape[0], selection.shape
    per_block = OWNER_MOST * STRIPE
    tiles = index_key.shape[0] // TILE
    row = lax.broadcasted_iota(jnp.int32, (rows, slots), 0)
    slot = lax.broadcasted_iota(jnp.int32, (rows, slots), 1)
    first = slot * per_block
    repeat = ((row >= first) & (row < first + per_block)).astype(jnp.float32)
    picked = jnp.dot(
        repeat.astype(jnp.bfloat16),
        selection[...].astype(jnp.float32).astype(jnp.bfloat16),
        preferred_element_type=jnp.float32,
    ).astype(jnp.int32)
    inner = picked - ctx * tiles
    mine = (inner >= 0) & (inner < tiles)
    a = lax.broadcasted_iota(jnp.int32, (slots, slots), 0)
    b = lax.broadcasted_iota(jnp.int32, (slots, slots), 1)
    earlier = (a < b).astype(jnp.float32).astype(jnp.bfloat16)
    rank = jnp.dot(
        mine.astype(jnp.float32).astype(jnp.bfloat16), earlier, preferred_element_type=jnp.float32
    ).astype(jnp.int32)
    block = jnp.sum(jnp.where(repeat > 0, slot, 0), axis=1, keepdims=True)
    row = lax.broadcasted_iota(jnp.int32, (rows, 1), 0)
    wanted = lax.shift_right_logical(row - block * per_block, 3)
    source = inner * TILE + lane * STRIPE + (row & (STRIPE - 1)) + 1
    source = jnp.sum(jnp.where(mine & (rank == wanted), source, 0), axis=1, keepdims=True) - 1
    spot = lax.broadcasted_iota(jnp.int32, (rows, index_key.shape[0]), 1)
    pick = (spot == source).astype(jnp.float32).astype(jnp.bfloat16)
    send[:, :TILE] = jnp.dot(pick, index_key[...], preferred_element_type=jnp.float32).astype(
        jnp.bfloat16
    )
    send[:, TILE:] = lax.dot_general(
        pick, key_latent[...], (((1,), (1,)), ((), ())), preferred_element_type=jnp.float32
    ).astype(jnp.bfloat16)


def attend_kernel(facts, *refs):
    pieces, (q_own, q_other, target, index_keys, keys, total, *raw) = refs[:16], refs[16:]
    for i, piece in enumerate(pieces):
        spot = pl.ds(pl.multiple_of(facts[i] * TILE, TILE), TILE)
        index_keys[spot, :] = piece[:, :TILE]
        keys[spot, :] = piece[:, TILE:]
    span = keys.shape[0]
    shape = (STRIPE, 2 * TILE)
    behind = lax.broadcasted_iota(jnp.int32, shape, 0) - (
        lax.broadcasted_iota(jnp.int32, shape, 1) & (TILE - 1)
    )
    behind = behind - facts[CORE] * TILE
    half = pl.ds(pl.multiple_of(facts[CORE] * TILE, TILE), TILE)
    heads = [q_own.at[head, :, half] for head in range(q_own.shape[0])]
    heads += [q_other.at[head] for head in range(q_other.shape[0])]
    pairs = list(zip(heads[::2], heads[1::2]))

    def scores(step):
        both = jnp.concatenate([head[...] for head in pairs[step]], axis=1)
        out = raw[step % 2]
        out[...] = jnp.dot(keys[...], both, preferred_element_type=jnp.float32)
        for tile in range(2):
            for stripe in range(span // TILE):
                spot = pl.ds(pl.multiple_of(stripe * TILE + facts[SLOTS + tile] * STRIPE, STRIPE), STRIPE)
                late = behind + (tile * TILE + stripe * STRIPE) > 0
                out[spot, :] = jnp.where(late, far_below, out[spot, :])

    def softmax(step):
        part = raw[step % 2]
        spots = [slice(i, i + TILE) for i in range(0, span, TILE)]
        folded = (TILE // 8, 8, 2 * TILE)
        top = functools.reduce(
            jnp.maximum, [jnp.max(part[spot, :].reshape(folded), axis=0) for spot in spots]
        )
        top = jnp.max(top, axis=0, keepdims=True)
        row_sum = jnp.zeros((8, 2 * TILE), jnp.float32)
        for spot in spots:
            weights = jnp.exp2((part[spot, :] - top) * exp_scale)
            part[spot, :] = weights
            row_sum = row_sum + jnp.sum(weights.reshape(folded), axis=0)
        share = 1.0 / (jnp.sum(row_sum, axis=0, keepdims=True) * MLA_HEADS)
        for spot in spots:
            weights = part[spot, :] * share
            weights = weights[:, :TILE] + weights[:, TILE:]
            if step == 0:
                total[spot, :] = weights
            else:
                total[spot, :] += weights

    for step in range(len(pairs)):
        scores(step)
        if step:
            softmax(step - 1)
    softmax(len(pairs) - 1)
    for i in range(0, span, TILE):
        target[:, i : i + TILE] = total[i : i + TILE, :].T


def row_groups(rows, heads):
    row = lax.broadcasted_iota(jnp.int32, (rows, rows * heads), 0) * heads
    both = lax.broadcasted_iota(jnp.int32, (rows, rows * heads), 1)
    return ((both >= row) & (both < row + heads)).astype(jnp.float32)


def index_logits(block, keys):
    return lax.dot_general(
        block[:, :, :TILE].reshape(-1, TILE),
        keys[...],
        (((1,), (1,)), ((), ())),
        preferred_element_type=jnp.float32,
    ).reshape(*block.shape[:2], keys.shape[0])


def index_weights(block):
    terms = block[:, :, TILE : 2 * TILE].astype(jnp.float32)
    return terms[:, :, 0:1] + terms[:, :, 1:2] + terms[:, :, 2:3]


def source_blocks(queries, count):
    return [queries.at[i : i + count] for i in range(0, queries.shape[0], count)]


def score_kernel(queries, keys, score):
    heads_rows = queries.shape[1]
    total = jnp.zeros((heads_rows, keys.shape[0]), jnp.float32)
    for block in source_blocks(queries, 2):
        lifted = jnp.maximum(index_logits(block, keys), 0.0)
        total = total + jnp.sum(lifted * index_weights(block), axis=0)
    score[...] = jnp.dot(
        row_groups(QROWS, heads_rows // QROWS),
        total,
        precision=lax.Precision.HIGHEST,
        preferred_element_type=jnp.float32,
    )


def index_coefs(block, keys, score_grad):
    logits = index_logits(block, keys)
    scaled = jnp.where(logits > 0, score_grad[None] * index_weights(block), 0.0)
    return logits, scaled.astype(jnp.bfloat16).reshape(-1, logits.shape[-1])


def key_grad_kernel(
    facts, target_parts, score, queries, keys, key_pos, loss_grad,
    score_grad, loss, key_grad, coef
):
    allowed = allowed_keys(facts[FIRST], key_pos[...])
    target = jnp.sum(target_parts[...], axis=0)
    masked = jnp.where(allowed, score[...], far_below)
    shifted = masked - jnp.max(masked, axis=-1, keepdims=True)
    weights = jnp.where(allowed, jnp.exp(shifted), 0.0)
    row_sum = jnp.sum(weights, axis=-1, keepdims=True)
    log_prob = shifted - jnp.log(row_sum)
    positive = target > 0
    self_term = jnp.where(positive, target * jnp.log(jnp.where(positive, target, 1.0)), 0.0)
    loss[...] = jnp.sum(
        jnp.where(allowed, self_term - target * log_prob, 0.0), axis=-1, keepdims=True
    )
    rows_grad = loss_grad[...] * jnp.where(allowed, weights / row_sum - target, 0.0)
    heads_rows = queries.shape[1]
    score_grad[...] = lax.dot_general(
        row_groups(QROWS, heads_rows // QROWS),
        rows_grad,
        (((0,), (0,)), ((), ())),
        precision=lax.Precision.HIGHEST,
        preferred_element_type=jnp.float32,
    )
    count = 2
    rows = count * heads_rows
    for step, block in enumerate(source_blocks(queries, count)):
        coef[step * rows : (step + 1) * rows, :] = index_coefs(block, keys, score_grad[...])[1]
    flat = queries[:, :, :TILE].reshape(-1, TILE)
    flat = lax.dot_general(
        flat, coef[...], (((0,), (0,)), ((), ())), preferred_element_type=jnp.float32
    ).astype(jnp.bfloat16)
    for lane in range(key_grad.shape[0]):
        key_grad[lane] = flat[:, lane * TILE : (lane + 1) * TILE]


def as_row(column):
    n = column.shape[0]
    here = lax.broadcasted_iota(jnp.int32, (n, n), 0) == lax.broadcasted_iota(
        jnp.int32, (n, n), 1
    )
    return jnp.sum(jnp.where(here, column, 0.0), axis=0, keepdims=True)


def query_grad_kernel(score_grad, loss, queries, keys, packed):
    count = 2
    heads_rows = queries.shape[1]
    losses = as_row(loss[...])
    blank = jnp.zeros((1, packed.shape[2] - heads_rows - QROWS), jnp.float32)
    rest = jnp.zeros((packed.shape[1] - heads_rows - STRIPE - 1, packed.shape[2]), jnp.float32)
    for step, block in enumerate(source_blocks(queries, count)):
        logits, coef = index_coefs(block, keys, score_grad[...])
        query = jnp.dot(coef, keys[...], preferred_element_type=jnp.float32)
        query = query.reshape(count, heads_rows, TILE)
        lifted = jnp.sum(score_grad[...][None] * jnp.maximum(logits, 0.0), axis=-1, keepdims=True)
        for i in range(count):
            place = step * count + i
            packed[place, :heads_rows] = query[i]
            last = jnp.concatenate([as_row(lifted[i]), losses, blank], axis=1)
            packed[place, heads_rows + STRIPE :] = jnp.concatenate([last, rest], axis=0)


def one_hot_rows(table, block):
    a, b = table.shape
    eye = jnp.eye(block, dtype=table.dtype)
    return (table[:, None, :, None] * eye[None, :, None, :]).reshape(a * block, b * block)


def body(main_query, key_latent, index_query, index_key, index_weight, selection, loss_grad):
    bf16, f32 = jnp.bfloat16, jnp.float32
    ctx_index = lax.axis_index(CTX)
    ctx_count = lax.axis_size(CTX)
    lane = lax.axis_index(HEAD)
    lanes = lax.axis_size(HEAD)
    yl, x, core = lax.axis_index("yl"), lax.axis_index("x"), lax.axis_index("core")
    x_count = lax.axis_size("x")
    query_rows, main_local, lat_width = main_query.shape
    index_local, idx_width = index_query.shape[1:]
    key_tiles = key_latent.shape[0] // TILE
    sel_count = selection.shape[1]
    key_span = sel_count * TILE
    context = key_tiles * TILE * ctx_count
    width = idx_width + lat_width
    heads_all = lanes * index_local
    rows_all = heads_all * QROWS
    heads_rows = index_local * QROWS
    swap = [(0, 1), (1, 0)]
    params = pltpu.CompilerParams(vmem_limit_bytes=VMEM)
    vmem = pl.BlockSpec(memory_space=pltpu.VMEM)
    smem = pl.BlockSpec(memory_space=pltpu.SMEM)

    def shifted(value, shift):
        ring = [(i, (i + shift) % x_count) for i in range(x_count)]
        return lax.ppermute(value, "x", ring)

    send = pl.pallas_call(
        stripes_kernel,
        in_specs=[smem, vmem, vmem, vmem],
        out_shape=jax.ShapeDtypeStruct((ctx_count * OWNER_MOST * STRIPE, width), bf16),
        compiler_params=params,
        name="stripes",
    )(jnp.stack([ctx_index, lane]).astype(jnp.int32), selection, index_key, key_latent.T)
    send, index_query, index_weight, main_query = lax.optimization_barrier(
        (send, index_query, index_weight, main_query)
    )
    arrived = lax.all_to_all(send, CTX, 0, 0, tiled=True)

    queries = jnp.transpose(main_query, (1, 2, 0))
    q_other = lax.dynamic_slice_in_dim(queries, (1 - core) * TILE, TILE, 2)
    q_other = lax.ppermute(q_other, "core", swap)

    first_term = lax.reduce_precision(index_weight, 8, 7)
    rest = index_weight - first_term
    second_term = lax.reduce_precision(rest, 8, 7)
    terms = jnp.stack([first_term, second_term, rest - second_term], axis=-1).astype(bf16)
    iq = jnp.concatenate(
        [index_query, jnp.pad(terms, ((0, 0), (0, 0), (0, idx_width - 3)))], axis=-1
    ).reshape(lanes, heads_rows, 2 * idx_width)

    owner = selection // key_tiles
    inner = selection % key_tiles
    earlier = jnp.tril(jnp.ones((sel_count, sel_count), jnp.int32), -1)
    rank = jnp.sum((owner[:, :, None] == owner[:, None, :]) * earlier[None], axis=2)
    ranks = jnp.arange(OWNER_MOST)
    picked = lax.dynamic_index_in_dim(selection, ctx_index, 0, keepdims=False)
    my_owner = lax.dynamic_index_in_dim(owner, ctx_index, 0, keepdims=False)
    my_rank = lax.dynamic_index_in_dim(rank, ctx_index, 0, keepdims=False)
    sent = jnp.any(
        (owner[:, None, :, None] == ctx_index)
        & (rank[:, None, :, None] == ranks[None, :, None, None])
        & (inner[:, None, :, None] == jnp.arange(key_tiles)[None, None, None, :]),
        axis=2,
    ).reshape(ctx_count * OWNER_MOST, key_tiles)
    got = (
        (my_owner[:, None, None] == jnp.arange(ctx_count)[None, :, None])
        & (my_rank[:, None, None] == ranks[None, None, :])
    ).reshape(sel_count, ctx_count * OWNER_MOST)
    got_rows = one_hot_rows(got.astype(bf16), STRIPE)
    sent_rows = one_hot_rows(sent.astype(bf16), STRIPE)
    chunk = core * (lanes // 2) + yl * x_count + x
    grad_rows = lax.dynamic_slice_in_dim(loss_grad, chunk * QROWS, QROWS, 0).reshape(QROWS, 1)
    key_pos = (
        jnp.arange(lanes)[:, None, None] * STRIPE
        + picked[None, :, None] * TILE
        + jnp.arange(STRIPE)[None, None, :]
    ).reshape(1, key_span)
    place = [
        ((yl ^ j) * x_count + (x - shift) % x_count) * 2 + (core ^ k)
        for k in range(2)
        for j in range(2)
        for shift in (0, 1, 3, 2)
    ]
    block_first = context - query_rows * ctx_count + ctx_index * query_rows
    own = block_first // TILE + jnp.arange(2)
    slots = jnp.argmax(picked[None, :] == own[:, None], axis=1)
    facts = jnp.concatenate(
        [jnp.stack(place), slots, jnp.stack([core, block_first + chunk * QROWS])]
    ).astype(jnp.int32)
    arrived, got_rows, sent_rows, key_pos, grad_rows, facts, iq = lax.optimization_barrier(
        (arrived, got_rows, sent_rows, key_pos, grad_rows, facts, iq)
    )
    stripe = jnp.dot(got_rows, arrived, preferred_element_type=bf16)

    other = lax.ppermute(stripe, "yl", swap)
    pieces = [stripe] + [shifted(stripe, shift) for shift in (1, 3, 2)]
    far_pieces = [shifted(other, shift) for shift in (1, 3, 2)]
    iq, *far_pieces = lax.optimization_barrier((iq, *far_pieces))
    iq = lax.all_to_all(iq, ROWS, 0, 0, tiled=True)
    pieces += [other] + far_pieces
    pieces += [lax.ppermute(piece, "core", swap) for piece in pieces]

    count = 2 * main_local * TILE
    target_part, index_keys = pl.pallas_call(
        attend_kernel,
        in_specs=[smem] + [vmem] * 18,
        scratch_shapes=[
            pltpu.VMEM((key_span, lat_width), bf16),
            pltpu.VMEM((key_span, TILE), f32),
            pltpu.VMEM((key_span, 2 * TILE), f32),
            pltpu.VMEM((key_span, 2 * TILE), f32),
        ],
        out_shape=[
            jax.ShapeDtypeStruct((TILE, key_span), f32),
            jax.ShapeDtypeStruct((key_span, idx_width), bf16),
        ],
        compiler_params=params,
        cost_estimate=pl.CostEstimate(
            flops=2 * count * key_span * lat_width,
            bytes_accessed=8 * 2**20,
            transcendentals=count * key_span,
        ),
        name="attend",
    )(facts, *pieces, queries, q_other)
    target_parts = lax.all_to_all(target_part, ("yl", "x"), 0, 0, tiled=True)
    target_parts = target_parts.reshape(lanes // 2, QROWS, key_span)

    score = pl.pallas_call(
        score_kernel,
        in_specs=[vmem] * 2,
        out_shape=jax.ShapeDtypeStruct((QROWS, key_span), f32),
        compiler_params=params,
        cost_estimate=pl.CostEstimate(
            flops=2 * rows_all * key_span * idx_width, bytes_accessed=2**20, transcendentals=0
        ),
        name="score",
    )(iq, index_keys)

    score_grad, loss, key_part = pl.pallas_call(
        key_grad_kernel,
        in_specs=[smem] + [vmem] * 6,
        out_shape=[
            jax.ShapeDtypeStruct((heads_rows, key_span), f32),
            jax.ShapeDtypeStruct((QROWS, 1), f32),
            jax.ShapeDtypeStruct((lanes, idx_width, TILE), bf16),
        ],
        scratch_shapes=[pltpu.VMEM((rows_all, key_span), bf16)],
        compiler_params=params,
        cost_estimate=pl.CostEstimate(
            flops=4 * rows_all * key_span * idx_width, bytes_accessed=4 * 2**20, transcendentals=0
        ),
        name="key_grad",
    )(facts, target_parts, score, iq, index_keys, key_pos, grad_rows)

    packed_shape = (lanes, heads_rows + 2 * STRIPE, idx_width)
    packed = pl.pallas_call(
        query_grad_kernel,
        in_specs=[vmem] * 4,
        out_shape=jax.ShapeDtypeStruct(packed_shape, f32),
        compiler_params=params,
        cost_estimate=pl.CostEstimate(
            flops=4 * rows_all * key_span * idx_width, bytes_accessed=4 * 2**20, transcendentals=0
        ),
        name="query_grad",
    )(score_grad, loss, iq, index_keys)

    exact = lax.Precision.HIGHEST
    key_sum = lax.all_to_all(key_part, HEAD, 0, 0, tiled=True)
    key_sum = jnp.sum(key_sum.astype(f32), axis=0)
    back = lax.dot_general(
        got_rows.astype(f32), key_sum, (((0,), (1,)), ((), ())), precision=exact
    )
    back = lax.all_to_all(back, CTX, 0, 0, tiled=True)
    own_blocks = lax.dot_general(
        sent_rows.astype(f32), back, (((0,), (0,)), ((), ())), precision=exact
    ).reshape(key_tiles, STRIPE, idx_width)
    order = jnp.arange(lanes)
    natural = order % (lanes // 2) * 2 + order // (lanes // 2)
    goes = (jnp.arange(key_tiles)[None, :] * lanes + lane) // key_tiles == natural[:, None]
    key_send = jnp.sum(jnp.where(goes[:, :, None, None], own_blocks[None], 0.0), axis=1)

    packed = lax.dynamic_update_slice(packed, key_send, (0, heads_rows, 0))
    packed = lax.all_to_all(packed, ROWS, 0, 0, tiled=True)
    query_out = packed[:, :heads_rows].reshape(query_rows, index_local, idx_width)
    blocks = packed[:, heads_rows : heads_rows + STRIPE]
    source = (lane * key_tiles + jnp.arange(key_tiles)) % lanes
    source = source % 2 * (lanes // 2) + source // 2
    comes = source[:, None] == order[None, :]
    key_out = jnp.sum(jnp.where(comes[:, :, None, None], blocks[None], 0.0), axis=1)
    key_out = key_out.reshape(key_tiles * STRIPE, idx_width)
    small = packed[:, heads_rows + STRIPE]
    weight_out = small[:, :heads_rows].reshape(query_rows, index_local)
    loss_out = small[:, heads_rows : heads_rows + QROWS].reshape(query_rows)
    return (query_out, weight_out, key_out, loss_out)


def solution(mesh):
    fine = Mesh(mesh.devices.reshape(8, 2, 2, 4, 2), CTX + HEAD)
    return jax.shard_map(
        body,
        mesh=fine,
        in_specs=(
            P(CTX, HEAD, None),
            P(CTX, None),
            P(CTX, HEAD, None),
            P(CTX, None),
            P(CTX, HEAD),
            P(),
            P(CTX),
        ),
        out_specs=(P(CTX, HEAD, None), P(CTX, HEAD), P(CTX + HEAD, None), P(CTX)),
        check_vma=False,
    )
```

```python
import functools
import math

import jax
import jax.numpy as jnp
from jax import lax
from jax.experimental import pallas as pl
from jax.experimental.pallas import tpu as pltpu
from jax.sharding import Mesh, PartitionSpec as P

TILE = 128
MLA_HEADS = 128
OWNER_MOST = 3
QROWS = 16
STRIPE = 8
VMEM = 60 * 1024 * 1024
SMALL_VMEM = 32 * 1024 * 1024

SLOTS, CORE, FIRST = 16, 18, 19

CTX = ("z", "yh")
HEAD = ("yl", "x", "core")
ROWS = ("core", "yl", "x")
exp_scale = 192.0 ** (-0.5) * math.log2(math.e)
far_below = -1e30


def allowed_keys(query_first, key_pos):
    rows = lax.broadcasted_iota(jnp.int32, (QROWS, key_pos.shape[1]), 0)
    return key_pos <= rows + query_first


def stripes_kernel(where, selection, index_key, key_latent, send):
    ctx, lane = where[0], where[1]
    rows, (blocks, slots) = send.shape[0], selection.shape
    per_block = OWNER_MOST * STRIPE
    tiles = index_key.shape[0] // TILE
    row = lax.broadcasted_iota(jnp.int32, (rows, slots), 0)
    slot = lax.broadcasted_iota(jnp.int32, (rows, slots), 1)
    first = slot * per_block
    repeat = ((row >= first) & (row < first + per_block)).astype(jnp.float32)
    picked = jnp.dot(
        repeat.astype(jnp.bfloat16),
        selection[...].astype(jnp.float32).astype(jnp.bfloat16),
        preferred_element_type=jnp.float32,
    ).astype(jnp.int32)
    inner = picked - ctx * tiles
    mine = (inner >= 0) & (inner < tiles)
    a = lax.broadcasted_iota(jnp.int32, (slots, slots), 0)
    b = lax.broadcasted_iota(jnp.int32, (slots, slots), 1)
    earlier = (a < b).astype(jnp.float32).astype(jnp.bfloat16)
    rank = jnp.dot(
        mine.astype(jnp.float32).astype(jnp.bfloat16), earlier, preferred_element_type=jnp.float32
    ).astype(jnp.int32)
    block = jnp.sum(jnp.where(repeat > 0, slot, 0), axis=1, keepdims=True)
    row = lax.broadcasted_iota(jnp.int32, (rows, 1), 0)
    wanted = lax.shift_right_logical(row - block * per_block, 3)
    source = inner * TILE + lane * STRIPE + (row & (STRIPE - 1)) + 1
    source = jnp.sum(jnp.where(mine & (rank == wanted), source, 0), axis=1, keepdims=True) - 1
    spot = lax.broadcasted_iota(jnp.int32, (rows, index_key.shape[0]), 1)
    pick = (spot == source).astype(jnp.float32).astype(jnp.bfloat16)
    send[:, :TILE] = jnp.dot(pick, index_key[...], preferred_element_type=jnp.float32).astype(
        jnp.bfloat16
    )
    send[:, TILE:] = lax.dot_general(
        pick, key_latent[...], (((1,), (1,)), ((), ())), preferred_element_type=jnp.float32
    ).astype(jnp.bfloat16)


def attend_kernel(facts, *refs):
    pieces, (q_own, q_other, target, index_keys, keys, total, *raw) = refs[:16], refs[16:]
    for i, piece in enumerate(pieces):
        spot = pl.ds(pl.multiple_of(facts[i] * TILE, TILE), TILE)
        index_keys[spot, :] = piece[:, :TILE]
        keys[spot, :] = piece[:, TILE:]
    span = keys.shape[0]
    shape = (STRIPE, 2 * TILE)
    behind = lax.broadcasted_iota(jnp.int32, shape, 0) - (
        lax.broadcasted_iota(jnp.int32, shape, 1) & (TILE - 1)
    )
    behind = behind - facts[CORE] * TILE
    pairs = [(part, head) for part in (q_own, q_other) for head in range(0, part.shape[0], 2)]

    def scores(step):
        part, head = pairs[step]
        both = jnp.concatenate([part[head], part[head + 1]], axis=1)
        out = raw[step % 2]
        out[...] = jnp.dot(keys[...], both, preferred_element_type=jnp.float32)
        for tile in range(2):
            for stripe in range(span // TILE):
                spot = pl.ds(pl.multiple_of(stripe * TILE + facts[SLOTS + tile] * STRIPE, STRIPE), STRIPE)
                late = behind + (tile * TILE + stripe * STRIPE) > 0
                out[spot, :] = jnp.where(late, far_below, out[spot, :])

    def softmax(step):
        part = raw[step % 2]
        spots = [slice(i, i + TILE) for i in range(0, span, TILE)]
        folded = (TILE // 8, 8, 2 * TILE)
        top = functools.reduce(
            jnp.maximum, [jnp.max(part[spot, :].reshape(folded), axis=0) for spot in spots]
        )
        top = jnp.max(top, axis=0, keepdims=True)
        row_sum = jnp.zeros((8, 2 * TILE), jnp.float32)
        for spot in spots:
            weights = jnp.exp2((part[spot, :] - top) * exp_scale)
            part[spot, :] = weights
            row_sum = row_sum + jnp.sum(weights.reshape(folded), axis=0)
        share = 1.0 / (jnp.sum(row_sum, axis=0, keepdims=True) * MLA_HEADS)
        for spot in spots:
            weights = part[spot, :] * share
            weights = weights[:, :TILE] + weights[:, TILE:]
            if step == 0:
                total[spot, :] = weights
            else:
                total[spot, :] += weights

    for step in range(len(pairs)):
        scores(step)
        if step:
            softmax(step - 1)
    softmax(len(pairs) - 1)
    for i in range(0, span, TILE):
        target[:, i : i + TILE] = total[i : i + TILE, :].T


def row_groups(rows, heads):
    row = lax.broadcasted_iota(jnp.int32, (rows, rows * heads), 0) * heads
    both = lax.broadcasted_iota(jnp.int32, (rows, rows * heads), 1)
    return ((both >= row) & (both < row + heads)).astype(jnp.float32)


def index_logits(block, keys):
    return lax.dot_general(
        block[:, :, :TILE].reshape(-1, TILE),
        keys[...],
        (((1,), (1,)), ((), ())),
        preferred_element_type=jnp.float32,
    ).reshape(*block.shape[:2], keys.shape[0])


def index_weights(block):
    terms = block[:, :, TILE : 2 * TILE].astype(jnp.float32)
    return terms[:, :, 0:1] + terms[:, :, 1:2] + terms[:, :, 2:3]


def source_blocks(queries, count):
    return [queries.at[i : i + count] for i in range(0, queries.shape[0], count)]


def score_kernel(queries, keys, score):
    heads_rows = queries.shape[1]
    total = jnp.zeros((heads_rows, keys.shape[0]), jnp.float32)
    for block in source_blocks(queries, 2):
        lifted = jnp.maximum(index_logits(block, keys), 0.0)
        total = total + jnp.sum(lifted * index_weights(block), axis=0)
    score[...] = jnp.dot(
        row_groups(QROWS, heads_rows // QROWS),
        total,
        precision=lax.Precision.HIGHEST,
        preferred_element_type=jnp.float32,
    )


def index_coefs(block, keys, score_grad):
    logits = index_logits(block, keys)
    scaled = jnp.where(logits > 0, score_grad[None] * index_weights(block), 0.0)
    return logits, scaled.astype(jnp.bfloat16).reshape(-1, logits.shape[-1])


def key_grad_kernel(
    facts, target_parts, score, queries, keys, key_pos, loss_grad,
    score_grad, loss, key_grad, coef
):
    allowed = allowed_keys(facts[FIRST], key_pos[...])
    target = jnp.sum(target_parts[...], axis=0)
    masked = jnp.where(allowed, score[...], far_below)
    shifted = masked - jnp.max(masked, axis=-1, keepdims=True)
    weights = jnp.where(allowed, jnp.exp(shifted), 0.0)
    row_sum = jnp.sum(weights, axis=-1, keepdims=True)
    log_prob = shifted - jnp.log(row_sum)
    positive = target > 0
    self_term = jnp.where(positive, target * jnp.log(jnp.where(positive, target, 1.0)), 0.0)
    loss[...] = jnp.sum(
        jnp.where(allowed, self_term - target * log_prob, 0.0), axis=-1, keepdims=True
    )
    rows_grad = loss_grad[...] * jnp.where(allowed, weights / row_sum - target, 0.0)
    heads_rows = queries.shape[1]
    score_grad[...] = lax.dot_general(
        row_groups(QROWS, heads_rows // QROWS),
        rows_grad,
        (((0,), (0,)), ((), ())),
        precision=lax.Precision.HIGHEST,
        preferred_element_type=jnp.float32,
    )
    count = 2
    rows = count * heads_rows
    for step, block in enumerate(source_blocks(queries, count)):
        coef[step * rows : (step + 1) * rows, :] = index_coefs(block, keys, score_grad[...])[1]
    flat = queries[:, :, :TILE].reshape(-1, TILE)
    flat = lax.dot_general(
        flat, coef[...], (((0,), (0,)), ((), ())), preferred_element_type=jnp.float32
    ).astype(jnp.bfloat16)
    for lane in range(key_grad.shape[0]):
        key_grad[lane] = flat[:, lane * TILE : (lane + 1) * TILE]


def as_row(column):
    n = column.shape[0]
    here = lax.broadcasted_iota(jnp.int32, (n, n), 0) == lax.broadcasted_iota(
        jnp.int32, (n, n), 1
    )
    return jnp.sum(jnp.where(here, column, 0.0), axis=0, keepdims=True)


def query_grad_kernel(score_grad, loss, queries, keys, packed):
    count = 2
    heads_rows = queries.shape[1]
    losses = as_row(loss[...])
    blank = jnp.zeros((1, packed.shape[2] - heads_rows - QROWS), jnp.float32)
    rest = jnp.zeros((packed.shape[1] - heads_rows - STRIPE - 1, packed.shape[2]), jnp.float32)
    for step, block in enumerate(source_blocks(queries, count)):
        logits, coef = index_coefs(block, keys, score_grad[...])
        query = jnp.dot(coef, keys[...], preferred_element_type=jnp.float32)
        query = query.reshape(count, heads_rows, TILE)
        lifted = jnp.sum(score_grad[...][None] * jnp.maximum(logits, 0.0), axis=-1, keepdims=True)
        for i in range(count):
            place = step * count + i
            packed[place, :heads_rows] = query[i]
            last = jnp.concatenate([as_row(lifted[i]), losses, blank], axis=1)
            packed[place, heads_rows + STRIPE :] = jnp.concatenate([last, rest], axis=0)


def whole(shape):
    return pl.BlockSpec(shape, lambda *_: (0,) * len(shape))


def one_hot_rows(table, block):
    a, b = table.shape
    eye = jnp.eye(block, dtype=table.dtype)
    return (table[:, None, :, None] * eye[None, :, None, :]).reshape(a * block, b * block)


def body(main_query, key_latent, index_query, index_key, index_weight, selection, loss_grad):
    bf16, f32 = jnp.bfloat16, jnp.float32
    ctx_index = lax.axis_index(CTX)
    ctx_count = lax.axis_size(CTX)
    lane = lax.axis_index(HEAD)
    lanes = lax.axis_size(HEAD)
    yl, x, core = lax.axis_index("yl"), lax.axis_index("x"), lax.axis_index("core")
    x_count = lax.axis_size("x")
    query_rows, main_local, lat_width = main_query.shape
    index_local, idx_width = index_query.shape[1:]
    key_tiles = key_latent.shape[0] // TILE
    sel_count = selection.shape[1]
    key_span = sel_count * TILE
    context = key_tiles * TILE * ctx_count
    width = idx_width + lat_width
    heads_all = lanes * index_local
    rows_all = heads_all * QROWS
    heads_rows = index_local * QROWS
    swap = [(0, 1), (1, 0)]
    params = pltpu.CompilerParams(vmem_limit_bytes=VMEM)
    small = pltpu.CompilerParams(vmem_limit_bytes=SMALL_VMEM)
    vmem = pl.BlockSpec(memory_space=pltpu.VMEM)
    smem = pl.BlockSpec(memory_space=pltpu.SMEM)

    def shifted(value, shift):
        ring = [(i, (i + shift) % x_count) for i in range(x_count)]
        return lax.ppermute(value, "x", ring)

    send = pl.pallas_call(
        stripes_kernel,
        in_specs=[smem, vmem, vmem, vmem],
        out_shape=jax.ShapeDtypeStruct((ctx_count * OWNER_MOST * STRIPE, width), bf16),
        compiler_params=params,
        name="stripes",
    )(jnp.stack([ctx_index, lane]).astype(jnp.int32), selection, index_key, key_latent.T)
    send, index_query, index_weight, main_query = lax.optimization_barrier(
        (send, index_query, index_weight, main_query)
    )
    arrived = lax.all_to_all(send, CTX, 0, 0, tiled=True)

    queries = jnp.transpose(main_query, (1, 2, 0))
    q_other = lax.dynamic_slice_in_dim(queries, (1 - core) * TILE, TILE, 2)
    q_other = lax.ppermute(q_other, "core", swap)

    first_term = lax.reduce_precision(index_weight, 8, 7)
    rest = index_weight - first_term
    second_term = lax.reduce_precision(rest, 8, 7)
    terms = jnp.stack([first_term, second_term, rest - second_term], axis=-1).astype(bf16)
    iq = jnp.concatenate(
        [index_query, jnp.pad(terms, ((0, 0), (0, 0), (0, idx_width - 3)))], axis=-1
    ).reshape(lanes, heads_rows, 2 * idx_width)

    owner = selection // key_tiles
    inner = selection % key_tiles
    earlier = jnp.tril(jnp.ones((sel_count, sel_count), jnp.int32), -1)
    rank = jnp.sum((owner[:, :, None] == owner[:, None, :]) * earlier[None], axis=2)
    ranks = jnp.arange(OWNER_MOST)
    picked = lax.dynamic_index_in_dim(selection, ctx_index, 0, keepdims=False)
    my_owner = lax.dynamic_index_in_dim(owner, ctx_index, 0, keepdims=False)
    my_rank = lax.dynamic_index_in_dim(rank, ctx_index, 0, keepdims=False)
    sent = jnp.any(
        (owner[:, None, :, None] == ctx_index)
        & (rank[:, None, :, None] == ranks[None, :, None, None])
        & (inner[:, None, :, None] == jnp.arange(key_tiles)[None, None, None, :]),
        axis=2,
    ).reshape(ctx_count * OWNER_MOST, key_tiles)
    got = (
        (my_owner[:, None, None] == jnp.arange(ctx_count)[None, :, None])
        & (my_rank[:, None, None] == ranks[None, None, :])
    ).reshape(sel_count, ctx_count * OWNER_MOST)
    got_rows = one_hot_rows(got.astype(bf16), STRIPE)
    sent_rows = one_hot_rows(sent.astype(bf16), STRIPE)
    chunk = core * (lanes // 2) + yl * x_count + x
    grad_rows = lax.dynamic_slice_in_dim(loss_grad, chunk * QROWS, QROWS, 0).reshape(QROWS, 1)
    key_pos = (
        jnp.arange(lanes)[:, None, None] * STRIPE
        + picked[None, :, None] * TILE
        + jnp.arange(STRIPE)[None, None, :]
    ).reshape(1, key_span)
    place = [
        ((yl ^ j) * x_count + (x - shift) % x_count) * 2 + (core ^ k)
        for k in range(2)
        for j in range(2)
        for shift in (0, 1, 3, 2)
    ]
    block_first = context - query_rows * ctx_count + ctx_index * query_rows
    own = block_first // TILE + jnp.arange(2)
    slots = jnp.argmax(picked[None, :] == own[:, None], axis=1)
    facts = jnp.concatenate(
        [jnp.stack(place), slots, jnp.stack([core, block_first + chunk * QROWS])]
    ).astype(jnp.int32)
    arrived, got_rows, sent_rows, key_pos, grad_rows, facts, iq = lax.optimization_barrier(
        (arrived, got_rows, sent_rows, key_pos, grad_rows, facts, iq)
    )
    stripe = jnp.dot(got_rows, arrived, preferred_element_type=bf16)

    other = lax.ppermute(stripe, "yl", swap)
    pieces = [stripe] + [shifted(stripe, shift) for shift in (1, 3, 2)]
    far_pieces = [shifted(other, shift) for shift in (1, 3, 2)]
    iq, *far_pieces = lax.optimization_barrier((iq, *far_pieces))
    iq = lax.all_to_all(iq, ROWS, 0, 0, tiled=True)
    pieces += [other] + far_pieces
    pieces += [lax.ppermute(piece, "core", swap) for piece in pieces]

    count = 2 * main_local * TILE
    target_part, index_keys = pl.pallas_call(
        attend_kernel,
        grid_spec=pltpu.PrefetchScalarGridSpec(
            num_scalar_prefetch=1,
            grid=(1,),
            in_specs=[whole((TILE, width))] * 16
            + [
                pl.BlockSpec((main_local, lat_width, TILE), lambda i, facts: (0, 0, facts[CORE])),
                whole((main_local, lat_width, TILE)),
            ],
            out_specs=[whole((TILE, key_span)), whole((key_span, idx_width))],
            scratch_shapes=[
                pltpu.VMEM((key_span, lat_width), bf16),
                pltpu.VMEM((key_span, TILE), f32),
                pltpu.VMEM((key_span, 2 * TILE), f32),
                pltpu.VMEM((key_span, 2 * TILE), f32),
            ],
        ),
        out_shape=[
            jax.ShapeDtypeStruct((TILE, key_span), f32),
            jax.ShapeDtypeStruct((key_span, idx_width), bf16),
        ],
        compiler_params=params,
        cost_estimate=pl.CostEstimate(
            flops=2 * count * key_span * lat_width,
            bytes_accessed=8 * 2**20,
            transcendentals=count * key_span,
        ),
        name="attend",
    )(facts, *pieces, queries, q_other)
    target_parts = lax.all_to_all(target_part, ("yl", "x"), 0, 0, tiled=True)
    target_parts = target_parts.reshape(lanes // 2, QROWS, key_span)

    score = pl.pallas_call(
        score_kernel,
        in_specs=[vmem] * 2,
        out_shape=jax.ShapeDtypeStruct((QROWS, key_span), f32),
        compiler_params=small,
        cost_estimate=pl.CostEstimate(
            flops=2 * rows_all * key_span * idx_width, bytes_accessed=2**20, transcendentals=0
        ),
        name="score",
    )(iq, index_keys)

    score_grad, loss, key_part = pl.pallas_call(
        key_grad_kernel,
        in_specs=[smem] + [vmem] * 6,
        out_shape=[
            jax.ShapeDtypeStruct((heads_rows, key_span), f32),
            jax.ShapeDtypeStruct((QROWS, 1), f32),
            jax.ShapeDtypeStruct((lanes, idx_width, TILE), bf16),
        ],
        scratch_shapes=[pltpu.VMEM((rows_all, key_span), bf16)],
        compiler_params=small,
        cost_estimate=pl.CostEstimate(
            flops=4 * rows_all * key_span * idx_width, bytes_accessed=4 * 2**20, transcendentals=0
        ),
        name="key_grad",
    )(facts, target_parts, score, iq, index_keys, key_pos, grad_rows)

    packed_shape = (lanes, heads_rows + 2 * STRIPE, idx_width)
    packed = pl.pallas_call(
        query_grad_kernel,
        in_specs=[vmem] * 4,
        out_shape=jax.ShapeDtypeStruct(packed_shape, f32),
        compiler_params=small,
        cost_estimate=pl.CostEstimate(
            flops=4 * rows_all * key_span * idx_width, bytes_accessed=4 * 2**20, transcendentals=0
        ),
        name="query_grad",
    )(score_grad, loss, iq, index_keys)

    exact = lax.Precision.HIGHEST
    key_sum = lax.all_to_all(key_part, HEAD, 0, 0, tiled=True)
    key_sum = jnp.sum(key_sum.astype(f32), axis=0)
    back = lax.dot_general(
        got_rows.astype(f32), key_sum, (((0,), (1,)), ((), ())), precision=exact
    )
    back = lax.all_to_all(back, CTX, 0, 0, tiled=True)
    own_blocks = lax.dot_general(
        sent_rows.astype(f32), back, (((0,), (0,)), ((), ())), precision=exact
    ).reshape(key_tiles, STRIPE, idx_width)
    order = jnp.arange(lanes)
    natural = order % (lanes // 2) * 2 + order // (lanes // 2)
    goes = (jnp.arange(key_tiles)[None, :] * lanes + lane) // key_tiles == natural[:, None]
    key_send = jnp.sum(jnp.where(goes[:, :, None, None], own_blocks[None], 0.0), axis=1)

    packed = lax.dynamic_update_slice(packed, key_send, (0, heads_rows, 0))
    packed = lax.all_to_all(packed, ROWS, 0, 0, tiled=True)
    query_out = packed[:, :heads_rows].reshape(query_rows, index_local, idx_width)
    blocks = packed[:, heads_rows : heads_rows + STRIPE]
    source = (lane * key_tiles + jnp.arange(key_tiles)) % lanes
    source = source % 2 * (lanes // 2) + source // 2
    comes = source[:, None] == order[None, :]
    key_out = jnp.sum(jnp.where(comes[:, :, None, None], blocks[None], 0.0), axis=1)
    key_out = key_out.reshape(key_tiles * STRIPE, idx_width)
    small = packed[:, heads_rows + STRIPE]
    weight_out = small[:, :heads_rows].reshape(query_rows, index_local)
    loss_out = small[:, heads_rows : heads_rows + QROWS].reshape(query_rows)
    return (query_out, weight_out, key_out, loss_out)


def solution(mesh):
    fine = Mesh(mesh.devices.reshape(8, 2, 2, 4, 2), CTX + HEAD)
    return jax.shard_map(
        body,
        mesh=fine,
        in_specs=(
            P(CTX, HEAD, None),
            P(CTX, None),
            P(CTX, HEAD, None),
            P(CTX, None),
            P(CTX, HEAD),
            P(),
            P(CTX),
        ),
        out_specs=(P(CTX, HEAD, None), P(CTX, HEAD), P(CTX + HEAD, None), P(CTX)),
        check_vma=False,
    )
```

```python
import functools
import math

import jax
import jax.numpy as jnp
from jax import lax
from jax.experimental import pallas as pl
from jax.experimental.pallas import tpu as pltpu
from jax.sharding import Mesh, PartitionSpec as P

TILE = 128
MLA_HEADS = 128
OWNER_MOST = 3
QROWS = 16
STRIPE = 8
VMEM = 60 * 1024 * 1024
SMALL_VMEM = 32 * 1024 * 1024

SLOTS, CORE, FIRST = 16, 18, 19

CTX = ("z", "yh")
HEAD = ("yl", "x", "core")
ROWS = ("core", "yl", "x")
exp_scale = 192.0 ** (-0.5) * math.log2(math.e)
far_below = -1e30


def allowed_keys(query_first, key_pos):
    rows = lax.broadcasted_iota(jnp.int32, (QROWS, key_pos.shape[1]), 0)
    return key_pos <= rows + query_first


def stripes_kernel(selection, index_key, key_latent, send):
    ctx, lane = lax.axis_index(CTX), lax.axis_index(HEAD)
    rows, (blocks, slots) = send.shape[0], selection.shape
    per_block = OWNER_MOST * STRIPE
    tiles = index_key.shape[0] // TILE
    row = lax.broadcasted_iota(jnp.int32, (rows, slots), 0)
    slot = lax.broadcasted_iota(jnp.int32, (rows, slots), 1)
    first = slot * per_block
    repeat = ((row >= first) & (row < first + per_block)).astype(jnp.float32)
    picked = jnp.dot(
        repeat.astype(jnp.bfloat16),
        selection[...].astype(jnp.float32).astype(jnp.bfloat16),
        preferred_element_type=jnp.float32,
    ).astype(jnp.int32)
    inner = picked - ctx * tiles
    mine = (inner >= 0) & (inner < tiles)
    a = lax.broadcasted_iota(jnp.int32, (slots, slots), 0)
    b = lax.broadcasted_iota(jnp.int32, (slots, slots), 1)
    earlier = (a < b).astype(jnp.float32).astype(jnp.bfloat16)
    rank = jnp.dot(
        mine.astype(jnp.float32).astype(jnp.bfloat16), earlier, preferred_element_type=jnp.float32
    ).astype(jnp.int32)
    block = jnp.sum(jnp.where(repeat > 0, slot, 0), axis=1, keepdims=True)
    row = lax.broadcasted_iota(jnp.int32, (rows, 1), 0)
    wanted = lax.shift_right_logical(row - block * per_block, 3)
    source = inner * TILE + lane * STRIPE + (row & (STRIPE - 1)) + 1
    source = jnp.sum(jnp.where(mine & (rank == wanted), source, 0), axis=1, keepdims=True) - 1
    spot = lax.broadcasted_iota(jnp.int32, (rows, index_key.shape[0]), 1)
    pick = (spot == source).astype(jnp.float32).astype(jnp.bfloat16)
    send[:, :TILE] = jnp.dot(pick, index_key[...], preferred_element_type=jnp.float32).astype(
        jnp.bfloat16
    )
    send[:, TILE:] = lax.dot_general(
        pick, key_latent[...], (((1,), (1,)), ((), ())), preferred_element_type=jnp.float32
    ).astype(jnp.bfloat16)


def attend_kernel(facts, *refs):
    pieces, (q_own, q_other, target, index_keys, keys, total, *raw) = refs[:16], refs[16:]
    for i, piece in enumerate(pieces):
        spot = pl.ds(pl.multiple_of(facts[i] * TILE, TILE), TILE)
        index_keys[spot, :] = piece[:, :TILE]
        keys[spot, :] = piece[:, TILE:]
    span = keys.shape[0]
    shape = (STRIPE, 2 * TILE)
    behind = lax.broadcasted_iota(jnp.int32, shape, 0) - (
        lax.broadcasted_iota(jnp.int32, shape, 1) & (TILE - 1)
    )
    behind = behind - facts[CORE] * TILE
    pairs = [(part, head) for part in (q_own, q_other) for head in range(0, part.shape[0], 2)]

    def scores(step):
        part, head = pairs[step]
        both = jnp.concatenate([part[head], part[head + 1]], axis=1)
        out = raw[step % 2]
        out[...] = jnp.dot(keys[...], both, preferred_element_type=jnp.float32)
        for tile in range(2):
            for stripe in range(span // TILE):
                spot = pl.ds(pl.multiple_of(stripe * TILE + facts[SLOTS + tile] * STRIPE, STRIPE), STRIPE)
                late = behind + (tile * TILE + stripe * STRIPE) > 0
                out[spot, :] = jnp.where(late, far_below, out[spot, :])

    def softmax(step):
        part = raw[step % 2]
        spots = [slice(i, i + TILE) for i in range(0, span, TILE)]
        folded = (TILE // 8, 8, 2 * TILE)
        top = functools.reduce(
            jnp.maximum, [jnp.max(part[spot, :].reshape(folded), axis=0) for spot in spots]
        )
        top = jnp.max(top, axis=0, keepdims=True)
        row_sum = jnp.zeros((8, 2 * TILE), jnp.float32)
        for spot in spots:
            weights = jnp.exp2((part[spot, :] - top) * exp_scale)
            part[spot, :] = weights
            row_sum = row_sum + jnp.sum(weights.reshape(folded), axis=0)
        share = 1.0 / (jnp.sum(row_sum, axis=0, keepdims=True) * MLA_HEADS)
        for spot in spots:
            weights = part[spot, :] * share
            weights = weights[:, :TILE] + weights[:, TILE:]
            if step == 0:
                total[spot, :] = weights
            else:
                total[spot, :] += weights

    for step in range(len(pairs)):
        scores(step)
        if step:
            softmax(step - 1)
    softmax(len(pairs) - 1)
    for i in range(0, span, TILE):
        target[:, i : i + TILE] = total[i : i + TILE, :].T


def row_groups(rows, heads):
    row = lax.broadcasted_iota(jnp.int32, (rows, rows * heads), 0) * heads
    both = lax.broadcasted_iota(jnp.int32, (rows, rows * heads), 1)
    return ((both >= row) & (both < row + heads)).astype(jnp.float32)


def index_logits(block, keys):
    return lax.dot_general(
        block[:, :, :TILE].reshape(-1, TILE),
        keys[...],
        (((1,), (1,)), ((), ())),
        preferred_element_type=jnp.float32,
    ).reshape(*block.shape[:2], keys.shape[0])


def index_weights(block):
    terms = block[:, :, TILE : 2 * TILE].astype(jnp.float32)
    return terms[:, :, 0:1] + terms[:, :, 1:2] + terms[:, :, 2:3]


def source_blocks(queries, count):
    return [queries.at[i : i + count] for i in range(0, queries.shape[0], count)]


def score_kernel(queries, keys, score):
    heads_rows = queries.shape[1]
    total = jnp.zeros((heads_rows, keys.shape[0]), jnp.float32)
    for block in source_blocks(queries, 2):
        lifted = jnp.maximum(index_logits(block, keys), 0.0)
        total = total + jnp.sum(lifted * index_weights(block), axis=0)
    score[...] = jnp.dot(
        row_groups(QROWS, heads_rows // QROWS),
        total,
        precision=lax.Precision.HIGHEST,
        preferred_element_type=jnp.float32,
    )


def index_coefs(block, keys, score_grad):
    logits = index_logits(block, keys)
    scaled = jnp.where(logits > 0, score_grad[None] * index_weights(block), 0.0)
    return logits, scaled.astype(jnp.bfloat16).reshape(-1, logits.shape[-1])


def key_grad_kernel(
    facts, target_parts, score, queries, keys, key_pos, loss_grad,
    score_grad, loss, key_grad, coef
):
    allowed = allowed_keys(facts[FIRST], key_pos[...])
    target = jnp.sum(target_parts[...], axis=0)
    masked = jnp.where(allowed, score[...], far_below)
    shifted = masked - jnp.max(masked, axis=-1, keepdims=True)
    weights = jnp.where(allowed, jnp.exp(shifted), 0.0)
    row_sum = jnp.sum(weights, axis=-1, keepdims=True)
    log_prob = shifted - jnp.log(row_sum)
    positive = target > 0
    self_term = jnp.where(positive, target * jnp.log(jnp.where(positive, target, 1.0)), 0.0)
    loss[...] = jnp.sum(
        jnp.where(allowed, self_term - target * log_prob, 0.0), axis=-1, keepdims=True
    )
    rows_grad = loss_grad[...] * jnp.where(allowed, weights / row_sum - target, 0.0)
    heads_rows = queries.shape[1]
    score_grad[...] = lax.dot_general(
        row_groups(QROWS, heads_rows // QROWS),
        rows_grad,
        (((0,), (0,)), ((), ())),
        precision=lax.Precision.HIGHEST,
        preferred_element_type=jnp.float32,
    )
    count = 2
    rows = count * heads_rows
    for step, block in enumerate(source_blocks(queries, count)):
        coef[step * rows : (step + 1) * rows, :] = index_coefs(block, keys, score_grad[...])[1]
    flat = queries[:, :, :TILE].reshape(-1, TILE)
    flat = lax.dot_general(
        flat, coef[...], (((0,), (0,)), ((), ())), preferred_element_type=jnp.float32
    ).astype(jnp.bfloat16)
    for lane in range(key_grad.shape[0]):
        key_grad[lane] = flat[:, lane * TILE : (lane + 1) * TILE]


def as_row(column):
    n = column.shape[0]
    here = lax.broadcasted_iota(jnp.int32, (n, n), 0) == lax.broadcasted_iota(
        jnp.int32, (n, n), 1
    )
    return jnp.sum(jnp.where(here, column, 0.0), axis=0, keepdims=True)


def query_grad_kernel(score_grad, loss, queries, keys, packed):
    count = 2
    heads_rows = queries.shape[1]
    losses = as_row(loss[...])
    blank = jnp.zeros((1, packed.shape[2] - heads_rows - QROWS), jnp.float32)
    rest = jnp.zeros((packed.shape[1] - heads_rows - STRIPE - 1, packed.shape[2]), jnp.float32)
    for step, block in enumerate(source_blocks(queries, count)):
        logits, coef = index_coefs(block, keys, score_grad[...])
        query = jnp.dot(coef, keys[...], preferred_element_type=jnp.float32)
        query = query.reshape(count, heads_rows, TILE)
        lifted = jnp.sum(score_grad[...][None] * jnp.maximum(logits, 0.0), axis=-1, keepdims=True)
        for i in range(count):
            place = step * count + i
            packed[place, :heads_rows] = query[i]
            last = jnp.concatenate([as_row(lifted[i]), losses, blank], axis=1)
            packed[place, heads_rows + STRIPE :] = jnp.concatenate([last, rest], axis=0)


def whole(shape):
    return pl.BlockSpec(shape, lambda *_: (0,) * len(shape))


def one_hot_rows(table, block):
    a, b = table.shape
    eye = jnp.eye(block, dtype=table.dtype)
    return (table[:, None, :, None] * eye[None, :, None, :]).reshape(a * block, b * block)


def body(main_query, key_latent, index_query, index_key, index_weight, selection, loss_grad):
    bf16, f32 = jnp.bfloat16, jnp.float32
    ctx_index = lax.axis_index(CTX)
    ctx_count = lax.axis_size(CTX)
    lane = lax.axis_index(HEAD)
    lanes = lax.axis_size(HEAD)
    yl, x, core = lax.axis_index("yl"), lax.axis_index("x"), lax.axis_index("core")
    x_count = lax.axis_size("x")
    query_rows, main_local, lat_width = main_query.shape
    index_local, idx_width = index_query.shape[1:]
    key_tiles = key_latent.shape[0] // TILE
    sel_count = selection.shape[1]
    key_span = sel_count * TILE
    context = key_tiles * TILE * ctx_count
    width = idx_width + lat_width
    heads_all = lanes * index_local
    rows_all = heads_all * QROWS
    heads_rows = index_local * QROWS
    swap = [(0, 1), (1, 0)]
    params = pltpu.CompilerParams(vmem_limit_bytes=VMEM)
    small = pltpu.CompilerParams(vmem_limit_bytes=SMALL_VMEM)
    vmem = pl.BlockSpec(memory_space=pltpu.VMEM)
    smem = pl.BlockSpec(memory_space=pltpu.SMEM)

    def shifted(value, shift):
        ring = [(i, (i + shift) % x_count) for i in range(x_count)]
        return lax.ppermute(value, "x", ring)

    send = pl.pallas_call(
        stripes_kernel,
        in_specs=[vmem] * 3,
        out_shape=jax.ShapeDtypeStruct((ctx_count * OWNER_MOST * STRIPE, width), bf16),
        compiler_params=params,
        name="stripes",
    )(selection, index_key, key_latent.T)
    send, index_query, index_weight, main_query = lax.optimization_barrier(
        (send, index_query, index_weight, main_query)
    )
    arrived = lax.all_to_all(send, CTX, 0, 0, tiled=True)

    queries = jnp.transpose(main_query, (1, 2, 0))
    q_other = lax.dynamic_slice_in_dim(queries, (1 - core) * TILE, TILE, 2)
    q_other = lax.ppermute(q_other, "core", swap)

    first_term = lax.reduce_precision(index_weight, 8, 7)
    rest = index_weight - first_term
    second_term = lax.reduce_precision(rest, 8, 7)
    terms = jnp.stack([first_term, second_term, rest - second_term], axis=-1).astype(bf16)
    iq = jnp.concatenate(
        [index_query, jnp.pad(terms, ((0, 0), (0, 0), (0, idx_width - 3)))], axis=-1
    ).reshape(lanes, heads_rows, 2 * idx_width)

    owner = selection // key_tiles
    inner = selection % key_tiles
    earlier = jnp.tril(jnp.ones((sel_count, sel_count), jnp.int32), -1)
    rank = jnp.sum((owner[:, :, None] == owner[:, None, :]) * earlier[None], axis=2)
    ranks = jnp.arange(OWNER_MOST)
    picked = lax.dynamic_index_in_dim(selection, ctx_index, 0, keepdims=False)
    my_owner = lax.dynamic_index_in_dim(owner, ctx_index, 0, keepdims=False)
    my_rank = lax.dynamic_index_in_dim(rank, ctx_index, 0, keepdims=False)
    sent = jnp.any(
        (owner[:, None, :, None] == ctx_index)
        & (rank[:, None, :, None] == ranks[None, :, None, None])
        & (inner[:, None, :, None] == jnp.arange(key_tiles)[None, None, None, :]),
        axis=2,
    ).reshape(ctx_count * OWNER_MOST, key_tiles)
    got = (
        (my_owner[:, None, None] == jnp.arange(ctx_count)[None, :, None])
        & (my_rank[:, None, None] == ranks[None, None, :])
    ).reshape(sel_count, ctx_count * OWNER_MOST)
    got_rows = one_hot_rows(got.astype(bf16), STRIPE)
    sent_rows = one_hot_rows(sent.astype(bf16), STRIPE)
    chunk = core * (lanes // 2) + yl * x_count + x
    grad_rows = lax.dynamic_slice_in_dim(loss_grad, chunk * QROWS, QROWS, 0).reshape(QROWS, 1)
    key_pos = (
        jnp.arange(lanes)[:, None, None] * STRIPE
        + picked[None, :, None] * TILE
        + jnp.arange(STRIPE)[None, None, :]
    ).reshape(1, key_span)
    place = [
        ((yl ^ j) * x_count + (x - shift) % x_count) * 2 + (core ^ k)
        for k in range(2)
        for j in range(2)
        for shift in (0, 1, 3, 2)
    ]
    block_first = context - query_rows * ctx_count + ctx_index * query_rows
    own = block_first // TILE + jnp.arange(2)
    slots = jnp.argmax(picked[None, :] == own[:, None], axis=1)
    facts = jnp.concatenate(
        [jnp.stack(place), slots, jnp.stack([core, block_first + chunk * QROWS])]
    ).astype(jnp.int32)
    arrived, got_rows, sent_rows, key_pos, grad_rows, facts, iq = lax.optimization_barrier(
        (arrived, got_rows, sent_rows, key_pos, grad_rows, facts, iq)
    )
    stripe = jnp.dot(got_rows, arrived, preferred_element_type=bf16)

    other = lax.ppermute(stripe, "yl", swap)
    pieces = [stripe] + [shifted(stripe, shift) for shift in (1, 3, 2)]
    far_pieces = [shifted(other, shift) for shift in (1, 3, 2)]
    iq, *far_pieces = lax.optimization_barrier((iq, *far_pieces))
    iq = lax.all_to_all(iq, ROWS, 0, 0, tiled=True)
    pieces += [other] + far_pieces
    pieces += [lax.ppermute(piece, "core", swap) for piece in pieces]

    count = 2 * main_local * TILE
    target_part, index_keys = pl.pallas_call(
        attend_kernel,
        grid_spec=pltpu.PrefetchScalarGridSpec(
            num_scalar_prefetch=1,
            grid=(1,),
            in_specs=[whole((TILE, width))] * 16
            + [
                pl.BlockSpec((main_local, lat_width, TILE), lambda i, facts: (0, 0, facts[CORE])),
                whole((main_local, lat_width, TILE)),
            ],
            out_specs=[whole((TILE, key_span)), whole((key_span, idx_width))],
            scratch_shapes=[
                pltpu.VMEM((key_span, lat_width), bf16),
                pltpu.VMEM((key_span, TILE), f32),
                pltpu.VMEM((key_span, 2 * TILE), f32),
                pltpu.VMEM((key_span, 2 * TILE), f32),
            ],
        ),
        out_shape=[
            jax.ShapeDtypeStruct((TILE, key_span), f32),
            jax.ShapeDtypeStruct((key_span, idx_width), bf16),
        ],
        compiler_params=params,
        cost_estimate=pl.CostEstimate(
            flops=2 * count * key_span * lat_width,
            bytes_accessed=8 * 2**20,
            transcendentals=count * key_span,
        ),
        name="attend",
    )(facts, *pieces, queries, q_other)
    target_parts = lax.all_to_all(target_part, ("yl", "x"), 0, 0, tiled=True)
    target_parts = target_parts.reshape(lanes // 2, QROWS, key_span)

    score = pl.pallas_call(
        score_kernel,
        in_specs=[vmem] * 2,
        out_shape=jax.ShapeDtypeStruct((QROWS, key_span), f32),
        compiler_params=small,
        cost_estimate=pl.CostEstimate(
            flops=2 * rows_all * key_span * idx_width, bytes_accessed=2**20, transcendentals=0
        ),
        name="score",
    )(iq, index_keys)

    score_grad, loss, key_part = pl.pallas_call(
        key_grad_kernel,
        in_specs=[smem] + [vmem] * 6,
        out_shape=[
            jax.ShapeDtypeStruct((heads_rows, key_span), f32),
            jax.ShapeDtypeStruct((QROWS, 1), f32),
            jax.ShapeDtypeStruct((lanes, idx_width, TILE), bf16),
        ],
        scratch_shapes=[pltpu.VMEM((rows_all, key_span), bf16)],
        compiler_params=small,
        cost_estimate=pl.CostEstimate(
            flops=4 * rows_all * key_span * idx_width, bytes_accessed=4 * 2**20, transcendentals=0
        ),
        name="key_grad",
    )(facts, target_parts, score, iq, index_keys, key_pos, grad_rows)

    packed_shape = (lanes, heads_rows + 2 * STRIPE, idx_width)
    packed = pl.pallas_call(
        query_grad_kernel,
        in_specs=[vmem] * 4,
        out_shape=jax.ShapeDtypeStruct(packed_shape, f32),
        compiler_params=small,
        cost_estimate=pl.CostEstimate(
            flops=4 * rows_all * key_span * idx_width, bytes_accessed=4 * 2**20, transcendentals=0
        ),
        name="query_grad",
    )(score_grad, loss, iq, index_keys)

    key_sum = lax.all_to_all(key_part, HEAD, 0, 0, tiled=True)
    key_sum = jnp.sum(key_sum.astype(f32), axis=0)
    back = lax.dot_general(
        got_rows, key_sum.astype(bf16), (((0,), (1,)), ((), ())), preferred_element_type=bf16
    )
    back = lax.all_to_all(back, CTX, 0, 0, tiled=True)
    own_blocks = lax.dot_general(
        sent_rows, back, (((0,), (0,)), ((), ())), preferred_element_type=f32
    ).reshape(key_tiles, STRIPE, idx_width)
    order = jnp.arange(lanes)
    natural = order % (lanes // 2) * 2 + order // (lanes // 2)
    goes = (jnp.arange(key_tiles)[None, :] * lanes + lane) // key_tiles == natural[:, None]
    key_send = jnp.sum(jnp.where(goes[:, :, None, None], own_blocks[None], 0.0), axis=1)

    packed = lax.dynamic_update_slice(packed, key_send, (0, heads_rows, 0))
    packed = lax.all_to_all(packed, ROWS, 0, 0, tiled=True)
    query_out = packed[:, :heads_rows].reshape(query_rows, index_local, idx_width)
    blocks = packed[:, heads_rows : heads_rows + STRIPE]
    source = (lane * key_tiles + jnp.arange(key_tiles)) % lanes
    source = source % 2 * (lanes // 2) + source // 2
    comes = source[:, None] == order[None, :]
    key_out = jnp.sum(jnp.where(comes[:, :, None, None], blocks[None], 0.0), axis=1)
    key_out = key_out.reshape(key_tiles * STRIPE, idx_width)
    small = packed[:, heads_rows + STRIPE]
    weight_out = small[:, :heads_rows].reshape(query_rows, index_local)
    loss_out = small[:, heads_rows : heads_rows + QROWS].reshape(query_rows)
    return (query_out, weight_out, key_out, loss_out)


def solution(mesh):
    fine = Mesh(mesh.devices.reshape(8, 2, 2, 4, 2), CTX + HEAD)
    return jax.shard_map(
        body,
        mesh=fine,
        in_specs=(
            P(CTX, HEAD, None),
            P(CTX, None),
            P(CTX, HEAD, None),
            P(CTX, None),
            P(CTX, HEAD),
            P(),
            P(CTX),
        ),
        out_specs=(P(CTX, HEAD, None), P(CTX, HEAD), P(CTX + HEAD, None), P(CTX)),
        check_vma=False,
    )
```

```python
import functools
import math

import jax
import jax.numpy as jnp
from jax import lax
from jax.experimental import pallas as pl
from jax.experimental.pallas import tpu as pltpu
from jax.sharding import Mesh, PartitionSpec as P

TILE = 128
MLA_HEADS = 128
OWNER_MOST = 3
QROWS = 16
STRIPE = 8
VMEM = 60 * 1024 * 1024
SMALL_VMEM = 32 * 1024 * 1024

SLOTS, CORE, FIRST = 16, 18, 19

CTX = ("z", "yh")
HEAD = ("yl", "x", "core")
ROWS = ("core", "yl", "x")
exp_scale = 192.0 ** (-0.5) * math.log2(math.e)
far_below = -1e30


def allowed_keys(query_first, key_pos):
    rows = lax.broadcasted_iota(jnp.int32, (QROWS, key_pos.shape[1]), 0)
    return key_pos <= rows + query_first


def stripes_kernel(selection, index_key, key_latent, send):
    ctx, lane = lax.axis_index(CTX), lax.axis_index(HEAD)
    rows, (blocks, slots) = send.shape[0], selection.shape
    per_block = OWNER_MOST * STRIPE
    tiles = index_key.shape[0] // TILE
    row = lax.broadcasted_iota(jnp.int32, (rows, slots), 0)
    slot = lax.broadcasted_iota(jnp.int32, (rows, slots), 1)
    first = slot * per_block
    repeat = ((row >= first) & (row < first + per_block)).astype(jnp.float32)
    picked = jnp.dot(
        repeat.astype(jnp.bfloat16),
        selection[...].astype(jnp.float32).astype(jnp.bfloat16),
        preferred_element_type=jnp.float32,
    ).astype(jnp.int32)
    inner = picked - ctx * tiles
    mine = (inner >= 0) & (inner < tiles)
    a = lax.broadcasted_iota(jnp.int32, (slots, slots), 0)
    b = lax.broadcasted_iota(jnp.int32, (slots, slots), 1)
    earlier = (a < b).astype(jnp.float32).astype(jnp.bfloat16)
    rank = jnp.dot(
        mine.astype(jnp.float32).astype(jnp.bfloat16), earlier, preferred_element_type=jnp.float32
    ).astype(jnp.int32)
    block = jnp.sum(jnp.where(repeat > 0, slot, 0), axis=1, keepdims=True)
    row = lax.broadcasted_iota(jnp.int32, (rows, 1), 0)
    wanted = lax.shift_right_logical(row - block * per_block, 3)
    source = inner * TILE + lane * STRIPE + (row & (STRIPE - 1)) + 1
    source = jnp.sum(jnp.where(mine & (rank == wanted), source, 0), axis=1, keepdims=True) - 1
    spot = lax.broadcasted_iota(jnp.int32, (rows, index_key.shape[0]), 1)
    pick = (spot == source).astype(jnp.float32).astype(jnp.bfloat16)
    send[:, :TILE] = jnp.dot(pick, index_key[...], preferred_element_type=jnp.float32).astype(
        jnp.bfloat16
    )
    send[:, TILE:] = lax.dot_general(
        pick, key_latent[...], (((1,), (1,)), ((), ())), preferred_element_type=jnp.float32
    ).astype(jnp.bfloat16)


def attend_kernel(facts, *refs):
    pieces, (q_own, q_other, target, index_keys, keys, total, *raw) = refs[:16], refs[16:]
    for i, piece in enumerate(pieces):
        spot = pl.ds(pl.multiple_of(facts[i] * TILE, TILE), TILE)
        index_keys[spot, :] = piece[:, :TILE]
        keys[spot, :] = piece[:, TILE:]
    span = keys.shape[0]
    shape = (STRIPE, 2 * TILE)
    behind = lax.broadcasted_iota(jnp.int32, shape, 0) - (
        lax.broadcasted_iota(jnp.int32, shape, 1) & (TILE - 1)
    )
    behind = behind - facts[CORE] * TILE
    pairs = [(part, head) for part in (q_own, q_other) for head in range(0, part.shape[0], 2)]

    def scores(step):
        part, head = pairs[step]
        both = jnp.concatenate([part[head], part[head + 1]], axis=1)
        out = raw[step % 2]
        out[...] = jnp.dot(keys[...], both, preferred_element_type=jnp.float32)
        for tile in range(2):
            for stripe in range(span // TILE):
                spot = pl.ds(pl.multiple_of(stripe * TILE + facts[SLOTS + tile] * STRIPE, STRIPE), STRIPE)
                late = behind + (tile * TILE + stripe * STRIPE) > 0
                out[spot, :] = jnp.where(late, far_below, out[spot, :])

    def softmax(step):
        part = raw[step % 2]
        spots = [slice(i, i + TILE) for i in range(0, span, TILE)]
        folded = (TILE // 8, 8, 2 * TILE)
        top = functools.reduce(
            jnp.maximum, [jnp.max(part[spot, :].reshape(folded), axis=0) for spot in spots]
        )
        top = jnp.max(top, axis=0, keepdims=True)
        row_sum = jnp.zeros((8, 2 * TILE), jnp.float32)
        for spot in spots:
            weights = jnp.exp2((part[spot, :] - top) * exp_scale)
            part[spot, :] = weights
            row_sum = row_sum + jnp.sum(weights.reshape(folded), axis=0)
        share = 1.0 / (jnp.sum(row_sum, axis=0, keepdims=True) * MLA_HEADS)
        for spot in spots:
            weights = part[spot, :] * share
            weights = weights[:, :TILE] + weights[:, TILE:]
            if step == 0:
                total[spot, :] = weights
            else:
                total[spot, :] += weights

    for step in range(len(pairs)):
        scores(step)
        if step:
            softmax(step - 1)
    softmax(len(pairs) - 1)
    for i in range(0, span, TILE):
        target[:, i : i + TILE] = total[i : i + TILE, :].T


def row_groups(rows, heads):
    row = lax.broadcasted_iota(jnp.int32, (rows, rows * heads), 0) * heads
    both = lax.broadcasted_iota(jnp.int32, (rows, rows * heads), 1)
    return ((both >= row) & (both < row + heads)).astype(jnp.float32)


def index_logits(block, keys):
    return lax.dot_general(
        block[:, :, :TILE].reshape(-1, TILE),
        keys[...],
        (((1,), (1,)), ((), ())),
        preferred_element_type=jnp.float32,
    ).reshape(*block.shape[:2], keys.shape[0])


def index_weights(block):
    terms = block[:, :, TILE : 2 * TILE].astype(jnp.float32)
    return terms[:, :, 0:1] + terms[:, :, 1:2] + terms[:, :, 2:3]


def source_blocks(queries, count):
    return [queries.at[i : i + count] for i in range(0, queries.shape[0], count)]


def score_kernel(queries, keys, score):
    heads_rows = queries.shape[1]
    total = jnp.zeros((heads_rows, keys.shape[0]), jnp.float32)
    for block in source_blocks(queries, 2):
        lifted = jnp.maximum(index_logits(block, keys), 0.0)
        total = total + jnp.sum(lifted * index_weights(block), axis=0)
    score[...] = jnp.dot(
        row_groups(QROWS, heads_rows // QROWS),
        total,
        precision=lax.Precision.HIGHEST,
        preferred_element_type=jnp.float32,
    )


def index_coefs(block, keys, score_grad):
    logits = index_logits(block, keys)
    scaled = jnp.where(logits > 0, score_grad[None] * index_weights(block), 0.0)
    return logits, scaled.astype(jnp.bfloat16).reshape(-1, logits.shape[-1])


def key_grad_kernel(
    facts, target_parts, score, queries, keys, key_pos, loss_grad,
    score_grad, loss, key_grad, coef
):
    allowed = allowed_keys(facts[FIRST], key_pos[...])
    target = jnp.sum(target_parts[...], axis=0)
    masked = jnp.where(allowed, score[...], far_below)
    shifted = masked - jnp.max(masked, axis=-1, keepdims=True)
    weights = jnp.where(allowed, jnp.exp(shifted), 0.0)
    row_sum = jnp.sum(weights, axis=-1, keepdims=True)
    log_prob = shifted - jnp.log(row_sum)
    positive = target > 0
    self_term = jnp.where(positive, target * jnp.log(jnp.where(positive, target, 1.0)), 0.0)
    loss[...] = jnp.sum(
        jnp.where(allowed, self_term - target * log_prob, 0.0), axis=-1, keepdims=True
    )
    rows_grad = loss_grad[...] * jnp.where(allowed, weights / row_sum - target, 0.0)
    heads_rows = queries.shape[1]
    score_grad[...] = lax.dot_general(
        row_groups(QROWS, heads_rows // QROWS),
        rows_grad,
        (((0,), (0,)), ((), ())),
        precision=lax.Precision.HIGHEST,
        preferred_element_type=jnp.float32,
    )
    count = 2
    rows = count * heads_rows
    for step, block in enumerate(source_blocks(queries, count)):
        coef[step * rows : (step + 1) * rows, :] = index_coefs(block, keys, score_grad[...])[1]
    flat = queries[:, :, :TILE].reshape(-1, TILE)
    flat = lax.dot_general(
        flat, coef[...], (((0,), (0,)), ((), ())), preferred_element_type=jnp.float32
    ).astype(jnp.bfloat16)
    for lane in range(key_grad.shape[0]):
        key_grad[lane] = flat[:, lane * TILE : (lane + 1) * TILE]


def as_row(column):
    n = column.shape[0]
    here = lax.broadcasted_iota(jnp.int32, (n, n), 0) == lax.broadcasted_iota(
        jnp.int32, (n, n), 1
    )
    return jnp.sum(jnp.where(here, column, 0.0), axis=0, keepdims=True)


def query_grad_kernel(score_grad, loss, queries, keys, packed):
    count = 2
    heads_rows = queries.shape[1]
    losses = as_row(loss[...])
    blank = jnp.zeros((1, packed.shape[2] - heads_rows - QROWS), jnp.float32)
    rest = jnp.zeros((packed.shape[1] - heads_rows - STRIPE - 1, packed.shape[2]), jnp.float32)
    for step, block in enumerate(source_blocks(queries, count)):
        logits, coef = index_coefs(block, keys, score_grad[...])
        query = jnp.dot(coef, keys[...], preferred_element_type=jnp.float32)
        query = query.reshape(count, heads_rows, TILE)
        lifted = jnp.sum(score_grad[...][None] * jnp.maximum(logits, 0.0), axis=-1, keepdims=True)
        for i in range(count):
            place = step * count + i
            packed[place, :heads_rows] = query[i]
            last = jnp.concatenate([as_row(lifted[i]), losses, blank], axis=1)
            packed[place, heads_rows + STRIPE :] = jnp.concatenate([last, rest], axis=0)


def whole(shape):
    return pl.BlockSpec(shape, lambda *_: (0,) * len(shape))


def one_hot_rows(table, block):
    a, b = table.shape
    eye = jnp.eye(block, dtype=table.dtype)
    return (table[:, None, :, None] * eye[None, :, None, :]).reshape(a * block, b * block)


def body(main_query, key_latent, index_query, index_key, index_weight, selection, loss_grad):
    bf16, f32 = jnp.bfloat16, jnp.float32
    ctx_index = lax.axis_index(CTX)
    ctx_count = lax.axis_size(CTX)
    lane = lax.axis_index(HEAD)
    lanes = lax.axis_size(HEAD)
    yl, x, core = lax.axis_index("yl"), lax.axis_index("x"), lax.axis_index("core")
    x_count = lax.axis_size("x")
    query_rows, main_local, lat_width = main_query.shape
    index_local, idx_width = index_query.shape[1:]
    key_tiles = key_latent.shape[0] // TILE
    sel_count = selection.shape[1]
    key_span = sel_count * TILE
    context = key_tiles * TILE * ctx_count
    width = idx_width + lat_width
    heads_all = lanes * index_local
    rows_all = heads_all * QROWS
    heads_rows = index_local * QROWS
    swap = [(0, 1), (1, 0)]
    params = pltpu.CompilerParams(vmem_limit_bytes=VMEM)
    small = pltpu.CompilerParams(vmem_limit_bytes=SMALL_VMEM)
    vmem = pl.BlockSpec(memory_space=pltpu.VMEM)
    smem = pl.BlockSpec(memory_space=pltpu.SMEM)

    def shifted(value, shift):
        ring = [(i, (i + shift) % x_count) for i in range(x_count)]
        return lax.ppermute(value, "x", ring)

    send = pl.pallas_call(
        stripes_kernel,
        in_specs=[vmem] * 3,
        out_shape=jax.ShapeDtypeStruct((ctx_count * OWNER_MOST * STRIPE, width), bf16),
        compiler_params=params,
        name="stripes",
    )(selection, index_key, key_latent.T)
    send, index_query, index_weight, main_query = lax.optimization_barrier(
        (send, index_query, index_weight, main_query)
    )
    arrived = lax.all_to_all(send, CTX, 0, 0, tiled=True)

    queries = jnp.transpose(main_query, (1, 2, 0))
    q_other = lax.dynamic_slice_in_dim(queries, (1 - core) * TILE, TILE, 2)
    q_other = lax.ppermute(q_other, "core", swap)

    first_term = lax.reduce_precision(index_weight, 8, 7)
    rest = index_weight - first_term
    second_term = lax.reduce_precision(rest, 8, 7)
    terms = jnp.stack([first_term, second_term, rest - second_term], axis=-1).astype(bf16)
    iq = jnp.concatenate(
        [index_query, jnp.pad(terms, ((0, 0), (0, 0), (0, idx_width - 3)))], axis=-1
    ).reshape(lanes, heads_rows, 2 * idx_width)

    owner = selection // key_tiles
    inner = selection % key_tiles
    earlier = jnp.tril(jnp.ones((sel_count, sel_count), jnp.int32), -1)
    rank = jnp.sum((owner[:, :, None] == owner[:, None, :]) * earlier[None], axis=2)
    ranks = jnp.arange(OWNER_MOST)
    picked = lax.dynamic_index_in_dim(selection, ctx_index, 0, keepdims=False)
    my_owner = lax.dynamic_index_in_dim(owner, ctx_index, 0, keepdims=False)
    my_rank = lax.dynamic_index_in_dim(rank, ctx_index, 0, keepdims=False)
    sent = jnp.any(
        (owner[:, None, :, None] == ctx_index)
        & (rank[:, None, :, None] == ranks[None, :, None, None])
        & (inner[:, None, :, None] == jnp.arange(key_tiles)[None, None, None, :]),
        axis=2,
    ).reshape(ctx_count * OWNER_MOST, key_tiles)
    got = (
        (my_owner[:, None, None] == jnp.arange(ctx_count)[None, :, None])
        & (my_rank[:, None, None] == ranks[None, None, :])
    ).reshape(sel_count, ctx_count * OWNER_MOST)
    got_rows = one_hot_rows(got.astype(bf16), STRIPE)
    sent_rows = one_hot_rows(sent.astype(bf16), STRIPE)
    chunk = core * (lanes // 2) + yl * x_count + x
    grad_rows = lax.dynamic_slice_in_dim(loss_grad, chunk * QROWS, QROWS, 0).reshape(QROWS, 1)
    key_pos = (
        jnp.arange(lanes)[:, None, None] * STRIPE
        + picked[None, :, None] * TILE
        + jnp.arange(STRIPE)[None, None, :]
    ).reshape(1, key_span)
    place = [
        ((yl ^ j) * x_count + (x - shift) % x_count) * 2 + (core ^ k)
        for k in range(2)
        for j in range(2)
        for shift in (0, 1, 3, 2)
    ]
    block_first = context - query_rows * ctx_count + ctx_index * query_rows
    own = block_first // TILE + jnp.arange(2)
    slots = jnp.argmax(picked[None, :] == own[:, None], axis=1)
    facts = jnp.concatenate(
        [jnp.stack(place), slots, jnp.stack([core, block_first + chunk * QROWS])]
    ).astype(jnp.int32)
    arrived, got_rows, sent_rows, key_pos, grad_rows, facts, iq = lax.optimization_barrier(
        (arrived, got_rows, sent_rows, key_pos, grad_rows, facts, iq)
    )
    stripe = jnp.dot(got_rows, arrived, preferred_element_type=bf16)

    other = lax.ppermute(stripe, "yl", swap)
    pieces = [stripe] + [shifted(stripe, shift) for shift in (1, 3, 2)]
    far_pieces = [shifted(other, shift) for shift in (1, 3, 2)]
    iq, *far_pieces = lax.optimization_barrier((iq, *far_pieces))
    iq = lax.all_to_all(iq, ROWS, 0, 0, tiled=True)
    pieces += [other] + far_pieces
    pieces += [lax.ppermute(piece, "core", swap) for piece in pieces]

    count = 2 * main_local * TILE
    target_part, index_keys = pl.pallas_call(
        attend_kernel,
        grid_spec=pltpu.PrefetchScalarGridSpec(
            num_scalar_prefetch=1,
            grid=(1,),
            in_specs=[whole((TILE, width))] * 16
            + [
                pl.BlockSpec((main_local, lat_width, TILE), lambda i, facts: (0, 0, facts[CORE])),
                whole((main_local, lat_width, TILE)),
            ],
            out_specs=[whole((TILE, key_span)), whole((key_span, idx_width))],
            scratch_shapes=[
                pltpu.VMEM((key_span, lat_width), bf16),
                pltpu.VMEM((key_span, TILE), f32),
                pltpu.VMEM((key_span, 2 * TILE), f32),
                pltpu.VMEM((key_span, 2 * TILE), f32),
            ],
        ),
        out_shape=[
            jax.ShapeDtypeStruct((TILE, key_span), f32),
            jax.ShapeDtypeStruct((key_span, idx_width), bf16),
        ],
        compiler_params=params,
        cost_estimate=pl.CostEstimate(
            flops=2 * count * key_span * lat_width,
            bytes_accessed=8 * 2**20,
            transcendentals=count * key_span,
        ),
        name="attend",
    )(facts, *pieces, queries, q_other)
    target_parts = lax.all_to_all(target_part, ("yl", "x"), 0, 0, tiled=True)
    target_parts = target_parts.reshape(lanes // 2, QROWS, key_span)

    score = pl.pallas_call(
        score_kernel,
        in_specs=[vmem] * 2,
        out_shape=jax.ShapeDtypeStruct((QROWS, key_span), f32),
        compiler_params=small,
        cost_estimate=pl.CostEstimate(
            flops=2 * rows_all * key_span * idx_width, bytes_accessed=2**20, transcendentals=0
        ),
        name="score",
    )(iq, index_keys)

    score_grad, loss, key_part = pl.pallas_call(
        key_grad_kernel,
        in_specs=[smem] + [vmem] * 6,
        out_shape=[
            jax.ShapeDtypeStruct((heads_rows, key_span), f32),
            jax.ShapeDtypeStruct((QROWS, 1), f32),
            jax.ShapeDtypeStruct((lanes, idx_width, TILE), bf16),
        ],
        scratch_shapes=[pltpu.VMEM((rows_all, key_span), bf16)],
        compiler_params=small,
        cost_estimate=pl.CostEstimate(
            flops=4 * rows_all * key_span * idx_width, bytes_accessed=4 * 2**20, transcendentals=0
        ),
        name="key_grad",
    )(facts, target_parts, score, iq, index_keys, key_pos, grad_rows)

    packed_shape = (lanes, heads_rows + 2 * STRIPE, idx_width)
    packed = pl.pallas_call(
        query_grad_kernel,
        in_specs=[vmem] * 4,
        out_shape=jax.ShapeDtypeStruct(packed_shape, f32),
        compiler_params=small,
        cost_estimate=pl.CostEstimate(
            flops=4 * rows_all * key_span * idx_width, bytes_accessed=4 * 2**20, transcendentals=0
        ),
        name="query_grad",
    )(score_grad, loss, iq, index_keys)

    key_sum = lax.all_to_all(key_part, HEAD, 0, 0, tiled=True)
    key_sum, packed = lax.optimization_barrier((key_sum, packed))
    key_sum = jnp.sum(key_sum.astype(f32), axis=0)
    back = lax.dot_general(
        got_rows, key_sum.astype(bf16), (((0,), (1,)), ((), ())), preferred_element_type=bf16
    )
    back = lax.all_to_all(back, CTX, 0, 0, tiled=True)
    own_blocks = lax.dot_general(
        sent_rows, back, (((0,), (0,)), ((), ())), preferred_element_type=f32
    ).reshape(key_tiles, STRIPE, idx_width)
    order = jnp.arange(lanes)
    natural = order % (lanes // 2) * 2 + order // (lanes // 2)
    goes = (jnp.arange(key_tiles)[None, :] * lanes + lane) // key_tiles == natural[:, None]
    key_send = jnp.sum(jnp.where(goes[:, :, None, None], own_blocks[None], 0.0), axis=1)

    packed = lax.dynamic_update_slice(packed, key_send, (0, heads_rows, 0))
    packed = lax.all_to_all(packed, ROWS, 0, 0, tiled=True)
    query_out = packed[:, :heads_rows].reshape(query_rows, index_local, idx_width)
    blocks = packed[:, heads_rows : heads_rows + STRIPE]
    source = (lane * key_tiles + jnp.arange(key_tiles)) % lanes
    source = source % 2 * (lanes // 2) + source // 2
    comes = source[:, None] == order[None, :]
    key_out = jnp.sum(jnp.where(comes[:, :, None, None], blocks[None], 0.0), axis=1)
    key_out = key_out.reshape(key_tiles * STRIPE, idx_width)
    small = packed[:, heads_rows + STRIPE]
    weight_out = small[:, :heads_rows].reshape(query_rows, index_local)
    loss_out = small[:, heads_rows : heads_rows + QROWS].reshape(query_rows)
    return (query_out, weight_out, key_out, loss_out)


def solution(mesh):
    fine = Mesh(mesh.devices.reshape(8, 2, 2, 4, 2), CTX + HEAD)
    return jax.shard_map(
        body,
        mesh=fine,
        in_specs=(
            P(CTX, HEAD, None),
            P(CTX, None),
            P(CTX, HEAD, None),
            P(CTX, None),
            P(CTX, HEAD),
            P(),
            P(CTX),
        ),
        out_specs=(P(CTX, HEAD, None), P(CTX, HEAD), P(CTX + HEAD, None), P(CTX)),
        check_vma=False,
    )
```
